256 devices in a mesh: seq: 32 (over y, x, core), head: 8 (over z).
Axes of the slice: x: 4, y: 4, z: 8, core: 2. Of those that a mesh axis runs over, the one named last changes fastest.
Arguments:
- query_rows: bfloat16 [8192, 1024], P('seq', 'head'), may hold values from -6 to 6
- key_rows: bfloat16 [8192, 1024], P('seq', 'head'), may hold values from -6 to 6
- value_rows: bfloat16 [8192, 2048], P('seq', 'head'), may hold values from -6 to 6
- output_gate: bfloat16 [8192, 2048], P('seq', 'head'), may hold values from -6 to 6
- write_rate: float32 [16, 8192], P('head', 'seq'), may hold values from 0.05 to 1
- log_decay: float32 [16, 8192], P('head', 'seq'), may hold values from -1.2 to 0, as said below
- out_weight: bfloat16 [2048, 2048], P(None, 'head'), may hold values from -0.125 to 0.125
- out_cotangent: bfloat16 [8192, 2048], P('seq', 'head'), may hold values from -6 to 6
- block_response: int32 [96], replicated, may hold values from 0 to 63, as said below
- prefix_owner: int32 [32], replicated, may hold values from 0 to 31, each once
Outputs:
- layer_out: bfloat16 [8192, 2048], P('seq', 'head')
- grad_query: float32 [8192, 1024], P('seq', 'head')
- grad_key: float32 [8192, 1024], P('seq', 'head')
- grad_value: float32 [8192, 2048], P('seq', 'head')
- grad_gate: float32 [8192, 2048], P('seq', 'head')
- grad_write: float32 [16, 8192], P('head', 'seq')
- grad_decay: float32 [16, 8192], P('head', 'seq')
- grad_weight: float32 [2048, 2048], P('seq', 'head')
The draws below stay inside these ranges and needn't reach their ends.
Inputs may be any that keep to these rules, and one draw needn't show every extreme that they name: `block_response`: blocks of one response are consecutive and lie within the 3 blocks of one index of seq; responses appear in increasing order; each response has 1 to 3 blocks and one has exactly 3; every response of 0 to 63 appears. `prefix_owner`: each index of seq holds exactly one prompt's prefix. `log_decay`: every entry is negative.
All inputs are finite; a program needn't handle non-finite values.
Results may differ from the reference program's by a relative error of at most 0.015.
Values may be sent and summed in bfloat16 or wider, within the bound.
A program may use at most 64 MiB of HBM per device.

```python
import math
from functools import partial
import jax
import jax.numpy as jnp
from jax import lax

D = 2048
VALUE_HEADS = 16
K_HEADS = 8
DK = 128
DV = 128
SPAN = 64
PREFIX = 64
BLK_DEV = 3
RESP_PER = 2
MOST = 3
ROWS = 256
TOKEN_ROWS = 8192
PROMPTS = 32
RESPONSES = 64
NBLK = 96
KEYS = 1024
VALUE = 2048
N_SEQ = 32


def draw_log_decay(key, part):
    chain_length = PREFIX + MOST * SPAN
    every_key = jax.random.split(key, 6)
    head_shape = (VALUE_HEADS, 1)
    base_rate = jnp.exp(jax.random.uniform(every_key[0], head_shape, jnp.float32, math.log(0.1 / chain_length), math.log(1.0 / 30.0)))
    block_total = TOKEN_ROWS // SPAN
    block_factor = jnp.exp(jax.random.uniform(every_key[3], (VALUE_HEADS, block_total, 1), jnp.float32, -0.7, 0.7))
    token_factor = jnp.exp(jax.random.uniform(every_key[4], (VALUE_HEADS, block_total, SPAN), jnp.float32, -0.7, 0.7))
    spike_key, depth_random_key = jax.random.split(every_key[5])
    spike_groups = jax.random.uniform(spike_key, (VALUE_HEADS, TOKEN_ROWS), jnp.float32) < 3.0 / chain_length
    spike_depth = jax.random.uniform(depth_random_key, (VALUE_HEADS, TOKEN_ROWS), jnp.float32, 0.2, 0.7)
    decay_speed = (base_rate[:, :, None] * block_factor * token_factor).reshape(VALUE_HEADS, TOKEN_ROWS)
    decay_speed = decay_speed + jnp.where(spike_groups, spike_depth, 0.0)
    return -decay_speed


def draw_block_response(key, part):
    lone_key, order_key = jax.random.split(jax.random.fold_in(key, 17))
    spare = BLK_DEV - 1
    cand_total = N_SEQ * spare
    extra = RESPONSES - N_SEQ
    lone = jax.random.randint(lone_key, (), 0, N_SEQ).astype(jnp.int32)
    order = jax.random.permutation(order_key, cand_total).astype(jnp.int32)
    cand_ids = jnp.arange(cand_total, dtype=jnp.int32)
    cand_dev = cand_ids // spare
    score = order + jnp.where(cand_dev == lone, cand_total, 0).astype(jnp.int32)
    ranks = jnp.argsort(jnp.argsort(score))
    chosen = (ranks < extra).astype(jnp.int32)
    flat_pos = cand_dev * BLK_DEV + cand_ids % spare + 1
    starts = jnp.zeros((NBLK,), jnp.int32).at[flat_pos].set(chosen)
    first_pos = jnp.arange(N_SEQ, dtype=jnp.int32) * BLK_DEV
    starts = starts.at[first_pos].set(1)
    return (jnp.cumsum(starts) - 1).astype(jnp.int32)


def shard_levels(rng, extent, cuts, low, high):
    def one(position, blocks):
        steps = jax.random.uniform(jax.random.fold_in(jax.random.fold_in(rng, 6), position), (blocks,), jnp.float32, low / len(cuts), high / len(cuts))
        return jnp.repeat(jnp.exp(steps), extent[position] // blocks).reshape((-1,) + (1,) * (len(extent) - position - 1))

    gain = one(*cuts[0])
    for cut in cuts[1:]:
        gain = gain * one(*cut)
    return gain


def gaussian(own_key, dims, scale, reach, cuts=(), kind=jnp.bfloat16):
    values = jax.random.normal(own_key, dims, jnp.float32) * scale
    if len(cuts) > 0:
        values = shard_levels(own_key, dims, cuts, -0.22, 0.18) * values
    return jnp.clip(values, min=-reach, max=reach).astype(kind)


def setup_inputs(seed: int = 0) -> dict:
    streams_of = jax.random.split(jax.random.key(seed), 11)
    return {
        "query_rows": gaussian(streams_of[0], (TOKEN_ROWS, KEYS), 1.0, 6.0, ((0, 32), (1, 8))),
        "key_rows": gaussian(streams_of[1], (TOKEN_ROWS, KEYS), 1.0, 6.0, ((0, 32), (1, 8))),
        "value_rows": gaussian(streams_of[2], (TOKEN_ROWS, VALUE), 1.0, 6.0, ((0, 32), (1, 8))),
        "output_gate": gaussian(streams_of[3], (TOKEN_ROWS, VALUE), 1.0, 6.0, ((0, 32), (1, 8))),
        "write_rate": jnp.clip(0.05 + 0.95 * jax.random.uniform(streams_of[4], (VALUE_HEADS, TOKEN_ROWS), jnp.float32) ** shard_levels(streams_of[4], (VALUE_HEADS, TOKEN_ROWS), ((0, 8), (1, 32)), -0.2, 0.2), 0.05, 1.0),
        "log_decay": draw_log_decay(jax.random.fold_in(streams_of[10], 71), 0),
        "out_weight": gaussian(streams_of[6], (D, VALUE), VALUE ** -0.5, 0.125, ((1, 8),)),
        "out_cotangent": gaussian(streams_of[7], (TOKEN_ROWS, D), 1.0, 6.0, ((0, 32), (1, 8))),
        "block_response": draw_block_response(jax.random.fold_in(streams_of[10], 71), 0),
        "prefix_owner": jax.random.permutation(streams_of[9], PROMPTS).astype(jnp.int32),
    }


highest = lax.Precision.HIGHEST
tiny_eps = 1e-06

def unit_rows(raw_rows):
    return raw_rows * lax.rsqrt(lax.optimization_barrier(jnp.sum(raw_rows * raw_rows, axis=-1, keepdims=True)) + tiny_eps)

def span_parts(query_unit, key_unit, value_part, write_part, decay_part):
    span_len = decay_part.shape[-1]
    dim_key = key_unit.shape[-1]
    cumulative = jnp.cumsum(decay_part, axis=-1)
    row_ids = lax.broadcasted_iota(jnp.int32, (span_len, span_len), 0)
    col_ids = lax.broadcasted_iota(jnp.int32, (span_len, span_len), 1)
    strict = row_ids > col_ids
    causal = row_ids >= col_ids
    spread = cumulative[..., :, None] - cumulative[..., None, :]
    below_diag = jnp.where(strict, jnp.exp(jnp.where(strict, spread, 0.0)), 0.0)
    within = jnp.where(causal, jnp.exp(jnp.where(causal, spread, 0.0)), 0.0)
    key_key = jnp.einsum('...ik,...jk->...ij', key_unit, key_unit, precision=highest)
    system = jnp.eye(span_len, dtype=jnp.float32) + write_part[..., :, None] * below_diag * key_key
    growth = jnp.exp(cumulative)
    right_side = jnp.concatenate([(write_part * growth)[..., None] * key_unit, write_part[..., None] * value_part], axis=-1)
    solved = lax.linalg.triangular_solve(system, right_side, left_side=True, lower=True, unit_diagonal=True)
    weights_w = solved[..., :dim_key]
    base_u = solved[..., dim_key:]
    query_key = jnp.einsum('...ik,...jk->...ij', query_unit, key_unit, precision=highest) * within
    remain = jnp.exp(cumulative[..., -1:] - cumulative)
    key_tail = remain[..., None] * key_unit
    transfer = growth[..., -1][..., None, None] * jnp.eye(dim_key, dtype=jnp.float32) - jnp.einsum('...ck,...cl->...kl', weights_w, key_tail, precision=highest)
    offset = jnp.einsum('...cv,...ck->...vk', base_u, key_tail, precision=highest)
    return (transfer, offset, weights_w, base_u, query_key, growth, query_unit)

def span_apply(span_terms, state_in):
    transfer, offset, weights_w, base_u, query_key, growth, query_unit = span_terms
    update = base_u - jnp.einsum('...ck,...vk->...cv', weights_w, state_in, precision=highest)
    block_out = growth[..., None] * jnp.einsum('...ck,...vk->...cv', query_unit, state_in, precision=highest)
    block_out = block_out + jnp.einsum('...ij,...jv->...iv', query_key, update, precision=highest)
    state_out = jnp.einsum('...vk,...kl->...vl', state_in, transfer, precision=highest) + offset
    return (block_out, state_out)

def prefix_region(head_array):
    feat_width = head_array.shape[3]
    piece = jnp.transpose(head_array[:, :, :PREFIX], (1, 0, 2, 3)).reshape(N_SEQ * VALUE_HEADS, PREFIX, feat_width)
    return jnp.transpose(piece.reshape(N_SEQ * VALUE_HEADS, PREFIX // SPAN, SPAN, feat_width), (1, 0, 2, 3))

def answer_region(head_array):
    feat_width = head_array.shape[3]
    piece = head_array[:, :, PREFIX:].reshape(VALUE_HEADS, N_SEQ, BLK_DEV, SPAN, feat_width)
    return jnp.transpose(piece, (1, 2, 0, 3, 4)).reshape(N_SEQ * BLK_DEV, VALUE_HEADS, SPAN, feat_width)

def slot_major(flat_blocks):
    grouped_blocks = flat_blocks.reshape((N_SEQ, BLK_DEV) + flat_blocks.shape[1:])
    return jnp.swapaxes(grouped_blocks, 0, 1)

def gated_layer(query32, key32, value32, gate32, write_rate, log_decay, block_response, prefix_owner):
    query_unit = unit_rows(query32.reshape(TOKEN_ROWS, K_HEADS, DK)) * DK ** (-0.5)
    key_unit = unit_rows(key32.reshape(TOKEN_ROWS, K_HEADS, DK))
    query_unit = jnp.repeat(jnp.transpose(query_unit, (1, 0, 2)), VALUE_HEADS // K_HEADS, axis=0)
    key_unit = jnp.repeat(jnp.transpose(key_unit, (1, 0, 2)), VALUE_HEADS // K_HEADS, axis=0)
    values = jnp.transpose(value32.reshape(TOKEN_ROWS, VALUE_HEADS, DV), (1, 0, 2))
    grouped = (query_unit.reshape(VALUE_HEADS, N_SEQ, ROWS, DK), key_unit.reshape(VALUE_HEADS, N_SEQ, ROWS, DK), values.reshape(VALUE_HEADS, N_SEQ, ROWS, DV), write_rate.reshape(VALUE_HEADS, N_SEQ, ROWS, 1), log_decay.reshape(VALUE_HEADS, N_SEQ, ROWS, 1))
    prefix_in = tuple((prefix_region(item) for item in grouped))
    prefix_in = prefix_in[:3] + (prefix_in[3][..., 0], prefix_in[4][..., 0])

    def advance(state_in, block_in):
        block_out, state_out = span_apply(span_parts(*block_in), state_in)
        return (state_out, block_out)
    last_state, prefix_outs = lax.scan(advance, jnp.zeros((N_SEQ * VALUE_HEADS, DV, DK), jnp.float32), prefix_in)
    last_state = last_state.reshape(N_SEQ, VALUE_HEADS, DV, DK)
    rounded = lax.optimization_barrier(last_state.astype(jnp.bfloat16)).astype(jnp.float32)
    states_all = last_state + lax.stop_gradient(rounded - last_state)
    answer_in = tuple((answer_region(item) for item in grouped))
    answer_in = answer_in[:3] + (answer_in[3][..., 0], answer_in[4][..., 0])
    answer_in = tuple((slot_major(item) for item in answer_in))
    block_flags = jnp.concatenate([jnp.ones((1,), dtype=bool), block_response[1:] != block_response[:-1]])
    owners = jnp.take(prefix_owner, block_response // RESP_PER).astype(jnp.int32)
    slot_flags = slot_major(block_flags)
    slot_owners = slot_major(owners)

    def respond(state_in, block_in):
        inputs_here, block_flag, block_owner = block_in
        chosen = jnp.take(states_all, block_owner, axis=0)
        state_in = jnp.where(block_flag[:, None, None, None], chosen, state_in)
        block_out, state_out = span_apply(span_parts(*inputs_here), state_in)
        return (state_out, block_out)
    ignored, answer_outs = lax.scan(respond, jnp.zeros((N_SEQ, VALUE_HEADS, DV, DK), jnp.float32), (answer_in, slot_flags, slot_owners))
    answer_outs = jnp.swapaxes(answer_outs, 0, 1).reshape(N_SEQ * BLK_DEV, VALUE_HEADS, SPAN, DV)
    prefix_rows = jnp.transpose(prefix_outs.reshape(PREFIX // SPAN, N_SEQ, VALUE_HEADS, SPAN, DV), (1, 0, 3, 2, 4)).reshape(N_SEQ, PREFIX, VALUE)
    answer_rows = jnp.transpose(answer_outs.reshape(N_SEQ, BLK_DEV, VALUE_HEADS, SPAN, DV), (0, 1, 3, 2, 4)).reshape(N_SEQ, BLK_DEV * SPAN, VALUE)
    outs_all = jnp.concatenate([prefix_rows, answer_rows], axis=1).reshape(TOKEN_ROWS, VALUE_HEADS, DV)
    inv_scale = lax.rsqrt(lax.optimization_barrier(jnp.mean(outs_all * outs_all, axis=-1, keepdims=True)) + tiny_eps)
    gated_rows = outs_all * inv_scale * jax.nn.silu(gate32.reshape(TOKEN_ROWS, VALUE_HEADS, DV))
    return gated_rows.reshape(TOKEN_ROWS, VALUE)

def reference(query_rows, key_rows, value_rows, output_gate, write_rate, log_decay, out_weight, out_cotangent, block_response, prefix_owner):
    layer_fn = partial(gated_layer, block_response=block_response, prefix_owner=prefix_owner)
    floats = (query_rows.astype(jnp.float32), key_rows.astype(jnp.float32), value_rows.astype(jnp.float32), output_gate.astype(jnp.float32), write_rate, log_decay)
    normed, pullback = jax.vjp(layer_fn, *floats)
    rounded = normed.astype(jnp.bfloat16)
    layer_out = jnp.dot(rounded.astype(jnp.float32), out_weight.T.astype(jnp.float32), preferred_element_type=jnp.float32).astype(jnp.bfloat16)
    grad_normed = jnp.dot(out_cotangent.astype(jnp.float32), out_weight.astype(jnp.float32), preferred_element_type=jnp.float32)
    grad_weight = jnp.dot(out_cotangent.T.astype(jnp.float32), rounded.astype(jnp.float32), preferred_element_type=jnp.float32)
    all_grads = pullback(grad_normed)
    return (layer_out, all_grads[0], all_grads[1], all_grads[2], all_grads[3], all_grads[4], all_grads[5], grad_weight)
```

```python
import functools

import jax
import jax.numpy as jnp
from jax import lax
from jax.experimental import pallas as pl
from jax.experimental.pallas import tpu as pltpu
from jax.sharding import PartitionSpec as P

N_SEQ = 32
N_HEAD = 8
CHIPS = 16
SPAN = 64
EPS = 1e-06
F32 = jnp.float32
BF16 = jnp.bfloat16
HIGHEST = lax.Precision.HIGHEST
MESH = pl.DeviceIdType.MESH
SCALE = 128 ** (-0.5)

KINDS = {"nn": ((1,), (0,)), "nt": ((1,), (1,)), "tn": ((0,), (0,))}


def dot(a, b, kind="nn"):
    return lax.dot_general(
        a.astype(BF16), b.astype(BF16), (KINDS[kind], ((), ())), preferred_element_type=F32
    )


def parts(x):
    high = x.astype(BF16)
    return high, (x - high.astype(F32)).astype(BF16)


def dot3(a, b, kind="nn"):
    a_high, a_low = parts(a)
    b_high, b_low = parts(b)
    return dot(a_high, b_high, kind) + (dot(a_high, b_low, kind) + dot(a_low, b_high, kind))


def dot_exact(a, b):
    return lax.dot_general(
        a, b, (KINDS["nn"], ((), ())), precision=HIGHEST, preferred_element_type=F32
    )


def iotas(shape=(128, 128)):
    return lax.broadcasted_iota(jnp.int32, shape, 0), lax.broadcasted_iota(jnp.int32, shape, 1)


def stack_heads(x):
    return jnp.concatenate([x[:, :128], x[:, 128:]], axis=0)


def side_heads(x):
    return jnp.concatenate([x[:64], x[64:]], axis=1)


def diagonal_heads(x):
    zero = jnp.zeros_like(x[:64])
    return jnp.concatenate(
        [jnp.concatenate([x[:64], zero], axis=1), jnp.concatenate([zero, x[64:]], axis=1)], axis=0
    )


def twice(x):
    return jnp.concatenate([x, x], axis=0)


def fold(x):
    return x[:64] + x[64:]


def half_swap(x):
    return jnp.concatenate([x[:, 64:], x[:, :64]], axis=1)


def by_block(x):
    lower = lax.broadcasted_iota(jnp.int32, (1, 128), 1) < 64
    rows = []
    for pair in range(2):
        first = x[0:1, 128 * pair : 128 * pair + 128]
        second = x[1:2, 128 * pair : 128 * pair + 128]
        rows.append(jnp.where(lower, first, half_swap(second)))
        rows.append(jnp.where(lower, half_swap(first), second))
    return jnp.concatenate(rows, axis=0)


def by_head(x):
    lower = lax.broadcasted_iota(jnp.int32, (1, 128), 1) < 64
    heads = ([], [])
    for pair in range(2):
        even, odd = x[2 * pair : 2 * pair + 1], x[2 * pair + 1 : 2 * pair + 2]
        heads[0].append(jnp.where(lower, even, half_swap(odd)))
        heads[1].append(jnp.where(lower, half_swap(even), odd))
    return jnp.concatenate([jnp.concatenate(row, axis=1) for row in heads], axis=0)


def turned(x):
    return jnp.transpose(jnp.concatenate([x, jnp.zeros((120, 128), F32)], axis=0))


def unit_scale(x):
    return lax.rsqrt(jnp.sum(x * x, axis=-1, keepdims=True) + EPS)


def running_decay(write_rate, log_decay):
    row, col = iotas()
    same = (row >> 6) == (col >> 6)
    upto = jnp.where(same & (row <= col), 1.0, 0.0).astype(F32)
    both = jnp.concatenate([by_block(log_decay), by_block(write_rate)], axis=0)
    summed = dot_exact(both, upto)
    rows = jnp.concatenate([summed[:4], both[4:]], axis=0)
    return rows[:4], turned(rows)


def block_columns(rows, columns, b):
    cum_row = rows[b : b + 1]
    cum = columns[:, b : b + 1]
    rate = columns[:, 4 + b : 5 + b]
    first = lax.broadcasted_iota(jnp.int32, (128, 1), 0) < 64
    last = jnp.where(first, cum_row[:, 63:64], cum_row[:, 127:128])
    return cum_row, cum, rate, jnp.exp(cum), jnp.exp(last - cum)


def last_growth(rows, b):
    lane = lax.broadcasted_iota(jnp.int32, (1, 256), 1)
    return jnp.exp(jnp.where(lane < 128, rows[b : b + 1, 63:64], rows[b : b + 1, 127:128]))


def block_tables(query, key, rows, columns, b):
    row, col = iotas()
    causal = ((row >> 6) == (col >> 6)) & (row >= col)
    cum_row, cum, rate, _, _ = block_columns(rows, columns, b)
    within = jnp.where(causal, jnp.exp(jnp.where(causal, cum - cum_row, 0.0)), 0.0)
    key2 = twice(key)
    strict = jnp.where(row > col, within, 0.0) * rate
    system = strict * dot3(key2, key2, "nt")
    query_key = dot3(twice(query), key2, "nt") * within
    return within, system, query_key


def inverse(systems):
    row, col = iotas()
    found = None
    for level in range(6):
        here = ((row >> (level + 1)) == (col >> (level + 1))) & ((row >> level) != (col >> level))
        below = [jnp.where(here, system, 0.0) for system in systems]
        if found is None:
            eye = jnp.where(row == col, 1.0, 0.0).astype(F32)
            found = [eye - one for one in below]
        else:
            half = [dot3(one, two) for one, two in zip(found, below)]
            found = [one - dot3(two, one) for one, two in zip(found, half)]
    return found


def gated(out, gate):
    inv = lax.rsqrt(jnp.mean(out * out, axis=-1, keepdims=True) + EPS)
    return out * inv * (gate / (1.0 + jnp.exp(-gate)))


def gated_back(out, gate, grad):
    inv = lax.rsqrt(jnp.mean(out * out, axis=-1, keepdims=True) + EPS)
    sig = 1.0 / (1.0 + jnp.exp(-gate))
    weighted = grad * (gate * sig)
    grad_gate = grad * out * inv * (sig * (1.0 + gate * (1.0 - sig)))
    along = jnp.mean(weighted * out, axis=-1, keepdims=True)
    return inv * (weighted - out * (inv * inv * along)), grad_gate


def block_grads(
    query, key, value, cols, growth_last, tables, step, update, grad_out, grad_state, state_in
):
    _, _, rate, growth, remain = cols
    within, system, query_key = tables
    row, col = iotas()
    key2, query2 = twice(key), twice(query)
    grad_scores = dot3(grad_out, update, "nt")
    grad_system = -dot(step, update, "nt")
    masked = grad_scores * within
    strict = jnp.where(row > col, grad_system * within, 0.0) * rate
    pulled = grad_system * system
    spread = grad_scores * query_key + pulled
    grad_query = fold(dot(masked, key2))
    state_key = dot(diagonal_heads(update), grad_state, "nt")
    grad_key = fold(
        dot(masked, query2, "tn") + dot(strict, key2) + dot(strict, key2, "tn") + remain * state_key
    )
    tail = remain * jnp.sum(key2 * state_key, axis=-1, keepdims=True)
    grad_cum = jnp.sum(spread, axis=-1, keepdims=True) - tail
    grad_row = -jnp.sum(spread, axis=0, keepdims=True)
    end0 = jnp.sum(tail[:64], axis=0, keepdims=True)
    end1 = jnp.sum(tail[64:], axis=0, keepdims=True)
    grad_value = rate * step
    if state_in is None:
        inner = value
    else:
        state, key_state, query_state = state_in
        inner = value - growth * key_state
        out_growth = growth * grad_out
        in_growth = growth * grad_value
        grad_cum += jnp.sum(out_growth * query_state - in_growth * key_state, axis=-1, keepdims=True)
        grad_query += dot3(side_heads(out_growth), state, "nt")
        grad_key -= dot(side_heads(in_growth), state, "nt")
        kept = jnp.sum(growth_last * (state * grad_state), axis=0, keepdims=True)
        end0 += jnp.sum(kept[:, :128], axis=1, keepdims=True)
        end1 += jnp.sum(kept[:, 128:], axis=1, keepdims=True)
    lane = lax.broadcasted_iota(jnp.int32, (1, 128), 1)
    grad_row += jnp.where(lane == 63, end0, 0.0) + jnp.where(lane == 127, end1, 0.0)
    grad_rate = jnp.sum(step * inner, axis=-1, keepdims=True) + (
        jnp.sum(pulled, axis=-1, keepdims=True) / rate
    )
    return grad_query, grad_key, grad_value, grad_rate, grad_cum, grad_row


def decay_grads(grad_cums, grad_rates, grad_rows):
    row, col = iotas()
    packed = jnp.zeros((128, 128), F32)
    for b in range(4):
        packed = jnp.where(col == b, grad_cums[b], packed)
        packed = jnp.where(col == 4 + b, grad_rates[b], packed)
    packed = jnp.transpose(packed)[:8]
    since = jnp.where(((row >> 6) == (col >> 6)) & (row >= col), 1.0, 0.0).astype(F32)
    grad_cum = packed[:4] + jnp.concatenate(grad_rows, axis=0)
    grad_cum = jnp.concatenate([grad_cum, jnp.zeros((4, 128), F32)], axis=0)
    return by_head(packed[4:]), by_head(dot_exact(grad_cum, since)[:4])


BACK, APART, FLAGS = 32, 64, 80


def plan_kernel(response_ref, owner_ref, plan_ref, home_s):
    me = lax.axis_index("seq")
    chip, core = me // 2, me % 2

    def find_home(response, home):
        following = jnp.minimum(home + 1, N_SEQ - 1)
        here = (home < N_SEQ - 1) & (response_ref[3 * following] <= response)
        home = jnp.where(here, following, home)
        home_s[response] = home
        return home

    lax.fori_loop(0, 2 * N_SEQ, find_home, jnp.int32(0))

    def plan(offset, carry):
        to = 2 * ((chip + offset) % CHIPS) + core
        first = response_ref[3 * to] >> 1
        for slot in range(2):
            owner = owner_ref[jnp.minimum(first + slot, N_SEQ - 1)]
            plan_ref[2 * offset + slot] = (me - owner + 31) % N_SEQ
        prompt = jnp.int32(0)
        for candidate in range(N_SEQ):
            prompt = jnp.where(owner_ref[candidate] == to, candidate, prompt)
        homes = [home_s[2 * prompt + j] for j in range(2)]
        for j, home in enumerate(homes):
            slot = prompt - (response_ref[3 * home] >> 1)
            plan_ref[BACK + 2 * offset + j] = 2 * ((me - home + 31) % N_SEQ) + slot
        plan_ref[APART + offset] = jnp.where(homes[0] != homes[1], 1, 0)
        return carry

    lax.fori_loop(0, CHIPS, plan, 0)
    own = [response_ref[3 * me + j] for j in range(3)]
    for j in (1, 2):
        plan_ref[FLAGS + j - 1] = jnp.where(own[j] != own[j - 1], 1, 0)
        plan_ref[FLAGS + 1 + j] = jnp.where((own[j] >> 1) != (own[0] >> 1), 1, 0)


def rows_of(index, size):
    return pl.ds(pl.multiple_of(index * size, size), size)


def send(src, dst, send_sem, recv_sem, device):
    copy = pltpu.make_async_remote_copy(
        src_ref=src,
        dst_ref=dst,
        send_sem=send_sem,
        recv_sem=recv_sem,
        device_id=device,
        device_id_type=MESH,
    )
    copy.start()


def await_bytes(ref, sem):
    pltpu.make_async_copy(ref, ref, sem).wait()


def layer_kernel(
    query_ref,
    key_ref,
    value_ref,
    gate_ref,
    rate_ref,
    decay_ref,
    weight_ref,
    cot_ref,
    plan_ref,
    layer_ref,
    grad_query_ref,
    grad_key_ref,
    grad_value_ref,
    grad_gate_ref,
    grad_rate_ref,
    grad_decay_ref,
    grad_weight_ref,
    cots,
    piece_src,
    pieces,
    chosen_src,
    chosen,
    starts,
    grad_src,
    grad_pieces,
    owned_src,
    owned,
    sums_src,
    sums,
    weight_src,
    weight_pair,
    weight_sum,
    weight_in,
    within_s,
    system_s,
    scores_s,
    inverse_s,
    outs_s,
    update_s,
    step_s,
    grad_out_s,
    state_s,
    grad_state_s,
    key_state_s,
    query_state_s,
    normed_s,
    ring_send,
    ring_recv,
    sum_send,
    sum_recv,
    seq_send,
    seq_recv,
):
    me = lax.axis_index("seq")
    head = lax.axis_index("head")
    chip, core = me // 2, me % 2
    right, left = (head + 1) % N_HEAD, (head + N_HEAD - 1) % N_HEAD

    barrier = pltpu.get_barrier_semaphore()

    def greet(offset, carry):
        pl.semaphore_signal(
            barrier, inc=1, device_id={"seq": (me + offset) % N_SEQ}, device_id_type=MESH
        )
        return carry

    lax.fori_loop(1, N_SEQ, greet, 0)
    for neighbour in (left, right):
        pl.semaphore_signal(barrier, inc=1, device_id={"head": neighbour}, device_id_type=MESH)
    pl.semaphore_wait(barrier, N_SEQ + 1)

    def ring_piece(hop, to_right):
        if hop == 4:
            return cots.at[3, pl.ds(0 if to_right else 128, 128)]
        return cots.at[hop - 1 if to_right else 3 + hop]

    def ring_start(hop):
        for to_right in (True, False):
            if hop == 1:
                src = cot_ref
            else:
                src = cots.at[hop - 2 if to_right else 2 + hop]
                if hop == 4:
                    src = src.at[pl.ds(0 if to_right else 128, 128)]
            index = 2 * (hop - 1) + (0 if to_right else 1)
            send(
                src,
                ring_piece(hop, to_right),
                ring_send.at[index],
                ring_recv.at[index],
                {"head": right if to_right else left},
            )

    def ring_arrived(hop):
        for to_right in (True, False):
            index = 2 * (hop - 1) + (0 if to_right else 1)
            await_bytes(ring_piece(hop, to_right), ring_recv.at[index])

    ring_start(1)

    rate2, decay2 = rate_ref[...], decay_ref[...]
    rows, columns = running_decay(rate2, decay2)

    def unit_block(ref, b):
        raw = ref[SPAN * b : SPAN * b + SPAN, :].astype(F32)
        return raw * unit_scale(raw)

    def block_of(ref, b):
        return stack_heads(ref[SPAN * b : SPAN * b + SPAN, :]).astype(F32)

    queries = [unit_block(query_ref, b) * SCALE for b in range(4)]
    keys = [unit_block(key_ref, b) for b in range(4)]
    cols = [block_columns(rows, columns, b) for b in range(4)]

    def tables_of(b):
        within, system, query_key = block_tables(queries[b], keys[b], rows, columns, b)
        within_s[b] = within
        system_s[b] = system
        scores_s[b] = query_key
        return system

    def tail_of(b):
        return twice(keys[b]) * cols[b][4]

    inverse_s[0] = inverse([tables_of(0)])[0].astype(BF16)
    update = dot(inverse_s[0], cols[0][2] * block_of(value_ref, 0))
    update_s[0] = update
    final = dot(tail_of(0), diagonal_heads(update), "tn")
    piece_src[0:128, :] = final[:, :128].astype(BF16)
    piece_src[128:256, :] = final[:, 128:].astype(BF16)

    def send_pieces(offset, carry):
        to = (me + offset) % N_SEQ
        send(
            piece_src.at[rows_of(to // 2, 16)],
            pieces.at[offset - 1],
            seq_send.at[0],
            seq_recv.at[0],
            {"seq": to},
        )
        return carry

    lax.fori_loop(1, N_SEQ, send_pieces, 0)
    pieces[31] = piece_src[rows_of(chip, 16), :]

    ring_arrived(1)
    ring_start(2)
    for b, found in zip((1, 2, 3), inverse([tables_of(b) for b in (1, 2, 3)])):
        inverse_s[b] = found.astype(BF16)

    await_bytes(pieces.at[pl.ds(0, 31)], seq_recv.at[0])

    def choose(offset):
        return [pieces[plan_ref[2 * offset + slot]] for slot in range(2)]

    def send_chosen(offset, carry):
        for slot, piece in enumerate(choose(offset)):
            chosen_src[pl.ds(pl.multiple_of((offset - 1) * 32 + 16 * slot, 16), 16), :] = piece
        send(
            chosen_src.at[rows_of(offset - 1, 32)],
            chosen.at[rows_of(offset - 1, 32)],
            seq_send.at[1],
            seq_recv.at[1],
            {"seq": 2 * ((chip + offset) % CHIPS) + core},
        )
        return carry

    lax.fori_loop(1, CHIPS, send_chosen, 0)
    for slot, piece in enumerate(choose(0)):
        chosen[480 + 16 * slot : 496 + 16 * slot, :] = piece

    ring_arrived(2)
    ring_start(3)

    def norm_block(b, out):
        outs_s[b] = out
        result = side_heads(gated(out, block_of(gate_ref, b))).astype(BF16)
        normed_s[SPAN * b : SPAN * b + SPAN, :] = result

    norm_block(0, dot3(scores_s[0], update_s[0]))

    await_bytes(chosen.at[pl.ds(0, 480)], seq_recv.at[1])
    for slot in range(2):
        for piece in range(CHIPS):
            place = (chip - piece + 15) % CHIPS
            starts[slot, 16 * (piece % 8) : 16 * (piece % 8) + 16, 128 * (piece // 8) : 128 * (piece // 8) + 128] = (
                chosen[pl.ds(pl.multiple_of(place * 32 + 16 * slot, 16), 16), :].astype(F32)
            )
    ring_arrived(3)
    ring_start(4)

    fresh = [None, None] + [plan_ref[FLAGS + b].astype(F32) for b in range(2)]
    later = [None, None] + [plan_ref[FLAGS + 2 + b].astype(F32) for b in range(2)]

    state = None
    for b in (1, 2, 3):
        if b == 1:
            state = starts[0]
        else:
            begun = (1.0 - later[b]) * starts[0] + later[b] * starts[1]
            state = fresh[b] * begun + (1.0 - fresh[b]) * state
        state_s[b - 1] = state
        _, _, rate, growth, _ = cols[b]
        both = dot3(jnp.concatenate([keys[b], queries[b]], axis=0), state)
        key_state, query_state = stack_heads(both[:64]), stack_heads(both[64:])
        key_state_s[b - 1] = key_state
        query_state_s[b - 1] = query_state
        update = dot(inverse_s[b], rate * (block_of(value_ref, b) - growth * key_state))
        update_s[b] = update
        if b < 3:
            state = last_growth(rows, b) * state + dot(tail_of(b), diagonal_heads(update), "tn")
        norm_block(b, growth * query_state + dot3(scores_s[b], update))

    def share(distance):
        block = (head + distance + N_HEAD) % N_HEAD
        return dot(normed_s[...], weight_ref[rows_of(block, 256), :], "nt")

    def sums_start(hop):
        for to_right in (True, False):
            index = 2 * (hop - 1) + (0 if to_right else 1)
            if hop == 1:
                half = pl.ds(0 if to_right else 128, 128)
                block = (head + 4) % N_HEAD
                sums_src[index, half, :] = dot(
                    normed_s[half, :], weight_ref[rows_of(block, 256), :], "nt"
                ).astype(BF16)
                src, dst = sums_src.at[index, half], sums.at[index, half]
            else:
                total = share(5 - hop if to_right else hop - 5)
                if hop == 2:
                    low = 0 if to_right else 128
                    sums_src[index] = total.astype(BF16)
                    sums_src[index, low : low + 128, :] = (
                        total[low : low + 128] + sums[index - 2, low : low + 128, :].astype(F32)
                    ).astype(BF16)
                else:
                    sums_src[index] = (total + sums[index - 2].astype(F32)).astype(BF16)
                src, dst = sums_src.at[index], sums.at[index]
            send(
                src,
                dst,
                sum_send.at[index],
                sum_recv.at[index],
                {"head": right if to_right else left},
            )

    def sums_piece(hop, to_right):
        index = 2 * (hop - 1) + (0 if to_right else 1)
        if hop == 1:
            return sums.at[index, pl.ds(0 if to_right else 128, 128)]
        return sums.at[index]

    def sums_arrived(hop):
        for to_right in (True, False):
            await_bytes(
                sums_piece(hop, to_right), sum_recv.at[2 * (hop - 1) + (0 if to_right else 1)]
            )

    sums_start(1)

    ring_arrived(4)

    def cot_slots():
        yield cot_ref, head
        for hop in (1, 2, 3, 4):
            yield cots.at[hop - 1], (head - hop + N_HEAD) % N_HEAD
        for hop in (1, 2, 3):
            yield cots.at[3 + hop], (head + hop) % N_HEAD

    grad_normed = None
    for slot_ref, block in cot_slots():
        term = dot(slot_ref[...], weight_ref[rows_of(block, 256), :])
        grad_normed = term if grad_normed is None else grad_normed + term
    for b in range(4):
        grad_out, grad_gate = gated_back(
            outs_s[b], block_of(gate_ref, b), stack_heads(grad_normed[SPAN * b : SPAN * b + SPAN])
        )
        grad_out_s[b] = grad_out
        grad_gate_ref[SPAN * b : SPAN * b + SPAN, :] = side_heads(grad_gate)

    grad_state = jnp.zeros((128, 256), F32)
    begun = [jnp.zeros((128, 256), F32), jnp.zeros((128, 256), F32)]
    for b in (3, 2, 1):
        _, _, rate, growth, remain = cols[b]
        grad_out = grad_out_s[b]
        grad_state_s[b] = grad_state
        grad_update = dot(scores_s[b], grad_out, "tn")
        if b < 3:
            grad_update += remain * stack_heads(dot(keys[b], grad_state))
        step = dot(inverse_s[b], grad_update, "tn")
        step_s[b] = step
        sides = jnp.concatenate(
            [side_heads(-(rate * growth) * step), side_heads(growth * grad_out)], axis=0
        )
        grad_in = dot(jnp.concatenate([keys[b], queries[b]], axis=0), sides, "tn")
        if b < 3:
            grad_in += last_growth(rows, b) * grad_state
        if b > 1:
            begun[0] += (fresh[b] * (1.0 - later[b])) * grad_in
            begun[1] += (fresh[b] * later[b]) * grad_in
            grad_state = (1.0 - fresh[b]) * grad_in
        else:
            begun[0] += grad_in
    for slot in range(2):
        for piece in range(CHIPS):
            grad_src[2 * piece + slot] = begun[slot][
                16 * (piece % 8) : 16 * (piece % 8) + 16,
                128 * (piece // 8) : 128 * (piece // 8) + 128,
            ].astype(BF16)

    def send_grads(offset, carry):
        to = (me + offset) % N_SEQ
        send(
            grad_src.at[pl.ds(2 * (to // 2), 2)],
            grad_pieces.at[pl.ds(2 * (offset - 1), 2)],
            seq_send.at[2],
            seq_recv.at[2],
            {"seq": to},
        )
        return carry

    lax.fori_loop(1, N_SEQ, send_grads, 0)
    for slot in range(2):
        grad_pieces[62 + slot] = grad_src[2 * chip + slot]

    sums_arrived(1)
    sums_start(2)
    for slot_ref, block in cot_slots():
        share_w = dot(slot_ref[...], normed_s[...], "tn").astype(BF16)
        for quarter in range(4):
            place = (quarter % 2) * 1024 + (2 * block + quarter // 2) * 64
            weight_src[pl.ds(pl.multiple_of(place, 64), 64), :] = share_w[
                64 * quarter : 64 * quarter + 64
            ]
    send(
        weight_src.at[rows_of(1 - core, 1024)],
        weight_pair,
        seq_send.at[4],
        seq_recv.at[4],
        {"seq": 2 * chip + 1 - core},
    )

    await_bytes(grad_pieces.at[pl.ds(0, 62)], seq_recv.at[2])

    def owned_piece(offset):
        one = grad_pieces[plan_ref[BACK + 2 * offset]].astype(F32)
        two = grad_pieces[plan_ref[BACK + 2 * offset + 1]].astype(F32)
        return (one + plan_ref[APART + offset].astype(F32) * two).astype(BF16)

    def send_owned(offset, carry):
        owned_src[rows_of(offset - 1, 16), :] = owned_piece(offset)
        send(
            owned_src.at[rows_of(offset - 1, 16)],
            owned.at[rows_of(offset - 1, 16)],
            seq_send.at[3],
            seq_recv.at[3],
            {"seq": 2 * ((chip + offset) % CHIPS) + core},
        )
        return carry

    lax.fori_loop(1, CHIPS, send_owned, 0)
    owned[240:256, :] = owned_piece(0)

    await_bytes(weight_pair, seq_recv.at[4])
    for part in range(4):
        place = core * 1024 + 256 * part
        weight_sum[256 * part : 256 * part + 256, :] = (
            weight_src[pl.ds(pl.multiple_of(place, 256), 256), :].astype(F32)
            + weight_pair[256 * part : 256 * part + 256, :].astype(F32)
        ).astype(BF16)

    def send_weight(offset, carry):
        to = (chip + offset) % CHIPS
        send(
            weight_sum.at[rows_of(to, 64)],
            weight_in.at[rows_of(offset - 1, 64)],
            seq_send.at[5],
            seq_recv.at[5],
            {"seq": 2 * to + core},
        )
        return carry

    lax.fori_loop(1, CHIPS, send_weight, 0)
    sums_arrived(2)
    sums_start(3)

    grad_cums, grad_rates, grad_rows = [None] * 4, [None] * 4, [None] * 4

    def finish_block(b, grad_state, state_in):
        tables = (within_s[b], system_s[b], scores_s[b])
        found = block_grads(
            queries[b],
            keys[b],
            block_of(value_ref, b),
            cols[b],
            last_growth(rows, b),
            tables,
            step_s[b],
            update_s[b],
            grad_out_s[b],
            grad_state,
            state_in,
        )
        grad_query_ref[SPAN * b : SPAN * b + SPAN, :] = found[0]
        grad_key_ref[SPAN * b : SPAN * b + SPAN, :] = found[1]
        grad_value_ref[SPAN * b : SPAN * b + SPAN, :] = side_heads(found[2])
        grad_rates[b], grad_cums[b], grad_rows[b] = found[3:]

    for b in (1, 2, 3):
        finish_block(b, grad_state_s[b], (state_s[b - 1], key_state_s[b - 1], query_state_s[b - 1]))
        if b == 2:
            sums_arrived(3)
            sums_start(4)

    await_bytes(owned.at[pl.ds(0, 240)], seq_recv.at[3])
    for piece in range(CHIPS):
        place = (chip - piece + 15) % CHIPS
        grad_state_s[0, 16 * (piece % 8) : 16 * (piece % 8) + 16, 128 * (piece // 8) : 128 * (piece // 8) + 128] = (
            owned[rows_of(place, 16), :].astype(F32)
        )
    grad_state = grad_state_s[0]
    grad_update = dot(scores_s[0], grad_out_s[0], "tn")
    grad_update += cols[0][4] * stack_heads(dot(keys[0], grad_state))
    step_s[0] = dot(inverse_s[0], grad_update, "tn")
    finish_block(0, grad_state, None)
    grad_rate_ref[...], grad_decay_ref[...] = decay_grads(grad_cums, grad_rates, grad_rows)

    await_bytes(weight_in.at[pl.ds(0, 15 * 64)], seq_recv.at[5])
    total = weight_sum[rows_of(chip, 64), :].astype(F32)
    for slot in range(15):
        total += weight_in[64 * slot : 64 * slot + 64, :].astype(F32)
    grad_weight_ref[...] = total
    total = share(0)
    sums_arrived(4)
    layer_ref[...] = (total + sums[6].astype(F32) + sums[7].astype(F32)).astype(BF16)

    for hop in (1, 2, 3, 4):
        for to_right in (True, False):
            index = 2 * (hop - 1) + (0 if to_right else 1)
            await_bytes(ring_piece(hop, to_right), ring_send.at[index])
            await_bytes(sums_piece(hop, to_right), sum_send.at[index])
    await_bytes(pieces.at[pl.ds(0, 31)], seq_send.at[0])
    await_bytes(chosen.at[pl.ds(0, 480)], seq_send.at[1])
    await_bytes(grad_pieces.at[pl.ds(0, 62)], seq_send.at[2])
    await_bytes(owned.at[pl.ds(0, 240)], seq_send.at[3])
    await_bytes(weight_pair, seq_send.at[4])
    await_bytes(weight_in.at[pl.ds(0, 15 * 64)], seq_send.at[5])


SCRATCH = [
    pltpu.VMEM((7, 256, 256), BF16),
    pltpu.VMEM((256, 128), BF16),
    pltpu.VMEM((32, 16, 128), BF16),
    pltpu.VMEM((480, 128), BF16),
    pltpu.VMEM((512, 128), BF16),
    pltpu.VMEM((2, 128, 256), F32),
    pltpu.VMEM((32, 16, 128), BF16),
    pltpu.VMEM((64, 16, 128), BF16),
    pltpu.VMEM((240, 128), BF16),
    pltpu.VMEM((256, 128), BF16),
    pltpu.VMEM((8, 256, 256), BF16),
    pltpu.VMEM((8, 256, 256), BF16),
    pltpu.VMEM((2048, 256), BF16),
    pltpu.VMEM((1024, 256), BF16),
    pltpu.VMEM((1024, 256), BF16),
    pltpu.VMEM((960, 256), BF16),
    pltpu.VMEM((4, 128, 128), F32),
    pltpu.VMEM((4, 128, 128), F32),
    pltpu.VMEM((4, 128, 128), F32),
    pltpu.VMEM((4, 128, 128), BF16),
    pltpu.VMEM((4, 128, 128), F32),
    pltpu.VMEM((4, 128, 128), F32),
    pltpu.VMEM((4, 128, 128), F32),
    pltpu.VMEM((4, 128, 128), F32),
    pltpu.VMEM((3, 128, 256), F32),
    pltpu.VMEM((4, 128, 256), F32),
    pltpu.VMEM((3, 128, 128), F32),
    pltpu.VMEM((3, 128, 128), F32),
    pltpu.VMEM((256, 256), BF16),
    pltpu.SemaphoreType.DMA((8,)),
    pltpu.SemaphoreType.DMA((8,)),
    pltpu.SemaphoreType.DMA((8,)),
    pltpu.SemaphoreType.DMA((8,)),
    pltpu.SemaphoreType.DMA((6,)),
    pltpu.SemaphoreType.DMA((6,)),
]


def unit_back(raw, grad, scale):
    inv = unit_scale(raw)
    unit = raw * inv
    return (scale * inv) * (grad - unit * jnp.sum(grad * unit, axis=-1, keepdims=True))


def finish_kernel(
    query_ref, key_ref, layer, query, key, value, gate, rate, decay, weight,
    layer_out, query_out, key_out, value_out, gate_out, rate_out, decay_out, weight_out,
):
    layer_out[...] = layer[...]
    query_out[...] = unit_back(query_ref[...].astype(F32), query[...], SCALE)
    key_out[...] = unit_back(key_ref[...].astype(F32), key[...], 1.0)
    value_out[...] = value[...]
    gate_out[...] = gate[...]
    rate_out[...] = rate[...]
    decay_out[...] = decay[...]
    weight_out[...] = weight[...]


RESULTS = [
    jax.ShapeDtypeStruct((256, 256), BF16),
    jax.ShapeDtypeStruct((256, 128), F32),
    jax.ShapeDtypeStruct((256, 128), F32),
    jax.ShapeDtypeStruct((256, 256), F32),
    jax.ShapeDtypeStruct((256, 256), F32),
    jax.ShapeDtypeStruct((2, 256), F32),
    jax.ShapeDtypeStruct((2, 256), F32),
    jax.ShapeDtypeStruct((64, 256), F32),
]


def per_device(
    query_rows, key_rows, value_rows, output_gate, write_rate, log_decay,
    out_weight, out_cotangent, block_response, prefix_owner,
):
    vmem = pl.BlockSpec(memory_space=pltpu.VMEM)
    smem = pl.BlockSpec(memory_space=pltpu.SMEM)
    plan = pl.pallas_call(
        plan_kernel,
        out_shape=jax.ShapeDtypeStruct((96,), jnp.int32),
        in_specs=[smem] * 2,
        out_specs=smem,
        scratch_shapes=[pltpu.SMEM((64,), jnp.int32)],
    )(block_response, prefix_owner)
    results = pl.pallas_call(
        layer_kernel,
        out_shape=RESULTS,
        in_specs=[vmem] * 8 + [smem],
        out_specs=[vmem] * 8,
        scratch_shapes=SCRATCH,
        compiler_params=pltpu.CompilerParams(
            collective_id=0, has_side_effects=True, vmem_limit_bytes=48 * 1024 * 1024
        ),
    )(
        query_rows, key_rows, value_rows, output_gate, write_rate, log_decay,
        out_weight, out_cotangent, plan,
    )
    return pl.pallas_call(
        finish_kernel,
        out_shape=RESULTS,
        in_specs=[vmem] * 10,
        out_specs=[vmem] * 8,
    )(query_rows, key_rows, *results)


def solution(mesh):
    rows = P("seq", "head")
    return jax.shard_map(
        per_device,
        mesh=mesh,
        in_specs=(rows, rows, rows, rows, P("head", "seq"), P("head", "seq"), P(None, "head"), rows, P(), P()),
        out_specs=(rows, rows, rows, rows, rows, P("head", "seq"), P("head", "seq"), rows),
        check_vma=False,
    )
```

```python
import functools

import jax
import jax.numpy as jnp
from jax import lax
from jax.experimental import pallas as pl
from jax.experimental.pallas import tpu as pltpu
from jax.sharding import PartitionSpec as P

N_SEQ = 32
N_HEAD = 8
CHIPS = 16
SPAN = 64
EPS = 1e-06
F32 = jnp.float32
BF16 = jnp.bfloat16
HIGHEST = lax.Precision.HIGHEST
MESH = pl.DeviceIdType.MESH
SCALE = 128 ** (-0.5)

KINDS = {"nn": ((1,), (0,)), "nt": ((1,), (1,)), "tn": ((0,), (0,))}


def dot(a, b, kind="nn"):
    return lax.dot_general(
        a.astype(BF16), b.astype(BF16), (KINDS[kind], ((), ())), preferred_element_type=F32
    )


def parts(x):
    high = x.astype(BF16)
    return high, (x - high.astype(F32)).astype(BF16)


def dot3(a, b, kind="nn"):
    a_high, a_low = parts(a)
    b_high, b_low = parts(b)
    return dot(a_high, b_high, kind) + (dot(a_high, b_low, kind) + dot(a_low, b_high, kind))


def dot_exact(a, b):
    return lax.dot_general(
        a, b, (KINDS["nn"], ((), ())), precision=HIGHEST, preferred_element_type=F32
    )


def iotas(shape=(128, 128)):
    return lax.broadcasted_iota(jnp.int32, shape, 0), lax.broadcasted_iota(jnp.int32, shape, 1)


def stack_heads(x):
    return jnp.concatenate([x[:, :128], x[:, 128:]], axis=0)


def side_heads(x):
    return jnp.concatenate([x[:64], x[64:]], axis=1)


def diagonal_heads(x):
    zero = jnp.zeros_like(x[:64])
    return jnp.concatenate(
        [jnp.concatenate([x[:64], zero], axis=1), jnp.concatenate([zero, x[64:]], axis=1)], axis=0
    )


def twice(x):
    return jnp.concatenate([x, x], axis=0)


def fold(x):
    return x[:64] + x[64:]


def half_swap(x):
    return jnp.concatenate([x[:, 64:], x[:, :64]], axis=1)


def by_block(x):
    lower = lax.broadcasted_iota(jnp.int32, (1, 128), 1) < 64
    rows = []
    for pair in range(2):
        first = x[0:1, 128 * pair : 128 * pair + 128]
        second = x[1:2, 128 * pair : 128 * pair + 128]
        rows.append(jnp.where(lower, first, half_swap(second)))
        rows.append(jnp.where(lower, half_swap(first), second))
    return jnp.concatenate(rows, axis=0)


def by_head(x):
    lower = lax.broadcasted_iota(jnp.int32, (1, 128), 1) < 64
    heads = ([], [])
    for pair in range(2):
        even, odd = x[2 * pair : 2 * pair + 1], x[2 * pair + 1 : 2 * pair + 2]
        heads[0].append(jnp.where(lower, even, half_swap(odd)))
        heads[1].append(jnp.where(lower, half_swap(even), odd))
    return jnp.concatenate([jnp.concatenate(row, axis=1) for row in heads], axis=0)


def turned(x):
    return jnp.transpose(jnp.concatenate([x, jnp.zeros((120, 128), F32)], axis=0))


def unit_scale(x):
    return lax.rsqrt(jnp.sum(x * x, axis=-1, keepdims=True) + EPS)


def unit_back(raw, grad, scale):
    inv = unit_scale(raw)
    unit = raw * inv
    return (scale * inv) * (grad - unit * jnp.sum(grad * unit, axis=-1, keepdims=True))


def running_decay(write_rate, log_decay):
    row, col = iotas()
    same = (row >> 6) == (col >> 6)
    upto = jnp.where(same & (row <= col), 1.0, 0.0).astype(F32)
    both = jnp.concatenate([by_block(log_decay), by_block(write_rate)], axis=0)
    summed = dot_exact(both, upto)
    rows = jnp.concatenate([summed[:4], both[4:]], axis=0)
    return rows[:4], turned(rows)


def block_columns(rows, columns, b):
    cum_row = rows[b : b + 1]
    cum = columns[:, b : b + 1]
    rate = columns[:, 4 + b : 5 + b]
    first = lax.broadcasted_iota(jnp.int32, (128, 1), 0) < 64
    last = jnp.where(first, cum_row[:, 63:64], cum_row[:, 127:128])
    return cum_row, cum, rate, jnp.exp(cum), jnp.exp(last - cum)


def last_growth(rows, b):
    lane = lax.broadcasted_iota(jnp.int32, (1, 256), 1)
    return jnp.exp(jnp.where(lane < 128, rows[b : b + 1, 63:64], rows[b : b + 1, 127:128]))


def block_tables(query, key, rows, columns, b):
    row, col = iotas()
    causal = ((row >> 6) == (col >> 6)) & (row >= col)
    cum_row, cum, rate, _, _ = block_columns(rows, columns, b)
    within = jnp.where(causal, jnp.exp(jnp.where(causal, cum - cum_row, 0.0)), 0.0)
    key2 = twice(key)
    strict = jnp.where(row > col, within, 0.0) * rate
    system = strict * dot3(key2, key2, "nt")
    query_key = dot3(twice(query), key2, "nt") * within
    return within, system, query_key


def inverse(systems):
    row, col = iotas()
    found = None
    for level in range(6):
        here = ((row >> (level + 1)) == (col >> (level + 1))) & ((row >> level) != (col >> level))
        below = [jnp.where(here, system, 0.0) for system in systems]
        if found is None:
            eye = jnp.where(row == col, 1.0, 0.0).astype(F32)
            found = [eye - one for one in below]
        else:
            half = [dot3(one, two) for one, two in zip(found, below)]
            found = [one - dot3(two, one) for one, two in zip(found, half)]
    return found


def gated(out, gate):
    inv = lax.rsqrt(jnp.mean(out * out, axis=-1, keepdims=True) + EPS)
    return out * inv * (gate / (1.0 + jnp.exp(-gate)))


def gated_back(out, gate, grad):
    inv = lax.rsqrt(jnp.mean(out * out, axis=-1, keepdims=True) + EPS)
    sig = 1.0 / (1.0 + jnp.exp(-gate))
    weighted = grad * (gate * sig)
    grad_gate = grad * out * inv * (sig * (1.0 + gate * (1.0 - sig)))
    along = jnp.mean(weighted * out, axis=-1, keepdims=True)
    return inv * (weighted - out * (inv * inv * along)), grad_gate


def block_grads(
    query, key, value, cols, growth_last, tables, step, update, grad_out, grad_state, state_in
):
    _, _, rate, growth, remain = cols
    within, system, query_key = tables
    row, col = iotas()
    key2, query2 = twice(key), twice(query)
    grad_scores = dot3(grad_out, update, "nt")
    grad_system = -dot(step, update, "nt")
    masked = grad_scores * within
    strict = jnp.where(row > col, grad_system * within, 0.0) * rate
    pulled = grad_system * system
    spread = grad_scores * query_key + pulled
    grad_query = fold(dot(masked, key2))
    state_key = dot(diagonal_heads(update), grad_state, "nt")
    grad_key = fold(
        dot(masked, query2, "tn") + dot(strict, key2) + dot(strict, key2, "tn") + remain * state_key
    )
    tail = remain * jnp.sum(key2 * state_key, axis=-1, keepdims=True)
    grad_cum = jnp.sum(spread, axis=-1, keepdims=True) - tail
    grad_row = -jnp.sum(spread, axis=0, keepdims=True)
    end0 = jnp.sum(tail[:64], axis=0, keepdims=True)
    end1 = jnp.sum(tail[64:], axis=0, keepdims=True)
    grad_value = rate * step
    if state_in is None:
        inner = value
    else:
        state, key_state, query_state = state_in
        inner = value - growth * key_state
        out_growth = growth * grad_out
        in_growth = growth * grad_value
        grad_cum += jnp.sum(out_growth * query_state - in_growth * key_state, axis=-1, keepdims=True)
        grad_query += dot3(side_heads(out_growth), state, "nt")
        grad_key -= dot(side_heads(in_growth), state, "nt")
        kept = jnp.sum(growth_last * (state * grad_state), axis=0, keepdims=True)
        end0 += jnp.sum(kept[:, :128], axis=1, keepdims=True)
        end1 += jnp.sum(kept[:, 128:], axis=1, keepdims=True)
    lane = lax.broadcasted_iota(jnp.int32, (1, 128), 1)
    grad_row += jnp.where(lane == 63, end0, 0.0) + jnp.where(lane == 127, end1, 0.0)
    grad_rate = jnp.sum(step * inner, axis=-1, keepdims=True) + (
        jnp.sum(pulled, axis=-1, keepdims=True) / rate
    )
    return grad_query, grad_key, grad_value, grad_rate, grad_cum, grad_row


def decay_grads(grad_cums, grad_rates, grad_rows):
    row, col = iotas()
    packed = jnp.zeros((128, 128), F32)
    for b in range(4):
        packed = jnp.where(col == b, grad_cums[b], packed)
        packed = jnp.where(col == 4 + b, grad_rates[b], packed)
    packed = jnp.transpose(packed)[:8]
    since = jnp.where(((row >> 6) == (col >> 6)) & (row >= col), 1.0, 0.0).astype(F32)
    grad_cum = packed[:4] + jnp.concatenate(grad_rows, axis=0)
    grad_cum = jnp.concatenate([grad_cum, jnp.zeros((4, 128), F32)], axis=0)
    return by_head(packed[4:]), by_head(dot_exact(grad_cum, since)[:4])


def rows_of(index, size):
    return pl.ds(pl.multiple_of(index * size, size), size)


def send(src, dst, send_sem, recv_sem, device):
    copy = pltpu.make_async_remote_copy(
        src_ref=src,
        dst_ref=dst,
        send_sem=send_sem,
        recv_sem=recv_sem,
        device_id=device,
        device_id_type=MESH,
    )
    copy.start()


def await_bytes(ref, sem):
    pltpu.make_async_copy(ref, ref, sem).wait()


def layer_kernel(
    query_hbm,
    key_hbm,
    value_hbm,
    gate_hbm,
    rate_hbm,
    decay_hbm,
    weight_hbm,
    cot_hbm,
    response_ref,
    owner_ref,
    layer_ref,
    grad_query_ref,
    grad_key_ref,
    grad_value_ref,
    grad_gate_ref,
    grad_rate_ref,
    grad_decay_ref,
    grad_weight_ref,
    query_ref,
    key_ref,
    value_ref,
    gate_ref,
    rate_ref,
    decay_ref,
    weight_ref,
    cot_ref,
    cots,
    piece_src,
    pieces,
    chosen_src,
    chosen,
    starts,
    grad_src,
    grad_pieces,
    owned_src,
    owned,
    sums_src,
    sums,
    weight_src,
    weight_pair,
    weight_sum,
    weight_in,
    within_s,
    system_s,
    scores_s,
    inverse_s,
    outs_s,
    update_s,
    step_s,
    grad_out_s,
    state_s,
    grad_state_s,
    key_state_s,
    query_state_s,
    normed_s,
    pick_s,
    gather_s,
    load_sem,
    ring_send,
    ring_recv,
    sum_send,
    sum_recv,
    seq_send,
    seq_recv,
):
    me = lax.axis_index("seq")
    head = lax.axis_index("head")
    chip, core = me // 2, me % 2
    right, left = (head + 1) % N_HEAD, (head + N_HEAD - 1) % N_HEAD

    loads = [
        pltpu.make_async_copy(src, dst, load_sem.at[index])
        for index, (src, dst) in enumerate(
            (
                (rate_hbm, rate_ref),
                (decay_hbm, decay_ref),
                (key_hbm, key_ref),
                (query_hbm, query_ref),
                (value_hbm, value_ref),
                (gate_hbm, gate_ref),
                (cot_hbm, cot_ref),
                (weight_hbm, weight_ref),
            )
        )
    ]
    for load in loads:
        load.start()

    barrier = pltpu.get_barrier_semaphore()

    def greet(offset, carry):
        pl.semaphore_signal(
            barrier, inc=1, device_id={"seq": (me + offset) % N_SEQ}, device_id_type=MESH
        )
        return carry

    lax.fori_loop(1, N_SEQ, greet, 0)
    for neighbour in (left, right):
        pl.semaphore_signal(barrier, inc=1, device_id={"head": neighbour}, device_id_type=MESH)
    pl.semaphore_wait(barrier, N_SEQ + 1)

    def ring_piece(hop, to_right):
        if hop == 4:
            return cots.at[3, pl.ds(0 if to_right else 128, 128)]
        return cots.at[hop - 1 if to_right else 3 + hop]

    def ring_start(hop):
        for to_right in (True, False):
            if hop == 1:
                src = cot_hbm
            else:
                src = cots.at[hop - 2 if to_right else 2 + hop]
                if hop == 4:
                    src = src.at[pl.ds(0 if to_right else 128, 128)]
            index = 2 * (hop - 1) + (0 if to_right else 1)
            send(
                src,
                ring_piece(hop, to_right),
                ring_send.at[index],
                ring_recv.at[index],
                {"head": right if to_right else left},
            )

    def ring_arrived(hop):
        for to_right in (True, False):
            index = 2 * (hop - 1) + (0 if to_right else 1)
            await_bytes(ring_piece(hop, to_right), ring_recv.at[index])

    ring_start(1)

    for load in loads[:5]:
        load.wait()
    rate2, decay2 = rate_ref[...], decay_ref[...]
    rows, columns = running_decay(rate2, decay2)

    def unit_block(ref, b):
        raw = ref[SPAN * b : SPAN * b + SPAN, :].astype(F32)
        return raw * unit_scale(raw)

    def block_of(ref, b):
        return stack_heads(ref[SPAN * b : SPAN * b + SPAN, :]).astype(F32)

    queries = [unit_block(query_ref, b) * SCALE for b in range(4)]
    keys = [unit_block(key_ref, b) for b in range(4)]
    cols = [block_columns(rows, columns, b) for b in range(4)]

    def tables_of(b):
        within, system, query_key = block_tables(queries[b], keys[b], rows, columns, b)
        within_s[b] = within
        system_s[b] = system
        scores_s[b] = query_key
        return system

    def tail_of(b):
        return twice(keys[b]) * cols[b][4]

    inverse_s[0] = inverse([tables_of(0)])[0].astype(BF16)
    update = dot(inverse_s[0], cols[0][2] * block_of(value_ref, 0))
    update_s[0] = update
    final = dot(tail_of(0), diagonal_heads(update), "tn")
    piece_src[0:128, :] = final[:, :128].astype(BF16)
    piece_src[128:256, :] = final[:, 128:].astype(BF16)

    def send_pieces(offset, carry):
        to = (me + offset) % N_SEQ
        send(
            piece_src.at[rows_of(to // 2, 16)],
            pieces.at[rows_of(offset - 1, 16)],
            seq_send.at[0],
            seq_recv.at[0],
            {"seq": to},
        )
        return carry

    lax.fori_loop(1, N_SEQ, send_pieces, 0)
    pieces[496:512, :] = piece_src[rows_of(chip, 16), :]

    ring_arrived(1)
    ring_start(2)
    for b, found in zip((1, 2, 3), inverse([tables_of(b) for b in (1, 2, 3)])):
        inverse_s[b] = found.astype(BF16)

    def owner_of(device, slot):
        prompt = (response_ref[3 * device] >> 1) + slot
        found = owner_ref[jnp.minimum(prompt, N_SEQ - 1)]
        return jnp.where(prompt < N_SEQ, found, -1)

    row, col = iotas((32, 512))
    source = (me + 31 - (col >> 4)) % N_SEQ
    for place in range(CHIPS):
        to = 2 * ((chip + place + 1) % CHIPS) + core
        wanted = jnp.where(row < 16, owner_of(to, 0), owner_of(to, 1))
        here = (source == wanted) & ((row & 15) == (col & 15))
        pick_s[32 * place : 32 * place + 32, :] = jnp.where(here, 1.0, 0.0).astype(BF16)

    for quarter in range(8):
        columns_here = []
        for place in range(4 * quarter, 4 * quarter + 4):
            device = (me + 31 - place) % N_SEQ
            columns_here.append((owner_of(device, 0), owner_of(device, 1)))
        row, col = iotas((256, 128))
        owner = jnp.full((256, 128), -1, jnp.int32)
        for index, (one, two) in enumerate(columns_here):
            owner = jnp.where((col >> 4) == 2 * index, one, owner)
            owner = jnp.where((col >> 4) == 2 * index + 1, two, owner)
        target = 2 * ((chip + 1 + (row >> 4)) % CHIPS) + core
        here = (owner == target) & ((row & 15) == (col & 15))
        gather_s[:, 128 * quarter : 128 * quarter + 128] = jnp.where(here, 1.0, 0.0).astype(BF16)

    await_bytes(pieces.at[pl.ds(0, 496)], seq_recv.at[0])

    chosen_src[...] = dot(pick_s[...], pieces[...]).astype(BF16)

    def send_chosen(offset, carry):
        send(
            chosen_src.at[rows_of(offset - 1, 32)],
            chosen.at[rows_of(offset - 1, 32)],
            seq_send.at[1],
            seq_recv.at[1],
            {"seq": 2 * ((chip + offset) % CHIPS) + core},
        )
        return carry

    lax.fori_loop(1, CHIPS, send_chosen, 0)
    chosen[480:512, :] = chosen_src[480:512, :]

    ring_arrived(2)
    ring_start(3)

    loads[5].wait()

    def norm_block(b, out):
        outs_s[b] = out
        result = side_heads(gated(out, block_of(gate_ref, b))).astype(BF16)
        normed_s[SPAN * b : SPAN * b + SPAN, :] = result

    norm_block(0, dot3(scores_s[0], update_s[0]))

    await_bytes(chosen.at[pl.ds(0, 480)], seq_recv.at[1])
    for slot in range(2):
        for piece in range(CHIPS):
            place = (chip - piece + 15) % CHIPS
            starts[slot, 16 * (piece % 8) : 16 * (piece % 8) + 16, 128 * (piece // 8) : 128 * (piece // 8) + 128] = (
                chosen[pl.ds(pl.multiple_of(place * 32 + 16 * slot, 16), 16), :].astype(F32)
            )
    ring_arrived(3)
    ring_start(4)

    own = [response_ref[3 * me + j] for j in range(3)]
    fresh, later = [None, None], [None, None]
    for j in (1, 2):
        fresh.append(jnp.where(own[j] != own[j - 1], 1.0, 0.0).astype(F32))
        later.append(jnp.where((own[j] >> 1) != (own[0] >> 1), 1.0, 0.0).astype(F32))

    state = None
    for b in (1, 2, 3):
        if b == 1:
            state = starts[0]
        else:
            begun = (1.0 - later[b]) * starts[0] + later[b] * starts[1]
            state = fresh[b] * begun + (1.0 - fresh[b]) * state
        state_s[b - 1] = state
        _, _, rate, growth, _ = cols[b]
        both = dot3(jnp.concatenate([keys[b], queries[b]], axis=0), state)
        key_state, query_state = stack_heads(both[:64]), stack_heads(both[64:])
        key_state_s[b - 1] = key_state
        query_state_s[b - 1] = query_state
        update = dot(inverse_s[b], rate * (block_of(value_ref, b) - growth * key_state))
        update_s[b] = update
        if b < 3:
            state = last_growth(rows, b) * state + dot(tail_of(b), diagonal_heads(update), "tn")
        norm_block(b, growth * query_state + dot3(scores_s[b], update))

    def share(distance):
        block = (head + distance + N_HEAD) % N_HEAD
        return dot(normed_s[...], weight_ref[rows_of(block, 256), :], "nt")

    def sums_start(hop):
        for to_right in (True, False):
            index = 2 * (hop - 1) + (0 if to_right else 1)
            if hop == 1:
                half = pl.ds(0 if to_right else 128, 128)
                block = (head + 4) % N_HEAD
                sums_src[index, half, :] = dot(
                    normed_s[half, :], weight_ref[rows_of(block, 256), :], "nt"
                ).astype(BF16)
                src, dst = sums_src.at[index, half], sums.at[index, half]
            else:
                total = share(5 - hop if to_right else hop - 5)
                if hop == 2:
                    low = 0 if to_right else 128
                    sums_src[index] = total.astype(BF16)
                    sums_src[index, low : low + 128, :] = (
                        total[low : low + 128] + sums[index - 2, low : low + 128, :].astype(F32)
                    ).astype(BF16)
                else:
                    sums_src[index] = (total + sums[index - 2].astype(F32)).astype(BF16)
                src, dst = sums_src.at[index], sums.at[index]
            send(
                src,
                dst,
                sum_send.at[index],
                sum_recv.at[index],
                {"head": right if to_right else left},
            )

    def sums_piece(hop, to_right):
        index = 2 * (hop - 1) + (0 if to_right else 1)
        if hop == 1:
            return sums.at[index, pl.ds(0 if to_right else 128, 128)]
        return sums.at[index]

    def sums_arrived(hop):
        for to_right in (True, False):
            await_bytes(
                sums_piece(hop, to_right), sum_recv.at[2 * (hop - 1) + (0 if to_right else 1)]
            )

    loads[7].wait()
    sums_start(1)

    ring_arrived(4)
    loads[6].wait()

    def cot_slots():
        yield cot_ref, head
        for hop in (1, 2, 3, 4):
            yield cots.at[hop - 1], (head - hop + N_HEAD) % N_HEAD
        for hop in (1, 2, 3):
            yield cots.at[3 + hop], (head + hop) % N_HEAD

    grad_normed = None
    for slot_ref, block in cot_slots():
        term = dot(slot_ref[...], weight_ref[rows_of(block, 256), :])
        grad_normed = term if grad_normed is None else grad_normed + term
    for b in range(4):
        grad_out, grad_gate = gated_back(
            outs_s[b], block_of(gate_ref, b), stack_heads(grad_normed[SPAN * b : SPAN * b + SPAN])
        )
        grad_out_s[b] = grad_out
        grad_gate_ref[SPAN * b : SPAN * b + SPAN, :] = side_heads(grad_gate)

    grad_state = jnp.zeros((128, 256), F32)
    begun = [jnp.zeros((128, 256), F32), jnp.zeros((128, 256), F32)]
    for b in (3, 2, 1):
        _, _, rate, growth, remain = cols[b]
        grad_out = grad_out_s[b]
        grad_state_s[b] = grad_state
        grad_update = dot(scores_s[b], grad_out, "tn")
        if b < 3:
            grad_update += remain * stack_heads(dot(keys[b], grad_state))
        step = dot(inverse_s[b], grad_update, "tn")
        step_s[b] = step
        sides = jnp.concatenate(
            [side_heads(-(rate * growth) * step), side_heads(growth * grad_out)], axis=0
        )
        grad_in = dot(jnp.concatenate([keys[b], queries[b]], axis=0), sides, "tn")
        if b < 3:
            grad_in += last_growth(rows, b) * grad_state
        if b > 1:
            begun[0] += (fresh[b] * (1.0 - later[b])) * grad_in
            begun[1] += (fresh[b] * later[b]) * grad_in
            grad_state = (1.0 - fresh[b]) * grad_in
        else:
            begun[0] += grad_in
    for slot in range(2):
        for piece in range(CHIPS):
            grad_src[32 * piece + 16 * slot : 32 * piece + 16 * slot + 16, :] = begun[slot][
                16 * (piece % 8) : 16 * (piece % 8) + 16,
                128 * (piece // 8) : 128 * (piece // 8) + 128,
            ].astype(BF16)

    def send_grads(offset, carry):
        to = (me + offset) % N_SEQ
        send(
            grad_src.at[rows_of(to // 2, 32)],
            grad_pieces.at[rows_of(offset - 1, 32)],
            seq_send.at[2],
            seq_recv.at[2],
            {"seq": to},
        )
        return carry

    lax.fori_loop(1, N_SEQ, send_grads, 0)
    grad_pieces[992:1024, :] = grad_src[rows_of(chip, 32), :]

    sums_arrived(1)
    sums_start(2)
    for slot_ref, block in cot_slots():
        share_w = dot(slot_ref[...], normed_s[...], "tn").astype(BF16)
        for quarter in range(4):
            place = (quarter % 2) * 1024 + (2 * block + quarter // 2) * 64
            weight_src[pl.ds(pl.multiple_of(place, 64), 64), :] = share_w[
                64 * quarter : 64 * quarter + 64
            ]
    send(
        weight_src.at[rows_of(1 - core, 1024)],
        weight_pair,
        seq_send.at[4],
        seq_recv.at[4],
        {"seq": 2 * chip + 1 - core},
    )

    await_bytes(grad_pieces.at[pl.ds(0, 992)], seq_recv.at[2])

    owned_src[...] = dot(gather_s[...], grad_pieces[...]).astype(BF16)

    def send_owned(offset, carry):
        send(
            owned_src.at[rows_of(offset - 1, 16)],
            owned.at[rows_of(offset - 1, 16)],
            seq_send.at[3],
            seq_recv.at[3],
            {"seq": 2 * ((chip + offset) % CHIPS) + core},
        )
        return carry

    lax.fori_loop(1, CHIPS, send_owned, 0)
    owned[240:256, :] = owned_src[240:256, :]

    await_bytes(weight_pair, seq_recv.at[4])
    for part in range(4):
        place = core * 1024 + 256 * part
        weight_sum[256 * part : 256 * part + 256, :] = (
            weight_src[pl.ds(pl.multiple_of(place, 256), 256), :].astype(F32)
            + weight_pair[256 * part : 256 * part + 256, :].astype(F32)
        ).astype(BF16)

    def send_weight(offset, carry):
        to = (chip + offset) % CHIPS
        send(
            weight_sum.at[rows_of(to, 64)],
            weight_in.at[rows_of(offset - 1, 64)],
            seq_send.at[5],
            seq_recv.at[5],
            {"seq": 2 * to + core},
        )
        return carry

    lax.fori_loop(1, CHIPS, send_weight, 0)
    sums_arrived(2)
    sums_start(3)

    grad_cums, grad_rates, grad_rows = [None] * 4, [None] * 4, [None] * 4

    def finish_block(b, grad_state, state_in):
        tables = (within_s[b], system_s[b], scores_s[b])
        found = block_grads(
            queries[b],
            keys[b],
            block_of(value_ref, b),
            cols[b],
            last_growth(rows, b),
            tables,
            step_s[b],
            update_s[b],
            grad_out_s[b],
            grad_state,
            state_in,
        )
        for raw_ref, out_ref, grad, scale in (
            (query_ref, grad_query_ref, found[0], SCALE),
            (key_ref, grad_key_ref, found[1], 1.0),
        ):
            raw = raw_ref[SPAN * b : SPAN * b + SPAN, :].astype(F32)
            out_ref[SPAN * b : SPAN * b + SPAN, :] = unit_back(raw, grad, scale)
        grad_value_ref[SPAN * b : SPAN * b + SPAN, :] = side_heads(found[2])
        grad_rates[b], grad_cums[b], grad_rows[b] = found[3:]

    for b in (1, 2, 3):
        finish_block(b, grad_state_s[b], (state_s[b - 1], key_state_s[b - 1], query_state_s[b - 1]))
        if b == 2:
            sums_arrived(3)
            sums_start(4)

    await_bytes(owned.at[pl.ds(0, 240)], seq_recv.at[3])
    for piece in range(CHIPS):
        place = (chip - piece + 15) % CHIPS
        grad_state_s[0, 16 * (piece % 8) : 16 * (piece % 8) + 16, 128 * (piece // 8) : 128 * (piece // 8) + 128] = (
            owned[rows_of(place, 16), :].astype(F32)
        )
    grad_state = grad_state_s[0]
    grad_update = dot(scores_s[0], grad_out_s[0], "tn")
    grad_update += cols[0][4] * stack_heads(dot(keys[0], grad_state))
    step_s[0] = dot(inverse_s[0], grad_update, "tn")
    finish_block(0, grad_state, None)
    grad_rate_ref[...], grad_decay_ref[...] = decay_grads(grad_cums, grad_rates, grad_rows)

    await_bytes(weight_in.at[pl.ds(0, 15 * 64)], seq_recv.at[5])
    total = weight_sum[rows_of(chip, 64), :].astype(F32)
    for slot in range(15):
        total += weight_in[64 * slot : 64 * slot + 64, :].astype(F32)
    grad_weight_ref[...] = total
    total = share(0)
    sums_arrived(4)
    layer_ref[...] = (total + sums[6].astype(F32) + sums[7].astype(F32)).astype(BF16)

    for hop in (1, 2, 3, 4):
        for to_right in (True, False):
            index = 2 * (hop - 1) + (0 if to_right else 1)
            await_bytes(ring_piece(hop, to_right), ring_send.at[index])
            await_bytes(sums_piece(hop, to_right), sum_send.at[index])
    await_bytes(pieces.at[pl.ds(0, 496)], seq_send.at[0])
    await_bytes(chosen.at[pl.ds(0, 480)], seq_send.at[1])
    await_bytes(grad_pieces.at[pl.ds(0, 992)], seq_send.at[2])
    await_bytes(owned.at[pl.ds(0, 240)], seq_send.at[3])
    await_bytes(weight_pair, seq_send.at[4])
    await_bytes(weight_in.at[pl.ds(0, 15 * 64)], seq_send.at[5])


SCRATCH = [
    pltpu.VMEM((256, 128), BF16),
    pltpu.VMEM((256, 128), BF16),
    pltpu.VMEM((256, 256), BF16),
    pltpu.VMEM((256, 256), BF16),
    pltpu.VMEM((2, 256), F32),
    pltpu.VMEM((2, 256), F32),
    pltpu.VMEM((2048, 256), BF16),
    pltpu.VMEM((256, 256), BF16),
    pltpu.VMEM((7, 256, 256), BF16),
    pltpu.VMEM((256, 128), BF16),
    pltpu.VMEM((512, 128), BF16),
    pltpu.VMEM((512, 128), BF16),
    pltpu.VMEM((512, 128), BF16),
    pltpu.VMEM((2, 128, 256), F32),
    pltpu.VMEM((512, 128), BF16),
    pltpu.VMEM((1024, 128), BF16),
    pltpu.VMEM((256, 128), BF16),
    pltpu.VMEM((256, 128), BF16),
    pltpu.VMEM((8, 256, 256), BF16),
    pltpu.VMEM((8, 256, 256), BF16),
    pltpu.VMEM((2048, 256), BF16),
    pltpu.VMEM((1024, 256), BF16),
    pltpu.VMEM((1024, 256), BF16),
    pltpu.VMEM((960, 256), BF16),
    pltpu.VMEM((4, 128, 128), F32),
    pltpu.VMEM((4, 128, 128), F32),
    pltpu.VMEM((4, 128, 128), F32),
    pltpu.VMEM((4, 128, 128), BF16),
    pltpu.VMEM((4, 128, 128), F32),
    pltpu.VMEM((4, 128, 128), F32),
    pltpu.VMEM((4, 128, 128), F32),
    pltpu.VMEM((4, 128, 128), F32),
    pltpu.VMEM((3, 128, 256), F32),
    pltpu.VMEM((4, 128, 256), F32),
    pltpu.VMEM((3, 128, 128), F32),
    pltpu.VMEM((3, 128, 128), F32),
    pltpu.VMEM((256, 256), BF16),
    pltpu.VMEM((512, 512), BF16),
    pltpu.VMEM((256, 1024), BF16),
    pltpu.SemaphoreType.DMA((8,)),
    pltpu.SemaphoreType.DMA((8,)),
    pltpu.SemaphoreType.DMA((8,)),
    pltpu.SemaphoreType.DMA((8,)),
    pltpu.SemaphoreType.DMA((8,)),
    pltpu.SemaphoreType.DMA((6,)),
    pltpu.SemaphoreType.DMA((6,)),
]


def finish_kernel(*refs):
    copies = [
        pltpu.make_async_copy(refs[index], refs[8 + index], refs[16].at[index]) for index in range(8)
    ]
    for copy in copies:
        copy.start()
    for copy in copies:
        copy.wait()


RESULTS = [
    jax.ShapeDtypeStruct((256, 256), BF16),
    jax.ShapeDtypeStruct((256, 128), F32),
    jax.ShapeDtypeStruct((256, 128), F32),
    jax.ShapeDtypeStruct((256, 256), F32),
    jax.ShapeDtypeStruct((256, 256), F32),
    jax.ShapeDtypeStruct((2, 256), F32),
    jax.ShapeDtypeStruct((2, 256), F32),
    jax.ShapeDtypeStruct((64, 256), F32),
]


def per_device(
    query_rows, key_rows, value_rows, output_gate, write_rate, log_decay,
    out_weight, out_cotangent, block_response, prefix_owner,
):
    vmem = pl.BlockSpec(memory_space=pltpu.VMEM)
    smem = pl.BlockSpec(memory_space=pltpu.SMEM)
    whole = pl.BlockSpec(memory_space=pl.ANY)
    results = pl.pallas_call(
        layer_kernel,
        out_shape=RESULTS,
        in_specs=[whole] * 8 + [smem] * 2,
        out_specs=[vmem] * 8,
        scratch_shapes=SCRATCH,
        compiler_params=pltpu.CompilerParams(
            collective_id=0, has_side_effects=True, vmem_limit_bytes=56 * 1024 * 1024
        ),
    )(
        query_rows, key_rows, value_rows, output_gate, write_rate, log_decay,
        out_weight, out_cotangent, block_response, prefix_owner,
    )
    return pl.pallas_call(
        finish_kernel,
        out_shape=RESULTS,
        in_specs=[whole] * 8,
        out_specs=[whole] * 8,
        scratch_shapes=[pltpu.SemaphoreType.DMA((8,))],
    )(*results)


def solution(mesh):
    rows = P("seq", "head")
    return jax.shard_map(
        per_device,
        mesh=mesh,
        in_specs=(rows, rows, rows, rows, P("head", "seq"), P("head", "seq"), P(None, "head"), rows, P(), P()),
        out_specs=(rows, rows, rows, rows, rows, P("head", "seq"), P("head", "seq"), rows),
        check_vma=False,
    )
```

```python
import functools

import jax
import jax.numpy as jnp
from jax import lax
from jax.experimental import pallas as pl
from jax.experimental.pallas import tpu as pltpu
from jax.sharding import PartitionSpec as P

N_SEQ = 32
N_HEAD = 8
CHIPS = 16
SPAN = 64
EPS = 1e-06
F32 = jnp.float32
BF16 = jnp.bfloat16
HIGHEST = lax.Precision.HIGHEST
MESH = pl.DeviceIdType.MESH
SCALE = 128 ** (-0.5)

KINDS = {"nn": ((1,), (0,)), "nt": ((1,), (1,)), "tn": ((0,), (0,))}


def dot(a, b, kind="nn"):
    return lax.dot_general(
        a.astype(BF16), b.astype(BF16), (KINDS[kind], ((), ())), preferred_element_type=F32
    )


def parts(x):
    high = x.astype(BF16)
    return high, (x - high.astype(F32)).astype(BF16)


def dot3(a, b, kind="nn"):
    a_high, a_low = parts(a)
    b_high, b_low = parts(b)
    return dot(a_high, b_high, kind) + (dot(a_high, b_low, kind) + dot(a_low, b_high, kind))


def dot_exact(a, b):
    return lax.dot_general(
        a, b, (KINDS["nn"], ((), ())), precision=HIGHEST, preferred_element_type=F32
    )


def iotas(shape=(128, 128)):
    return lax.broadcasted_iota(jnp.int32, shape, 0), lax.broadcasted_iota(jnp.int32, shape, 1)


def stack_heads(x):
    return jnp.concatenate([x[:, :128], x[:, 128:]], axis=0)


def side_heads(x):
    return jnp.concatenate([x[:64], x[64:]], axis=1)


def diagonal_heads(x):
    zero = jnp.zeros_like(x[:64])
    return jnp.concatenate(
        [jnp.concatenate([x[:64], zero], axis=1), jnp.concatenate([zero, x[64:]], axis=1)], axis=0
    )


def twice(x):
    return jnp.concatenate([x, x], axis=0)


def fold(x):
    return x[:64] + x[64:]


def half_swap(x):
    return jnp.concatenate([x[:, 64:], x[:, :64]], axis=1)


def by_block(x):
    lower = lax.broadcasted_iota(jnp.int32, (1, 128), 1) < 64
    rows = []
    for pair in range(2):
        first = x[0:1, 128 * pair : 128 * pair + 128]
        second = x[1:2, 128 * pair : 128 * pair + 128]
        rows.append(jnp.where(lower, first, half_swap(second)))
        rows.append(jnp.where(lower, half_swap(first), second))
    return jnp.concatenate(rows, axis=0)


def by_head(x):
    lower = lax.broadcasted_iota(jnp.int32, (1, 128), 1) < 64
    heads = ([], [])
    for pair in range(2):
        even, odd = x[2 * pair : 2 * pair + 1], x[2 * pair + 1 : 2 * pair + 2]
        heads[0].append(jnp.where(lower, even, half_swap(odd)))
        heads[1].append(jnp.where(lower, half_swap(even), odd))
    return jnp.concatenate([jnp.concatenate(row, axis=1) for row in heads], axis=0)


def turned(x):
    return jnp.transpose(jnp.concatenate([x, jnp.zeros((120, 128), F32)], axis=0))


def unit_scale(x):
    return lax.rsqrt(jnp.sum(x * x, axis=-1, keepdims=True) + EPS)


def unit_back(raw, grad, scale):
    inv = unit_scale(raw)
    unit = raw * inv
    return (scale * inv) * (grad - unit * jnp.sum(grad * unit, axis=-1, keepdims=True))


def running_decay(write_rate, log_decay):
    row, col = iotas()
    same = (row >> 6) == (col >> 6)
    upto = jnp.where(same & (row <= col), 1.0, 0.0).astype(F32)
    both = jnp.concatenate([by_block(log_decay), by_block(write_rate)], axis=0)
    summed = dot_exact(both, upto)
    rows = jnp.concatenate([summed[:4], both[4:]], axis=0)
    return rows[:4], turned(rows)


def block_columns(rows, columns, b):
    cum_row = rows[b : b + 1]
    cum = columns[:, b : b + 1]
    rate = columns[:, 4 + b : 5 + b]
    first = lax.broadcasted_iota(jnp.int32, (128, 1), 0) < 64
    last = jnp.where(first, cum_row[:, 63:64], cum_row[:, 127:128])
    return cum_row, cum, rate, jnp.exp(cum), jnp.exp(last - cum)


def last_growth(rows, b):
    lane = lax.broadcasted_iota(jnp.int32, (1, 256), 1)
    return jnp.exp(jnp.where(lane < 128, rows[b : b + 1, 63:64], rows[b : b + 1, 127:128]))


def block_tables(query, key, rows, columns, b):
    row, col = iotas()
    causal = ((row >> 6) == (col >> 6)) & (row >= col)
    cum_row, cum, rate, _, _ = block_columns(rows, columns, b)
    within = jnp.where(causal, jnp.exp(jnp.where(causal, cum - cum_row, 0.0)), 0.0)
    key2 = twice(key)
    strict = jnp.where(row > col, within, 0.0) * rate
    system = strict * dot3(key2, key2, "nt")
    query_key = dot3(twice(query), key2, "nt") * within
    return within, system, query_key


def inverse(systems):
    row, col = iotas()
    found = None
    for level in range(6):
        here = ((row >> (level + 1)) == (col >> (level + 1))) & ((row >> level) != (col >> level))
        below = [jnp.where(here, system, 0.0) for system in systems]
        if found is None:
            eye = jnp.where(row == col, 1.0, 0.0).astype(F32)
            found = [eye - one for one in below]
        else:
            half = [dot3(one, two) for one, two in zip(found, below)]
            found = [one - dot3(two, one) for one, two in zip(found, half)]
    return found


def gated(out, gate):
    inv = lax.rsqrt(jnp.mean(out * out, axis=-1, keepdims=True) + EPS)
    return out * inv * (gate / (1.0 + jnp.exp(-gate)))


def gated_back(out, gate, grad):
    inv = lax.rsqrt(jnp.mean(out * out, axis=-1, keepdims=True) + EPS)
    sig = 1.0 / (1.0 + jnp.exp(-gate))
    weighted = grad * (gate * sig)
    grad_gate = grad * out * inv * (sig * (1.0 + gate * (1.0 - sig)))
    along = jnp.mean(weighted * out, axis=-1, keepdims=True)
    return inv * (weighted - out * (inv * inv * along)), grad_gate


def block_grads(
    query, key, value, cols, growth_last, tables, step, update, grad_out, grad_state, state_in
):
    _, _, rate, growth, remain = cols
    within, system, query_key = tables
    row, col = iotas()
    key2, query2 = twice(key), twice(query)
    grad_scores = dot3(grad_out, update, "nt")
    grad_system = -dot(step, update, "nt")
    masked = grad_scores * within
    strict = jnp.where(row > col, grad_system * within, 0.0) * rate
    pulled = grad_system * system
    spread = grad_scores * query_key + pulled
    grad_query = fold(dot(masked, key2))
    state_key = dot(diagonal_heads(update), grad_state, "nt")
    grad_key = fold(
        dot(masked, query2, "tn") + dot(strict, key2) + dot(strict, key2, "tn") + remain * state_key
    )
    tail = remain * jnp.sum(key2 * state_key, axis=-1, keepdims=True)
    grad_cum = jnp.sum(spread, axis=-1, keepdims=True) - tail
    grad_row = -jnp.sum(spread, axis=0, keepdims=True)
    end0 = jnp.sum(tail[:64], axis=0, keepdims=True)
    end1 = jnp.sum(tail[64:], axis=0, keepdims=True)
    grad_value = rate * step
    if state_in is None:
        inner = value
    else:
        state, key_state, query_state = state_in
        inner = value - growth * key_state
        out_growth = growth * grad_out
        in_growth = growth * grad_value
        grad_cum += jnp.sum(out_growth * query_state - in_growth * key_state, axis=-1, keepdims=True)
        grad_query += dot3(side_heads(out_growth), state, "nt")
        grad_key -= dot(side_heads(in_growth), state, "nt")
        kept = jnp.sum(growth_last * (state * grad_state), axis=0, keepdims=True)
        end0 += jnp.sum(kept[:, :128], axis=1, keepdims=True)
        end1 += jnp.sum(kept[:, 128:], axis=1, keepdims=True)
    lane = lax.broadcasted_iota(jnp.int32, (1, 128), 1)
    grad_row += jnp.where(lane == 63, end0, 0.0) + jnp.where(lane == 127, end1, 0.0)
    grad_rate = jnp.sum(step * inner, axis=-1, keepdims=True) + (
        jnp.sum(pulled, axis=-1, keepdims=True) / rate
    )
    return grad_query, grad_key, grad_value, grad_rate, grad_cum, grad_row


def decay_grads(grad_cums, grad_rates, grad_rows):
    row, col = iotas()
    packed = jnp.zeros((128, 128), F32)
    for b in range(4):
        packed = jnp.where(col == b, grad_cums[b], packed)
        packed = jnp.where(col == 4 + b, grad_rates[b], packed)
    packed = jnp.transpose(packed)[:8]
    since = jnp.where(((row >> 6) == (col >> 6)) & (row >= col), 1.0, 0.0).astype(F32)
    grad_cum = packed[:4] + jnp.concatenate(grad_rows, axis=0)
    grad_cum = jnp.concatenate([grad_cum, jnp.zeros((4, 128), F32)], axis=0)
    return by_head(packed[4:]), by_head(dot_exact(grad_cum, since)[:4])


def rows_of(index, size):
    return pl.ds(pl.multiple_of(index * size, size), size)


def send(src, dst, send_sem, recv_sem, device):
    copy = pltpu.make_async_remote_copy(
        src_ref=src,
        dst_ref=dst,
        send_sem=send_sem,
        recv_sem=recv_sem,
        device_id=device,
        device_id_type=MESH,
    )
    copy.start()


def await_bytes(ref, sem):
    pltpu.make_async_copy(ref, ref, sem).wait()


def layer_kernel(
    query_hbm,
    key_hbm,
    value_hbm,
    gate_hbm,
    rate_hbm,
    decay_hbm,
    weight_hbm,
    cot_hbm,
    response_ref,
    owner_ref,
    layer_ref,
    grad_query_ref,
    grad_key_ref,
    grad_value_ref,
    grad_gate_ref,
    grad_rate_ref,
    grad_decay_ref,
    grad_weight_ref,
    query_ref,
    key_ref,
    value_ref,
    gate_ref,
    rate_ref,
    decay_ref,
    weight_ref,
    cot_ref,
    cots,
    piece_src,
    pieces,
    chosen_src,
    chosen,
    starts,
    grad_src,
    grad_pieces,
    owned_src,
    owned,
    sums_src,
    sums,
    weight_src,
    weight_pair,
    weight_sum,
    weight_in,
    within_s,
    system_s,
    scores_s,
    inverse_s,
    outs_s,
    update_s,
    step_s,
    grad_out_s,
    state_s,
    grad_state_s,
    key_state_s,
    query_state_s,
    normed_s,
    share_s,
    pick_s,
    gather_s,
    load_sem,
    ring_send,
    ring_recv,
    sum_send,
    sum_recv,
    seq_send,
    seq_recv,
):
    me = lax.axis_index("seq")
    head = lax.axis_index("head")
    chip, core = me // 2, me % 2
    right, left = (head + 1) % N_HEAD, (head + N_HEAD - 1) % N_HEAD

    loads = [
        pltpu.make_async_copy(src, dst, load_sem.at[index])
        for index, (src, dst) in enumerate(
            (
                (rate_hbm, rate_ref),
                (decay_hbm, decay_ref),
                (key_hbm, key_ref),
                (query_hbm, query_ref),
                (value_hbm, value_ref),
                (gate_hbm, gate_ref),
                (cot_hbm, cot_ref),
                (weight_hbm, weight_ref),
            )
        )
    ]
    for load in loads:
        load.start()

    barrier = pltpu.get_barrier_semaphore()

    def greet(offset, carry):
        pl.semaphore_signal(
            barrier, inc=1, device_id={"seq": (me + offset) % N_SEQ}, device_id_type=MESH
        )
        return carry

    lax.fori_loop(1, N_SEQ, greet, 0)
    for neighbour in (left, right):
        pl.semaphore_signal(barrier, inc=1, device_id={"head": neighbour}, device_id_type=MESH)

    def ring_order(hop, to_right):
        order = (0, 1, 2, 3) if to_right else (2, 3, 0, 1)
        return order[:2] if hop == 4 else order

    def ring_chunk(hop, to_right, chunk):
        slot = hop - 1 if to_right or hop == 4 else 3 + hop
        return cots.at[slot, pl.ds(64 * chunk, 64)]

    def ring_index(hop, to_right, chunk):
        return 8 * (hop - 1) + (0 if to_right else 4) + chunk

    def ring_start(hop, to_right, chunk):
        if hop == 1:
            src = cot_hbm.at[pl.ds(64 * chunk, 64)]
        else:
            src = ring_chunk(hop - 1, to_right, chunk)
        send(
            src,
            ring_chunk(hop, to_right, chunk),
            ring_send.at[0],
            ring_recv.at[ring_index(hop, to_right, chunk)],
            {"head": right if to_right else left},
        )

    def ring_relay(hop):
        for place in range(2 if hop == 4 else 4):
            for to_right in (True, False):
                chunk = ring_order(hop, to_right)[place]
                await_bytes(
                    ring_chunk(hop, to_right, chunk), ring_recv.at[ring_index(hop, to_right, chunk)]
                )
                if hop < 4 and chunk in ring_order(hop + 1, to_right):
                    ring_start(hop + 1, to_right, chunk)

    for load in loads[:5]:
        load.wait()
    rate2, decay2 = rate_ref[...], decay_ref[...]
    rows, columns = running_decay(rate2, decay2)

    def unit_block(ref, b):
        raw = ref[SPAN * b : SPAN * b + SPAN, :].astype(F32)
        return raw * unit_scale(raw)

    def block_of(ref, b):
        return stack_heads(ref[SPAN * b : SPAN * b + SPAN, :]).astype(F32)

    queries = [unit_block(query_ref, b) * SCALE for b in range(4)]
    keys = [unit_block(key_ref, b) for b in range(4)]
    cols = [block_columns(rows, columns, b) for b in range(4)]

    def tables_of(b):
        within, system, query_key = block_tables(queries[b], keys[b], rows, columns, b)
        within_s[b] = within
        system_s[b] = system
        scores_s[b] = query_key
        return system

    def tail_of(b):
        return twice(keys[b]) * cols[b][4]

    first_system = tables_of(0)
    pl.semaphore_wait(barrier, N_SEQ + 1)
    for place in range(4):
        for to_right in (True, False):
            ring_start(1, to_right, ring_order(1, to_right)[place])
    inverse_s[0] = inverse([first_system])[0].astype(BF16)
    update = dot(inverse_s[0], cols[0][2] * block_of(value_ref, 0))
    update_s[0] = update
    final = dot(tail_of(0), diagonal_heads(update), "tn")
    piece_src[0:128, :] = final[:, :128].astype(BF16)
    piece_src[128:256, :] = final[:, 128:].astype(BF16)

    def send_pieces(offset, carry):
        to = (me + offset) % N_SEQ
        send(
            piece_src.at[rows_of(to // 2, 16)],
            pieces.at[rows_of(offset - 1, 16)],
            seq_send.at[0],
            seq_recv.at[0],
            {"seq": to},
        )
        return carry

    lax.fori_loop(1, N_SEQ, send_pieces, 0)
    pieces[496:512, :] = piece_src[rows_of(chip, 16), :]

    def owner_of(device, slot):
        prompt = (response_ref[3 * device] >> 1) + slot
        found = owner_ref[jnp.minimum(prompt, N_SEQ - 1)]
        return jnp.where(prompt < N_SEQ, found, -1)

    row, col = iotas((32, 512))
    source = (me + 31 - (col >> 4)) % N_SEQ
    for place in range(CHIPS):
        to = 2 * ((chip + place + 1) % CHIPS) + core
        wanted = jnp.where(row < 16, owner_of(to, 0), owner_of(to, 1))
        here = (source == wanted) & ((row & 15) == (col & 15))
        pick_s[32 * place : 32 * place + 32, :] = jnp.where(here, 1.0, 0.0).astype(BF16)

    for quarter in range(8):
        columns_here = []
        for place in range(4 * quarter, 4 * quarter + 4):
            device = (me + 31 - place) % N_SEQ
            columns_here.append((owner_of(device, 0), owner_of(device, 1)))
        row, col = iotas((256, 128))
        owner = jnp.full((256, 128), -1, jnp.int32)
        for index, (one, two) in enumerate(columns_here):
            owner = jnp.where((col >> 4) == 2 * index, one, owner)
            owner = jnp.where((col >> 4) == 2 * index + 1, two, owner)
        target = 2 * ((chip + 1 + (row >> 4)) % CHIPS) + core
        here = (owner == target) & ((row & 15) == (col & 15))
        gather_s[:, 128 * quarter : 128 * quarter + 128] = jnp.where(here, 1.0, 0.0).astype(BF16)

    systems = [tables_of(b) for b in (1, 2, 3)]
    ring_relay(1)
    for b, found in zip((1, 2, 3), inverse(systems)):
        inverse_s[b] = found.astype(BF16)
    ring_relay(2)

    await_bytes(pieces.at[pl.ds(0, 496)], seq_recv.at[0])

    chosen_src[...] = dot(pick_s[...], pieces[...]).astype(BF16)

    def send_chosen(offset, carry):
        send(
            chosen_src.at[rows_of(offset - 1, 32)],
            chosen.at[rows_of(offset - 1, 32)],
            seq_send.at[1],
            seq_recv.at[1],
            {"seq": 2 * ((chip + offset) % CHIPS) + core},
        )
        return carry

    lax.fori_loop(1, CHIPS, send_chosen, 0)
    chosen[480:512, :] = chosen_src[480:512, :]

    loads[5].wait()

    def norm_block(b, out):
        outs_s[b] = out
        result = side_heads(gated(out, block_of(gate_ref, b))).astype(BF16)
        normed_s[SPAN * b : SPAN * b + SPAN, :] = result

    norm_block(0, dot3(scores_s[0], update_s[0]))
    ring_relay(3)

    await_bytes(chosen.at[pl.ds(0, 480)], seq_recv.at[1])
    for slot in range(2):
        for piece in range(CHIPS):
            place = (chip - piece + 15) % CHIPS
            starts[slot, 16 * (piece % 8) : 16 * (piece % 8) + 16, 128 * (piece // 8) : 128 * (piece // 8) + 128] = (
                chosen[pl.ds(pl.multiple_of(place * 32 + 16 * slot, 16), 16), :].astype(F32)
            )
    own = [response_ref[3 * me + j] for j in range(3)]
    fresh, later = [None, None], [None, None]
    for j in (1, 2):
        fresh.append(jnp.where(own[j] != own[j - 1], 1.0, 0.0).astype(F32))
        later.append(jnp.where((own[j] >> 1) != (own[0] >> 1), 1.0, 0.0).astype(F32))

    state = None
    for b in (1, 2, 3):
        if b == 1:
            state = starts[0]
        else:
            begun = (1.0 - later[b]) * starts[0] + later[b] * starts[1]
            state = fresh[b] * begun + (1.0 - fresh[b]) * state
        state_s[b - 1] = state
        _, _, rate, growth, _ = cols[b]
        both = dot3(jnp.concatenate([keys[b], queries[b]], axis=0), state)
        key_state, query_state = stack_heads(both[:64]), stack_heads(both[64:])
        key_state_s[b - 1] = key_state
        query_state_s[b - 1] = query_state
        update = dot(inverse_s[b], rate * (block_of(value_ref, b) - growth * key_state))
        update_s[b] = update
        if b < 3:
            state = last_growth(rows, b) * state + dot(tail_of(b), diagonal_heads(update), "tn")
        norm_block(b, growth * query_state + dot3(scores_s[b], update))

    def share(distance):
        block = (head + distance + N_HEAD) % N_HEAD
        return dot(normed_s[...], weight_ref[rows_of(block, 256), :], "nt")

    def sums_order(hop, to_right):
        if hop == 1:
            return (0, 1) if to_right else (2, 3)
        return (2, 3, 0, 1) if to_right else (0, 1, 2, 3)

    def sums_slot(hop, to_right):
        return 2 * (hop - 1) + (0 if to_right else 1)

    def sums_start(hop, to_right, chunk):
        here = (sums_slot(hop, to_right), pl.ds(64 * chunk, 64))
        send(
            sums_src.at[here],
            sums.at[here],
            sum_send.at[0],
            sum_recv.at[ring_index(hop, to_right, chunk)],
            {"head": right if to_right else left},
        )

    def sums_prepare(hop):
        for to_right in (True, False):
            share_s[sums_slot(hop, to_right)] = share(5 - hop if to_right else hop - 5)

    def sums_begin():
        across = share(4)
        for to_right in (True, False):
            low = 0 if to_right else 128
            sums_src[sums_slot(1, to_right), low : low + 128, :] = across[low : low + 128].astype(BF16)
        for place in range(2):
            for to_right in (True, False):
                sums_start(1, to_right, sums_order(1, to_right)[place])
        sums_prepare(2)
        for to_right in (True, False):
            slot, low = sums_slot(2, to_right), 128 if to_right else 0
            sums_src[slot, low : low + 128, :] = share_s[slot, low : low + 128, :].astype(BF16)
        for place in range(2):
            for to_right in (True, False):
                sums_start(2, to_right, sums_order(2, to_right)[place])

    def sums_await(hop, to_right, chunk):
        here = (sums_slot(hop, to_right), pl.ds(64 * chunk, 64))
        await_bytes(sums.at[here], sum_recv.at[ring_index(hop, to_right, chunk)])

    def sums_relay(hop):
        for place in range(2 if hop == 1 else 4):
            for to_right in (True, False):
                chunk = sums_order(hop, to_right)[place]
                sums_await(hop, to_right, chunk)
                if hop < 4:
                    here = slice(64 * chunk, 64 * chunk + 64)
                    slot = sums_slot(hop + 1, to_right)
                    sums_src[slot, here, :] = (
                        share_s[slot, here, :]
                        + sums[sums_slot(hop, to_right), here, :].astype(F32)
                    ).astype(BF16)
                    sums_start(hop + 1, to_right, chunk)
        if hop < 3:
            sums_prepare(hop + 2)

    loads[7].wait()
    sums_begin()

    ring_relay(4)
    loads[6].wait()

    def cot_slots():
        yield cot_ref, head
        for hop in (1, 2, 3, 4):
            yield cots.at[hop - 1], (head - hop + N_HEAD) % N_HEAD
        for hop in (1, 2, 3):
            yield cots.at[3 + hop], (head + hop) % N_HEAD

    grad_normed = None
    for slot_ref, block in cot_slots():
        term = dot(slot_ref[...], weight_ref[rows_of(block, 256), :])
        grad_normed = term if grad_normed is None else grad_normed + term
    for b in range(4):
        grad_out, grad_gate = gated_back(
            outs_s[b], block_of(gate_ref, b), stack_heads(grad_normed[SPAN * b : SPAN * b + SPAN])
        )
        grad_out_s[b] = grad_out
        grad_gate_ref[SPAN * b : SPAN * b + SPAN, :] = side_heads(grad_gate)

    grad_state = jnp.zeros((128, 256), F32)
    begun = [jnp.zeros((128, 256), F32), jnp.zeros((128, 256), F32)]
    for b in (3, 2, 1):
        _, _, rate, growth, remain = cols[b]
        grad_out = grad_out_s[b]
        grad_state_s[b] = grad_state
        grad_update = dot(scores_s[b], grad_out, "tn")
        if b < 3:
            grad_update += remain * stack_heads(dot(keys[b], grad_state))
        step = dot(inverse_s[b], grad_update, "tn")
        step_s[b] = step
        sides = jnp.concatenate(
            [side_heads(-(rate * growth) * step), side_heads(growth * grad_out)], axis=0
        )
        grad_in = dot(jnp.concatenate([keys[b], queries[b]], axis=0), sides, "tn")
        if b < 3:
            grad_in += last_growth(rows, b) * grad_state
        if b > 1:
            begun[0] += (fresh[b] * (1.0 - later[b])) * grad_in
            begun[1] += (fresh[b] * later[b]) * grad_in
            grad_state = (1.0 - fresh[b]) * grad_in
        else:
            begun[0] += grad_in
    for slot in range(2):
        for piece in range(CHIPS):
            grad_src[32 * piece + 16 * slot : 32 * piece + 16 * slot + 16, :] = begun[slot][
                16 * (piece % 8) : 16 * (piece % 8) + 16,
                128 * (piece // 8) : 128 * (piece // 8) + 128,
            ].astype(BF16)

    def send_grads(offset, carry):
        to = (me + offset) % N_SEQ
        send(
            grad_src.at[rows_of(to // 2, 32)],
            grad_pieces.at[rows_of(offset - 1, 32)],
            seq_send.at[2],
            seq_recv.at[2],
            {"seq": to},
        )
        return carry

    lax.fori_loop(1, N_SEQ, send_grads, 0)
    grad_pieces[992:1024, :] = grad_src[rows_of(chip, 32), :]

    sums_relay(1)
    for slot_ref, block in cot_slots():
        share_w = dot(slot_ref[...], normed_s[...], "tn").astype(BF16)
        for quarter in range(4):
            place = (quarter % 2) * 1024 + (2 * block + quarter // 2) * 64
            weight_src[pl.ds(pl.multiple_of(place, 64), 64), :] = share_w[
                64 * quarter : 64 * quarter + 64
            ]
    send(
        weight_src.at[rows_of(1 - core, 1024)],
        weight_pair,
        seq_send.at[4],
        seq_recv.at[4],
        {"seq": 2 * chip + 1 - core},
    )

    sums_relay(2)

    await_bytes(grad_pieces.at[pl.ds(0, 992)], seq_recv.at[2])

    owned_src[...] = dot(gather_s[...], grad_pieces[...]).astype(BF16)

    def send_owned(offset, carry):
        send(
            owned_src.at[rows_of(offset - 1, 16)],
            owned.at[rows_of(offset - 1, 16)],
            seq_send.at[3],
            seq_recv.at[3],
            {"seq": 2 * ((chip + offset) % CHIPS) + core},
        )
        return carry

    lax.fori_loop(1, CHIPS, send_owned, 0)
    owned[240:256, :] = owned_src[240:256, :]

    await_bytes(weight_pair, seq_recv.at[4])
    for part in range(4):
        place = core * 1024 + 256 * part
        weight_sum[256 * part : 256 * part + 256, :] = (
            weight_src[pl.ds(pl.multiple_of(place, 256), 256), :].astype(F32)
            + weight_pair[256 * part : 256 * part + 256, :].astype(F32)
        ).astype(BF16)

    def send_weight(offset, carry):
        to = (chip + offset) % CHIPS
        send(
            weight_sum.at[rows_of(to, 64)],
            weight_in.at[rows_of(offset - 1, 64)],
            seq_send.at[5],
            seq_recv.at[5],
            {"seq": 2 * to + core},
        )
        return carry

    lax.fori_loop(1, CHIPS, send_weight, 0)

    grad_cums, grad_rates, grad_rows = [None] * 4, [None] * 4, [None] * 4

    def finish_block(b, grad_state, state_in):
        tables = (within_s[b], system_s[b], scores_s[b])
        found = block_grads(
            queries[b],
            keys[b],
            block_of(value_ref, b),
            cols[b],
            last_growth(rows, b),
            tables,
            step_s[b],
            update_s[b],
            grad_out_s[b],
            grad_state,
            state_in,
        )
        for raw_ref, out_ref, grad, scale in (
            (query_ref, grad_query_ref, found[0], SCALE),
            (key_ref, grad_key_ref, found[1], 1.0),
        ):
            raw = raw_ref[SPAN * b : SPAN * b + SPAN, :].astype(F32)
            out_ref[SPAN * b : SPAN * b + SPAN, :] = unit_back(raw, grad, scale)
        grad_value_ref[SPAN * b : SPAN * b + SPAN, :] = side_heads(found[2])
        grad_rates[b], grad_cums[b], grad_rows[b] = found[3:]

    for b in (1, 2, 3):
        finish_block(b, grad_state_s[b], (state_s[b - 1], key_state_s[b - 1], query_state_s[b - 1]))
        if b == 1:
            sums_relay(3)

    await_bytes(owned.at[pl.ds(0, 240)], seq_recv.at[3])
    for piece in range(CHIPS):
        place = (chip - piece + 15) % CHIPS
        grad_state_s[0, 16 * (piece % 8) : 16 * (piece % 8) + 16, 128 * (piece // 8) : 128 * (piece // 8) + 128] = (
            owned[rows_of(place, 16), :].astype(F32)
        )
    grad_state = grad_state_s[0]
    grad_update = dot(scores_s[0], grad_out_s[0], "tn")
    grad_update += cols[0][4] * stack_heads(dot(keys[0], grad_state))
    step_s[0] = dot(inverse_s[0], grad_update, "tn")
    finish_block(0, grad_state, None)
    grad_rate_ref[...], grad_decay_ref[...] = decay_grads(grad_cums, grad_rates, grad_rows)

    await_bytes(weight_in.at[pl.ds(0, 15 * 64)], seq_recv.at[5])
    total = weight_sum[rows_of(chip, 64), :].astype(F32)
    for slot in range(15):
        total += weight_in[64 * slot : 64 * slot + 64, :].astype(F32)
    grad_weight_ref[...] = total
    total = share(0)
    sums_relay(4)
    layer_ref[...] = (total + sums[6].astype(F32) + sums[7].astype(F32)).astype(BF16)

    await_bytes(cots, ring_send.at[0])
    await_bytes(sums.at[pl.ds(0, 7)], sum_send.at[0])
    await_bytes(pieces.at[pl.ds(0, 496)], seq_send.at[0])
    await_bytes(chosen.at[pl.ds(0, 480)], seq_send.at[1])
    await_bytes(grad_pieces.at[pl.ds(0, 992)], seq_send.at[2])
    await_bytes(owned.at[pl.ds(0, 240)], seq_send.at[3])
    await_bytes(weight_pair, seq_send.at[4])
    await_bytes(weight_in.at[pl.ds(0, 15 * 64)], seq_send.at[5])


SCRATCH = [
    pltpu.VMEM((256, 128), BF16),
    pltpu.VMEM((256, 128), BF16),
    pltpu.VMEM((256, 256), BF16),
    pltpu.VMEM((256, 256), BF16),
    pltpu.VMEM((2, 256), F32),
    pltpu.VMEM((2, 256), F32),
    pltpu.VMEM((2048, 256), BF16),
    pltpu.VMEM((256, 256), BF16),
    pltpu.VMEM((7, 256, 256), BF16),
    pltpu.VMEM((256, 128), BF16),
    pltpu.VMEM((512, 128), BF16),
    pltpu.VMEM((512, 128), BF16),
    pltpu.VMEM((512, 128), BF16),
    pltpu.VMEM((2, 128, 256), F32),
    pltpu.VMEM((512, 128), BF16),
    pltpu.VMEM((1024, 128), BF16),
    pltpu.VMEM((256, 128), BF16),
    pltpu.VMEM((256, 128), BF16),
    pltpu.VMEM((8, 256, 256), BF16),
    pltpu.VMEM((8, 256, 256), BF16),
    pltpu.VMEM((2048, 256), BF16),
    pltpu.VMEM((1024, 256), BF16),
    pltpu.VMEM((1024, 256), BF16),
    pltpu.VMEM((960, 256), BF16),
    pltpu.VMEM((4, 128, 128), F32),
    pltpu.VMEM((4, 128, 128), F32),
    pltpu.VMEM((4, 128, 128), F32),
    pltpu.VMEM((4, 128, 128), BF16),
    pltpu.VMEM((4, 128, 128), F32),
    pltpu.VMEM((4, 128, 128), F32),
    pltpu.VMEM((4, 128, 128), F32),
    pltpu.VMEM((4, 128, 128), F32),
    pltpu.VMEM((3, 128, 256), F32),
    pltpu.VMEM((4, 128, 256), F32),
    pltpu.VMEM((3, 128, 128), F32),
    pltpu.VMEM((3, 128, 128), F32),
    pltpu.VMEM((256, 256), BF16),
    pltpu.VMEM((8, 256, 256), F32),
    pltpu.VMEM((512, 512), BF16),
    pltpu.VMEM((256, 1024), BF16),
    pltpu.SemaphoreType.DMA((8,)),
    pltpu.SemaphoreType.DMA((1,)),
    pltpu.SemaphoreType.DMA((32,)),
    pltpu.SemaphoreType.DMA((1,)),
    pltpu.SemaphoreType.DMA((32,)),
    pltpu.SemaphoreType.DMA((6,)),
    pltpu.SemaphoreType.DMA((6,)),
]


def finish_kernel(*refs):
    for index in range(8):
        refs[8 + index][...] = refs[index][...]


RESULTS = [
    jax.ShapeDtypeStruct((256, 256), BF16),
    jax.ShapeDtypeStruct((256, 128), F32),
    jax.ShapeDtypeStruct((256, 128), F32),
    jax.ShapeDtypeStruct((256, 256), F32),
    jax.ShapeDtypeStruct((256, 256), F32),
    jax.ShapeDtypeStruct((2, 256), F32),
    jax.ShapeDtypeStruct((2, 256), F32),
    jax.ShapeDtypeStruct((64, 256), F32),
]


def per_device(
    query_rows, key_rows, value_rows, output_gate, write_rate, log_decay,
    out_weight, out_cotangent, block_response, prefix_owner,
):
    vmem = pl.BlockSpec(memory_space=pltpu.VMEM)
    smem = pl.BlockSpec(memory_space=pltpu.SMEM)
    whole = pl.BlockSpec(memory_space=pl.ANY)
    results = pl.pallas_call(
        layer_kernel,
        out_shape=RESULTS,
        in_specs=[whole] * 8 + [smem] * 2,
        out_specs=[vmem] * 8,
        scratch_shapes=SCRATCH,
        compiler_params=pltpu.CompilerParams(
            collective_id=0, has_side_effects=True, vmem_limit_bytes=56 * 1024 * 1024
        ),
    )(
        query_rows, key_rows, value_rows, output_gate, write_rate, log_decay,
        out_weight, out_cotangent, block_response, prefix_owner,
    )
    return pl.pallas_call(
        finish_kernel,
        out_shape=RESULTS,
        in_specs=[vmem] * 8,
        out_specs=[vmem] * 8,
    )(*results)


def solution(mesh):
    rows = P("seq", "head")
    return jax.shard_map(
        per_device,
        mesh=mesh,
        in_specs=(rows, rows, rows, rows, P("head", "seq"), P("head", "seq"), P(None, "head"), rows, P(), P()),
        out_specs=(rows, rows, rows, rows, rows, P("head", "seq"), P("head", "seq"), rows),
        check_vma=False,
    )
```

```python
import functools

import jax
import jax.numpy as jnp
from jax import lax
from jax.experimental import pallas as pl
from jax.experimental.pallas import tpu as pltpu
from jax.sharding import PartitionSpec as P

N_SEQ = 32
N_HEAD = 8
CHIPS = 16
SPAN = 64
EPS = 1e-06
F32 = jnp.float32
BF16 = jnp.bfloat16
HIGHEST = lax.Precision.HIGHEST
MESH = pl.DeviceIdType.MESH
SCALE = 128 ** (-0.5)

KINDS = {"nn": ((1,), (0,)), "nt": ((1,), (1,)), "tn": ((0,), (0,))}


def dot(a, b, kind="nn"):
    return lax.dot_general(
        a.astype(BF16), b.astype(BF16), (KINDS[kind], ((), ())), preferred_element_type=F32
    )


def parts(x):
    high = x.astype(BF16)
    return high, (x - high.astype(F32)).astype(BF16)


def dot3(a, b, kind="nn"):
    a_high, a_low = parts(a)
    b_high, b_low = parts(b)
    return dot(a_high, b_high, kind) + (dot(a_high, b_low, kind) + dot(a_low, b_high, kind))


def dot_exact(a, b):
    return lax.dot_general(
        a, b, (KINDS["nn"], ((), ())), precision=HIGHEST, preferred_element_type=F32
    )


def iotas(shape=(128, 128)):
    return lax.broadcasted_iota(jnp.int32, shape, 0), lax.broadcasted_iota(jnp.int32, shape, 1)


def stack_heads(x):
    return jnp.concatenate([x[:, :128], x[:, 128:]], axis=0)


def side_heads(x):
    return jnp.concatenate([x[:64], x[64:]], axis=1)


def diagonal_heads(x):
    zero = jnp.zeros_like(x[:64])
    return jnp.concatenate(
        [jnp.concatenate([x[:64], zero], axis=1), jnp.concatenate([zero, x[64:]], axis=1)], axis=0
    )


def twice(x):
    return jnp.concatenate([x, x], axis=0)


def fold(x):
    return x[:64] + x[64:]


def half_swap(x):
    return jnp.concatenate([x[:, 64:], x[:, :64]], axis=1)


def by_block(x):
    lower = lax.broadcasted_iota(jnp.int32, (1, 128), 1) < 64
    rows = []
    for pair in range(2):
        first = x[0:1, 128 * pair : 128 * pair + 128]
        second = x[1:2, 128 * pair : 128 * pair + 128]
        rows.append(jnp.where(lower, first, half_swap(second)))
        rows.append(jnp.where(lower, half_swap(first), second))
    return jnp.concatenate(rows, axis=0)


def by_head(x):
    lower = lax.broadcasted_iota(jnp.int32, (1, 128), 1) < 64
    heads = ([], [])
    for pair in range(2):
        even, odd = x[2 * pair : 2 * pair + 1], x[2 * pair + 1 : 2 * pair + 2]
        heads[0].append(jnp.where(lower, even, half_swap(odd)))
        heads[1].append(jnp.where(lower, half_swap(even), odd))
    return jnp.concatenate([jnp.concatenate(row, axis=1) for row in heads], axis=0)


def turned(x):
    return jnp.transpose(jnp.concatenate([x, jnp.zeros((120, 128), F32)], axis=0))


def unit_scale(x):
    return lax.rsqrt(jnp.sum(x * x, axis=-1, keepdims=True) + EPS)


def unit_back(raw, grad, scale):
    inv = unit_scale(raw)
    unit = raw * inv
    return (scale * inv) * (grad - unit * jnp.sum(grad * unit, axis=-1, keepdims=True))


def running_decay(write_rate, log_decay):
    row, col = iotas()
    same = (row >> 6) == (col >> 6)
    upto = jnp.where(same & (row <= col), 1.0, 0.0).astype(F32)
    both = jnp.concatenate([by_block(log_decay), by_block(write_rate)], axis=0)
    summed = dot_exact(both, upto)
    rows = jnp.concatenate([summed[:4], both[4:]], axis=0)
    return rows[:4], turned(rows)


def block_columns(rows, columns, b):
    cum_row = rows[b : b + 1]
    cum = columns[:, b : b + 1]
    rate = columns[:, 4 + b : 5 + b]
    first = lax.broadcasted_iota(jnp.int32, (128, 1), 0) < 64
    last = jnp.where(first, cum_row[:, 63:64], cum_row[:, 127:128])
    return cum_row, cum, rate, jnp.exp(cum), jnp.exp(last - cum)


def last_growth(rows, b):
    lane = lax.broadcasted_iota(jnp.int32, (1, 256), 1)
    return jnp.exp(jnp.where(lane < 128, rows[b : b + 1, 63:64], rows[b : b + 1, 127:128]))


def block_tables(query, key, rows, columns, b):
    row, col = iotas()
    causal = ((row >> 6) == (col >> 6)) & (row >= col)
    cum_row, cum, rate, _, _ = block_columns(rows, columns, b)
    within = jnp.where(causal, jnp.exp(jnp.where(causal, cum - cum_row, 0.0)), 0.0)
    key2 = twice(key)
    strict = jnp.where(row > col, within, 0.0) * rate
    system = strict * dot3(key2, key2, "nt")
    query_key = dot3(twice(query), key2, "nt") * within
    return within, system, query_key


def inverse(systems, between=None):
    row, col = iotas()
    found = None
    for level in range(6):
        here = ((row >> (level + 1)) == (col >> (level + 1))) & ((row >> level) != (col >> level))
        below = [jnp.where(here, system, 0.0) for system in systems]
        if found is None:
            eye = jnp.where(row == col, 1.0, 0.0).astype(F32)
            found = [eye - one for one in below]
        else:
            half = [dot3(one, two) for one, two in zip(found, below)]
            found = [one - dot3(two, one) for one, two in zip(found, half)]
            if between is not None:
                between(level)
    return found


def gated(out, gate):
    inv = lax.rsqrt(jnp.mean(out * out, axis=-1, keepdims=True) + EPS)
    return out * inv * (gate / (1.0 + jnp.exp(-gate)))


def gated_back(out, gate, grad):
    inv = lax.rsqrt(jnp.mean(out * out, axis=-1, keepdims=True) + EPS)
    sig = 1.0 / (1.0 + jnp.exp(-gate))
    weighted = grad * (gate * sig)
    grad_gate = grad * out * inv * (sig * (1.0 + gate * (1.0 - sig)))
    along = jnp.mean(weighted * out, axis=-1, keepdims=True)
    return inv * (weighted - out * (inv * inv * along)), grad_gate


def block_grads(
    query, key, value, cols, growth_last, tables, step, update, grad_out, grad_state, state_in
):
    _, _, rate, growth, remain = cols
    within, system, query_key = tables
    row, col = iotas()
    key2, query2 = twice(key), twice(query)
    grad_scores = dot3(grad_out, update, "nt")
    grad_system = -dot(step, update, "nt")
    masked = grad_scores * within
    strict = jnp.where(row > col, grad_system * within, 0.0) * rate
    pulled = grad_system * system
    spread = grad_scores * query_key + pulled
    grad_query = fold(dot(masked, key2))
    state_key = dot(diagonal_heads(update), grad_state, "nt")
    grad_key = fold(
        dot(masked, query2, "tn") + dot(strict, key2) + dot(strict, key2, "tn") + remain * state_key
    )
    tail = remain * jnp.sum(key2 * state_key, axis=-1, keepdims=True)
    grad_cum = jnp.sum(spread, axis=-1, keepdims=True) - tail
    grad_row = -jnp.sum(spread, axis=0, keepdims=True)
    end0 = jnp.sum(tail[:64], axis=0, keepdims=True)
    end1 = jnp.sum(tail[64:], axis=0, keepdims=True)
    grad_value = rate * step
    if state_in is None:
        inner = value
    else:
        state, key_state, query_state = state_in
        inner = value - growth * key_state
        out_growth = growth * grad_out
        in_growth = growth * grad_value
        grad_cum += jnp.sum(out_growth * query_state - in_growth * key_state, axis=-1, keepdims=True)
        grad_query += dot3(side_heads(out_growth), state, "nt")
        grad_key -= dot(side_heads(in_growth), state, "nt")
        kept = jnp.sum(growth_last * (state * grad_state), axis=0, keepdims=True)
        end0 += jnp.sum(kept[:, :128], axis=1, keepdims=True)
        end1 += jnp.sum(kept[:, 128:], axis=1, keepdims=True)
    lane = lax.broadcasted_iota(jnp.int32, (1, 128), 1)
    grad_row += jnp.where(lane == 63, end0, 0.0) + jnp.where(lane == 127, end1, 0.0)
    grad_rate = jnp.sum(step * inner, axis=-1, keepdims=True) + (
        jnp.sum(pulled, axis=-1, keepdims=True) / rate
    )
    return grad_query, grad_key, grad_value, grad_rate, grad_cum, grad_row


def decay_grads(grad_cums, grad_rates, grad_rows):
    row, col = iotas()
    packed = jnp.zeros((128, 128), F32)
    for b in range(4):
        packed = jnp.where(col == b, grad_cums[b], packed)
        packed = jnp.where(col == 4 + b, grad_rates[b], packed)
    packed = jnp.transpose(packed)[:8]
    since = jnp.where(((row >> 6) == (col >> 6)) & (row >= col), 1.0, 0.0).astype(F32)
    grad_cum = packed[:4] + jnp.concatenate(grad_rows, axis=0)
    grad_cum = jnp.concatenate([grad_cum, jnp.zeros((4, 128), F32)], axis=0)
    return by_head(packed[4:]), by_head(dot_exact(grad_cum, since)[:4])


def rows_of(index, size):
    return pl.ds(pl.multiple_of(index * size, size), size)


def send(src, dst, send_sem, recv_sem, device):
    copy = pltpu.make_async_remote_copy(
        src_ref=src,
        dst_ref=dst,
        send_sem=send_sem,
        recv_sem=recv_sem,
        device_id=device,
        device_id_type=MESH,
    )
    copy.start()


def await_bytes(ref, sem):
    pltpu.make_async_copy(ref, ref, sem).wait()


def layer_kernel(
    query_hbm,
    key_hbm,
    value_hbm,
    gate_hbm,
    rate_hbm,
    decay_hbm,
    weight_hbm,
    cot_hbm,
    response_ref,
    owner_ref,
    layer_ref,
    grad_query_ref,
    grad_key_ref,
    grad_value_ref,
    grad_gate_ref,
    grad_rate_ref,
    grad_decay_ref,
    grad_weight_ref,
    query_ref,
    key_ref,
    value_ref,
    gate_ref,
    rate_ref,
    decay_ref,
    weight_ref,
    cot_ref,
    cots,
    piece_src,
    pieces,
    chosen_src,
    chosen,
    starts,
    grad_src,
    grad_pieces,
    owned_src,
    owned,
    sums_src,
    sums,
    weight_src,
    weight_pair,
    weight_sum,
    weight_in,
    within_s,
    system_s,
    scores_s,
    inverse_s,
    outs_s,
    update_s,
    step_s,
    grad_out_s,
    state_s,
    grad_state_s,
    key_state_s,
    query_state_s,
    normed_s,
    share_s,
    pick_s,
    gather_s,
    load_sem,
    ring_send,
    ring_recv,
    sum_send,
    sum_recv,
    seq_send,
    seq_recv,
):
    me = lax.axis_index("seq")
    head = lax.axis_index("head")
    chip, core = me // 2, me % 2
    right, left = (head + 1) % N_HEAD, (head + N_HEAD - 1) % N_HEAD

    loads = [
        pltpu.make_async_copy(src, dst, load_sem.at[index])
        for index, (src, dst) in enumerate(
            (
                (rate_hbm, rate_ref),
                (decay_hbm, decay_ref),
                (key_hbm, key_ref),
                (query_hbm, query_ref),
                (value_hbm, value_ref),
                (gate_hbm, gate_ref),
                (cot_hbm, cot_ref),
                (weight_hbm, weight_ref),
            )
        )
    ]
    for load in loads:
        load.start()

    barrier = pltpu.get_barrier_semaphore()

    def greet(offset, carry):
        pl.semaphore_signal(
            barrier, inc=1, device_id={"seq": (me + offset) % N_SEQ}, device_id_type=MESH
        )
        return carry

    lax.fori_loop(1, N_SEQ, greet, 0)
    for neighbour in (left, right):
        pl.semaphore_signal(barrier, inc=1, device_id={"head": neighbour}, device_id_type=MESH)

    def ring_order(hop, to_right):
        order = (0, 1, 2, 3) if to_right else (2, 3, 0, 1)
        return order[:2] if hop == 4 else order

    def ring_chunk(hop, to_right, chunk):
        slot = hop - 1 if to_right or hop == 4 else 3 + hop
        return cots.at[slot, pl.ds(64 * chunk, 64)]

    def ring_index(hop, to_right, chunk):
        return 8 * (hop - 1) + (0 if to_right else 4) + chunk

    def ring_start(hop, to_right, chunk):
        if hop == 1:
            src = cot_hbm.at[pl.ds(64 * chunk, 64)]
        else:
            src = ring_chunk(hop - 1, to_right, chunk)
        send(
            src,
            ring_chunk(hop, to_right, chunk),
            ring_send.at[0],
            ring_recv.at[ring_index(hop, to_right, chunk)],
            {"head": right if to_right else left},
        )

    ring_steps = [(hop, place) for hop in (1, 2, 3, 4) for place in range(2 if hop == 4 else 4)]

    def ring_pump(count):
        for _ in range(count):
            hop, place = ring_steps.pop(0)
            for to_right in (True, False):
                chunk = ring_order(hop, to_right)[place]
                await_bytes(
                    ring_chunk(hop, to_right, chunk), ring_recv.at[ring_index(hop, to_right, chunk)]
                )
                if hop < 4 and chunk in ring_order(hop + 1, to_right):
                    ring_start(hop + 1, to_right, chunk)

    for load in loads[:5]:
        load.wait()
    rate2, decay2 = rate_ref[...], decay_ref[...]
    rows, columns = running_decay(rate2, decay2)

    def unit_block(ref, b):
        raw = ref[SPAN * b : SPAN * b + SPAN, :].astype(F32)
        return raw * unit_scale(raw)

    def block_of(ref, b):
        return stack_heads(ref[SPAN * b : SPAN * b + SPAN, :]).astype(F32)

    queries = [unit_block(query_ref, b) * SCALE for b in range(4)]
    keys = [unit_block(key_ref, b) for b in range(4)]
    cols = [block_columns(rows, columns, b) for b in range(4)]

    def tables_of(b):
        within, system, query_key = block_tables(queries[b], keys[b], rows, columns, b)
        within_s[b] = within
        system_s[b] = system
        scores_s[b] = query_key
        return system

    def tail_of(b):
        return twice(keys[b]) * cols[b][4]

    first_system = tables_of(0)
    pl.semaphore_wait(barrier, N_SEQ + 1)
    for place in range(4):
        for to_right in (True, False):
            ring_start(1, to_right, ring_order(1, to_right)[place])
    inverse_s[0] = inverse([first_system])[0].astype(BF16)
    update = dot(inverse_s[0], cols[0][2] * block_of(value_ref, 0))
    update_s[0] = update
    final = dot(tail_of(0), diagonal_heads(update), "tn")
    piece_src[0:128, :] = final[:, :128].astype(BF16)
    piece_src[128:256, :] = final[:, 128:].astype(BF16)

    def send_pieces(offset, carry):
        to = (me + offset) % N_SEQ
        send(
            piece_src.at[rows_of(to // 2, 16)],
            pieces.at[rows_of(offset - 1, 16)],
            seq_send.at[0],
            seq_recv.at[0],
            {"seq": to},
        )
        return carry

    lax.fori_loop(1, N_SEQ, send_pieces, 0)
    pieces[496:512, :] = piece_src[rows_of(chip, 16), :]

    def owner_of(device, slot):
        prompt = (response_ref[3 * device] >> 1) + slot
        found = owner_ref[jnp.minimum(prompt, N_SEQ - 1)]
        return jnp.where(prompt < N_SEQ, found, -1)

    row, _ = iotas((32, 1))
    _, col = iotas((1, 512))
    source = (me + 31 - (col >> 4)) % N_SEQ
    same_row = (row & 15) == (col & 15)
    for place in range(CHIPS):
        to = 2 * ((chip + place + 1) % CHIPS) + core
        wanted = jnp.where(row < 16, owner_of(to, 0), owner_of(to, 1))
        here = (source == wanted) & same_row
        pick_s[32 * place : 32 * place + 32, :] = jnp.where(here, 1.0, 0.0).astype(BF16)

    systems = []
    for b in (1, 2, 3):
        systems.append(tables_of(b))
        ring_pump(2 if b == 3 else 1)

    await_bytes(pieces.at[pl.ds(0, 496)], seq_recv.at[0])

    chosen_src[...] = dot(pick_s[...], pieces[...]).astype(BF16)

    def send_chosen(offset, carry):
        send(
            chosen_src.at[rows_of(offset - 1, 32)],
            chosen.at[rows_of(offset - 1, 32)],
            seq_send.at[1],
            seq_recv.at[1],
            {"seq": 2 * ((chip + offset) % CHIPS) + core},
        )
        return carry

    lax.fori_loop(1, CHIPS, send_chosen, 0)
    chosen[480:512, :] = chosen_src[480:512, :]

    def between(level):
        if level < 5:
            ring_pump(1)

    for b, found in zip((1, 2, 3), inverse(systems, between)):
        inverse_s[b] = found.astype(BF16)
    loads[5].wait()

    def norm_block(b, out):
        outs_s[b] = out
        result = side_heads(gated(out, block_of(gate_ref, b))).astype(BF16)
        normed_s[SPAN * b : SPAN * b + SPAN, :] = result

    norm_block(0, dot3(scores_s[0], update_s[0]))
    ring_pump(2)

    await_bytes(chosen.at[pl.ds(0, 480)], seq_recv.at[1])
    for slot in range(2):
        for piece in range(CHIPS):
            place = (chip - piece + 15) % CHIPS
            starts[slot, 16 * (piece % 8) : 16 * (piece % 8) + 16, 128 * (piece // 8) : 128 * (piece // 8) + 128] = (
                chosen[pl.ds(pl.multiple_of(place * 32 + 16 * slot, 16), 16), :].astype(F32)
            )
    own = [response_ref[3 * me + j] for j in range(3)]
    fresh, later = [None, None], [None, None]
    for j in (1, 2):
        fresh.append(jnp.where(own[j] != own[j - 1], 1.0, 0.0).astype(F32))
        later.append(jnp.where((own[j] >> 1) != (own[0] >> 1), 1.0, 0.0).astype(F32))

    state = None
    for b in (1, 2, 3):
        if b == 1:
            state = starts[0]
        else:
            begun = (1.0 - later[b]) * starts[0] + later[b] * starts[1]
            state = fresh[b] * begun + (1.0 - fresh[b]) * state
        state_s[b - 1] = state
        _, _, rate, growth, _ = cols[b]
        both = dot3(jnp.concatenate([keys[b], queries[b]], axis=0), state)
        key_state, query_state = stack_heads(both[:64]), stack_heads(both[64:])
        key_state_s[b - 1] = key_state
        query_state_s[b - 1] = query_state
        update = dot(inverse_s[b], rate * (block_of(value_ref, b) - growth * key_state))
        update_s[b] = update
        if b < 3:
            state = last_growth(rows, b) * state + dot(tail_of(b), diagonal_heads(update), "tn")
        norm_block(b, growth * query_state + dot3(scores_s[b], update))
        if b < 3:
            ring_pump(1)

    def share(distance):
        block = (head + distance + N_HEAD) % N_HEAD
        return dot(normed_s[...], weight_ref[rows_of(block, 256), :], "nt")

    def sums_order(hop, to_right):
        if hop == 1:
            return (0, 1) if to_right else (2, 3)
        return (2, 3, 0, 1) if to_right else (0, 1, 2, 3)

    def sums_slot(hop, to_right):
        return 2 * (hop - 1) + (0 if to_right else 1)

    def sums_start(hop, to_right, chunk):
        here = (sums_slot(hop, to_right), pl.ds(64 * chunk, 64))
        send(
            sums_src.at[here],
            sums.at[here],
            sum_send.at[0],
            sum_recv.at[ring_index(hop, to_right, chunk)],
            {"head": right if to_right else left},
        )

    def sums_prepare(hop):
        for to_right in (True, False):
            share_s[sums_slot(hop, to_right)] = share(5 - hop if to_right else hop - 5)

    def sums_begin():
        across = share(4)
        for to_right in (True, False):
            low = 0 if to_right else 128
            sums_src[sums_slot(1, to_right), low : low + 128, :] = across[low : low + 128].astype(BF16)
        for place in range(2):
            for to_right in (True, False):
                sums_start(1, to_right, sums_order(1, to_right)[place])
        sums_prepare(2)
        for to_right in (True, False):
            slot, low = sums_slot(2, to_right), 128 if to_right else 0
            sums_src[slot, low : low + 128, :] = share_s[slot, low : low + 128, :].astype(BF16)
        for place in range(2):
            for to_right in (True, False):
                sums_start(2, to_right, sums_order(2, to_right)[place])

    sums_steps = [(hop, place) for hop in (1, 2, 3, 4) for place in range(2 if hop == 1 else 4)]

    def sums_pump(count):
        for _ in range(count):
            hop, place = sums_steps.pop(0)
            for to_right in (True, False):
                chunk = sums_order(hop, to_right)[place]
                here = pl.ds(64 * chunk, 64)
                arrived = sums.at[sums_slot(hop, to_right), here]
                await_bytes(arrived, sum_recv.at[ring_index(hop, to_right, chunk)])
                if hop < 4:
                    slot = sums_slot(hop + 1, to_right)
                    sums_src[slot, here, :] = (
                        share_s[slot, here, :] + arrived[...].astype(F32)
                    ).astype(BF16)
                    sums_start(hop + 1, to_right, chunk)

    loads[7].wait()
    sums_begin()

    loads[6].wait()

    def cot_slots():
        yield cot_ref, head
        for hop in (1, 2, 3):
            yield cots.at[hop - 1], (head - hop + N_HEAD) % N_HEAD
            yield cots.at[3 + hop], (head + hop) % N_HEAD
        yield cots.at[3], (head + 4) % N_HEAD

    grad_normed = None
    for index, (slot_ref, block) in enumerate(cot_slots()):
        if index == 7:
            ring_pump(2)
        term = dot(slot_ref[...], weight_ref[rows_of(block, 256), :])
        grad_normed = term if grad_normed is None else grad_normed + term
    for b in range(4):
        grad_out, grad_gate = gated_back(
            outs_s[b], block_of(gate_ref, b), stack_heads(grad_normed[SPAN * b : SPAN * b + SPAN])
        )
        grad_out_s[b] = grad_out
        grad_gate_ref[SPAN * b : SPAN * b + SPAN, :] = side_heads(grad_gate)

    grad_state = jnp.zeros((128, 256), F32)
    begun = [jnp.zeros((128, 256), F32), jnp.zeros((128, 256), F32)]
    for b in (3, 2, 1):
        _, _, rate, growth, remain = cols[b]
        grad_out = grad_out_s[b]
        grad_state_s[b] = grad_state
        grad_update = dot(scores_s[b], grad_out, "tn")
        if b < 3:
            grad_update += remain * stack_heads(dot(keys[b], grad_state))
        step = dot(inverse_s[b], grad_update, "tn")
        step_s[b] = step
        sides = jnp.concatenate(
            [side_heads(-(rate * growth) * step), side_heads(growth * grad_out)], axis=0
        )
        grad_in = dot(jnp.concatenate([keys[b], queries[b]], axis=0), sides, "tn")
        if b < 3:
            grad_in += last_growth(rows, b) * grad_state
        if b > 1:
            begun[0] += (fresh[b] * (1.0 - later[b])) * grad_in
            begun[1] += (fresh[b] * later[b]) * grad_in
            grad_state = (1.0 - fresh[b]) * grad_in
            if b == 2:
                sums_pump(1)
        else:
            begun[0] += grad_in
    for slot in range(2):
        for piece in range(CHIPS):
            grad_src[32 * piece + 16 * slot : 32 * piece + 16 * slot + 16, :] = begun[slot][
                16 * (piece % 8) : 16 * (piece % 8) + 16,
                128 * (piece // 8) : 128 * (piece // 8) + 128,
            ].astype(BF16)

    def send_grads(offset, carry):
        to = (me + offset) % N_SEQ
        send(
            grad_src.at[rows_of(to // 2, 32)],
            grad_pieces.at[rows_of(offset - 1, 32)],
            seq_send.at[2],
            seq_recv.at[2],
            {"seq": to},
        )
        return carry

    lax.fori_loop(1, N_SEQ, send_grads, 0)
    grad_pieces[992:1024, :] = grad_src[rows_of(chip, 32), :]

    sums_prepare(3)
    sums_pump(1)

    for index, (slot_ref, block) in enumerate(cot_slots()):
        share_w = dot(slot_ref[...], normed_s[...], "tn").astype(BF16)
        for quarter in range(4):
            place = (quarter % 2) * 1024 + (2 * block + quarter // 2) * 64
            weight_src[pl.ds(pl.multiple_of(place, 64), 64), :] = share_w[
                64 * quarter : 64 * quarter + 64
            ]
        if index % 2 == 1:
            sums_pump(1)
    send(
        weight_src.at[rows_of(1 - core, 1024)],
        weight_pair,
        seq_send.at[4],
        seq_recv.at[4],
        {"seq": 2 * chip + 1 - core},
    )

    sums_prepare(4)
    _, col = iotas((1, 128))
    row, _ = iotas((256, 1))
    target = 2 * ((chip + 1 + (row >> 4)) % CHIPS) + core
    for part in range(8):
        owner = jnp.full((1, 128), -1, jnp.int32)
        for index in range(4):
            device = (me + 31 - (4 * part + index)) % N_SEQ
            for slot in range(2):
                owner = jnp.where((col >> 4) == 2 * index + slot, owner_of(device, slot), owner)
        here = (owner == target) & ((row & 15) == (col & 15))
        gather_s[:, 128 * part : 128 * part + 128] = jnp.where(here, 1.0, 0.0).astype(BF16)
    sums_pump(1)

    await_bytes(grad_pieces.at[pl.ds(0, 992)], seq_recv.at[2])

    owned_src[...] = dot(gather_s[...], grad_pieces[...]).astype(BF16)

    def send_owned(offset, carry):
        send(
            owned_src.at[rows_of(offset - 1, 16)],
            owned.at[rows_of(offset - 1, 16)],
            seq_send.at[3],
            seq_recv.at[3],
            {"seq": 2 * ((chip + offset) % CHIPS) + core},
        )
        return carry

    lax.fori_loop(1, CHIPS, send_owned, 0)
    sums_pump(1)
    owned[240:256, :] = owned_src[240:256, :]

    await_bytes(weight_pair, seq_recv.at[4])
    for part in range(4):
        place = core * 1024 + 256 * part
        weight_sum[256 * part : 256 * part + 256, :] = (
            weight_src[pl.ds(pl.multiple_of(place, 256), 256), :].astype(F32)
            + weight_pair[256 * part : 256 * part + 256, :].astype(F32)
        ).astype(BF16)

    def send_weight(offset, carry):
        to = (chip + offset) % CHIPS
        send(
            weight_sum.at[rows_of(to, 64)],
            weight_in.at[rows_of(offset - 1, 64)],
            seq_send.at[5],
            seq_recv.at[5],
            {"seq": 2 * to + core},
        )
        return carry

    lax.fori_loop(1, CHIPS, send_weight, 0)

    grad_cums, grad_rates, grad_rows = [None] * 4, [None] * 4, [None] * 4

    def finish_block(b, grad_state, state_in):
        tables = (within_s[b], system_s[b], scores_s[b])
        found = block_grads(
            queries[b],
            keys[b],
            block_of(value_ref, b),
            cols[b],
            last_growth(rows, b),
            tables,
            step_s[b],
            update_s[b],
            grad_out_s[b],
            grad_state,
            state_in,
        )
        for raw_ref, out_ref, grad, scale in (
            (query_ref, grad_query_ref, found[0], SCALE),
            (key_ref, grad_key_ref, found[1], 1.0),
        ):
            raw = raw_ref[SPAN * b : SPAN * b + SPAN, :].astype(F32)
            out_ref[SPAN * b : SPAN * b + SPAN, :] = unit_back(raw, grad, scale)
        grad_value_ref[SPAN * b : SPAN * b + SPAN, :] = side_heads(found[2])
        grad_rates[b], grad_cums[b], grad_rows[b] = found[3:]

    for b in (1, 2, 3):
        finish_block(b, grad_state_s[b], (state_s[b - 1], key_state_s[b - 1], query_state_s[b - 1]))
        if b < 3:
            sums_pump(1)

    share_s[0] = share(0)
    await_bytes(owned.at[pl.ds(0, 240)], seq_recv.at[3])
    for piece in range(CHIPS):
        place = (chip - piece + 15) % CHIPS
        grad_state_s[0, 16 * (piece % 8) : 16 * (piece % 8) + 16, 128 * (piece // 8) : 128 * (piece // 8) + 128] = (
            owned[rows_of(place, 16), :].astype(F32)
        )
    grad_state = grad_state_s[0]
    grad_update = dot(scores_s[0], grad_out_s[0], "tn")
    grad_update += cols[0][4] * stack_heads(dot(keys[0], grad_state))
    step_s[0] = dot(inverse_s[0], grad_update, "tn")
    finish_block(0, grad_state, None)
    grad_rate_ref[...], grad_decay_ref[...] = decay_grads(grad_cums, grad_rates, grad_rows)

    await_bytes(weight_in.at[pl.ds(0, 15 * 64)], seq_recv.at[5])
    total = weight_sum[rows_of(chip, 64), :].astype(F32)
    for slot in range(15):
        total += weight_in[64 * slot : 64 * slot + 64, :].astype(F32)
    grad_weight_ref[...] = total
    sums_pump(4)
    layer_ref[...] = (share_s[0] + sums[6].astype(F32) + sums[7].astype(F32)).astype(BF16)

    await_bytes(cots, ring_send.at[0])
    await_bytes(sums.at[pl.ds(0, 7)], sum_send.at[0])
    await_bytes(pieces.at[pl.ds(0, 496)], seq_send.at[0])
    await_bytes(chosen.at[pl.ds(0, 480)], seq_send.at[1])
    await_bytes(grad_pieces.at[pl.ds(0, 992)], seq_send.at[2])
    await_bytes(owned.at[pl.ds(0, 240)], seq_send.at[3])
    await_bytes(weight_pair, seq_send.at[4])
    await_bytes(weight_in.at[pl.ds(0, 15 * 64)], seq_send.at[5])


SCRATCH = [
    pltpu.VMEM((256, 128), BF16),
    pltpu.VMEM((256, 128), BF16),
    pltpu.VMEM((256, 256), BF16),
    pltpu.VMEM((256, 256), BF16),
    pltpu.VMEM((2, 256), F32),
    pltpu.VMEM((2, 256), F32),
    pltpu.VMEM((2048, 256), BF16),
    pltpu.VMEM((256, 256), BF16),
    pltpu.VMEM((7, 256, 256), BF16),
    pltpu.VMEM((256, 128), BF16),
    pltpu.VMEM((512, 128), BF16),
    pltpu.VMEM((512, 128), BF16),
    pltpu.VMEM((512, 128), BF16),
    pltpu.VMEM((2, 128, 256), F32),
    pltpu.VMEM((512, 128), BF16),
    pltpu.VMEM((1024, 128), BF16),
    pltpu.VMEM((256, 128), BF16),
    pltpu.VMEM((256, 128), BF16),
    pltpu.VMEM((8, 256, 256), BF16),
    pltpu.VMEM((8, 256, 256), BF16),
    pltpu.VMEM((2048, 256), BF16),
    pltpu.VMEM((1024, 256), BF16),
    pltpu.VMEM((1024, 256), BF16),
    pltpu.VMEM((960, 256), BF16),
    pltpu.VMEM((4, 128, 128), F32),
    pltpu.VMEM((4, 128, 128), F32),
    pltpu.VMEM((4, 128, 128), F32),
    pltpu.VMEM((4, 128, 128), BF16),
    pltpu.VMEM((4, 128, 128), F32),
    pltpu.VMEM((4, 128, 128), F32),
    pltpu.VMEM((4, 128, 128), F32),
    pltpu.VMEM((4, 128, 128), F32),
    pltpu.VMEM((3, 128, 256), F32),
    pltpu.VMEM((4, 128, 256), F32),
    pltpu.VMEM((3, 128, 128), F32),
    pltpu.VMEM((3, 128, 128), F32),
    pltpu.VMEM((256, 256), BF16),
    pltpu.VMEM((8, 256, 256), F32),
    pltpu.VMEM((512, 512), BF16),
    pltpu.VMEM((256, 1024), BF16),
    pltpu.SemaphoreType.DMA((8,)),
    pltpu.SemaphoreType.DMA((1,)),
    pltpu.SemaphoreType.DMA((32,)),
    pltpu.SemaphoreType.DMA((1,)),
    pltpu.SemaphoreType.DMA((32,)),
    pltpu.SemaphoreType.DMA((6,)),
    pltpu.SemaphoreType.DMA((6,)),
]


def finish_kernel(*refs):
    for index in range(8):
        refs[8 + index][...] = refs[index][...]


RESULTS = [
    jax.ShapeDtypeStruct((256, 256), BF16),
    jax.ShapeDtypeStruct((256, 128), F32),
    jax.ShapeDtypeStruct((256, 128), F32),
    jax.ShapeDtypeStruct((256, 256), F32),
    jax.ShapeDtypeStruct((256, 256), F32),
    jax.ShapeDtypeStruct((2, 256), F32),
    jax.ShapeDtypeStruct((2, 256), F32),
    jax.ShapeDtypeStruct((64, 256), F32),
]


def per_device(
    query_rows, key_rows, value_rows, output_gate, write_rate, log_decay,
    out_weight, out_cotangent, block_response, prefix_owner,
):
    vmem = pl.BlockSpec(memory_space=pltpu.VMEM)
    smem = pl.BlockSpec(memory_space=pltpu.SMEM)
    whole = pl.BlockSpec(memory_space=pl.ANY)
    results = pl.pallas_call(
        layer_kernel,
        out_shape=RESULTS,
        in_specs=[whole] * 8 + [smem] * 2,
        out_specs=[vmem] * 8,
        scratch_shapes=SCRATCH,
        compiler_params=pltpu.CompilerParams(
            collective_id=0, has_side_effects=True, vmem_limit_bytes=56 * 1024 * 1024
        ),
    )(
        query_rows, key_rows, value_rows, output_gate, write_rate, log_decay,
        out_weight, out_cotangent, block_response, prefix_owner,
    )
    return pl.pallas_call(
        finish_kernel,
        out_shape=RESULTS,
        in_specs=[vmem] * 8,
        out_specs=[vmem] * 8,
    )(*results)


def solution(mesh):
    rows = P("seq", "head")
    return jax.shard_map(
        per_device,
        mesh=mesh,
        in_specs=(rows, rows, rows, rows, P("head", "seq"), P("head", "seq"), P(None, "head"), rows, P(), P()),
        out_specs=(rows, rows, rows, rows, rows, P("head", "seq"), P("head", "seq"), rows),
        check_vma=False,
    )
```

```python
import functools

import jax
import jax.numpy as jnp
from jax import lax
from jax.experimental import pallas as pl
from jax.experimental.pallas import tpu as pltpu
from jax.sharding import PartitionSpec as P

N_SEQ = 32
N_HEAD = 8
CHIPS = 16
SPAN = 64
EPS = 1e-06
F32 = jnp.float32
BF16 = jnp.bfloat16
HIGHEST = lax.Precision.HIGHEST
MESH = pl.DeviceIdType.MESH
SCALE = 128 ** (-0.5)

KINDS = {"nn": ((1,), (0,)), "nt": ((1,), (1,)), "tn": ((0,), (0,))}


def dot(a, b, kind="nn"):
    return lax.dot_general(
        a.astype(BF16), b.astype(BF16), (KINDS[kind], ((), ())), preferred_element_type=F32
    )


def parts(x):
    high = x.astype(BF16)
    return high, (x - high.astype(F32)).astype(BF16)


def dot3(a, b, kind="nn"):
    a_high, a_low = parts(a)
    b_high, b_low = parts(b)
    return dot(a_high, b_high, kind) + (dot(a_high, b_low, kind) + dot(a_low, b_high, kind))


def dot_exact(a, b):
    return lax.dot_general(
        a, b, (KINDS["nn"], ((), ())), precision=HIGHEST, preferred_element_type=F32
    )


def iotas(shape=(128, 128)):
    return lax.broadcasted_iota(jnp.int32, shape, 0), lax.broadcasted_iota(jnp.int32, shape, 1)


def stack_heads(x):
    return jnp.concatenate([x[:, :128], x[:, 128:]], axis=0)


def side_heads(x):
    return jnp.concatenate([x[:64], x[64:]], axis=1)


def diagonal_heads(x):
    zero = jnp.zeros_like(x[:64])
    return jnp.concatenate(
        [jnp.concatenate([x[:64], zero], axis=1), jnp.concatenate([zero, x[64:]], axis=1)], axis=0
    )


def twice(x):
    return jnp.concatenate([x, x], axis=0)


def fold(x):
    return x[:64] + x[64:]


def half_swap(x):
    return jnp.concatenate([x[:, 64:], x[:, :64]], axis=1)


def by_block(x):
    lower = lax.broadcasted_iota(jnp.int32, (1, 128), 1) < 64
    rows = []
    for pair in range(2):
        first = x[0:1, 128 * pair : 128 * pair + 128]
        second = x[1:2, 128 * pair : 128 * pair + 128]
        rows.append(jnp.where(lower, first, half_swap(second)))
        rows.append(jnp.where(lower, half_swap(first), second))
    return jnp.concatenate(rows, axis=0)


def by_head(x):
    lower = lax.broadcasted_iota(jnp.int32, (1, 128), 1) < 64
    heads = ([], [])
    for pair in range(2):
        even, odd = x[2 * pair : 2 * pair + 1], x[2 * pair + 1 : 2 * pair + 2]
        heads[0].append(jnp.where(lower, even, half_swap(odd)))
        heads[1].append(jnp.where(lower, half_swap(even), odd))
    return jnp.concatenate([jnp.concatenate(row, axis=1) for row in heads], axis=0)


def turned(x):
    return jnp.transpose(jnp.concatenate([x, jnp.zeros((120, 128), F32)], axis=0))


def unit_scale(x):
    return lax.rsqrt(jnp.sum(x * x, axis=-1, keepdims=True) + EPS)


def unit_back(raw, grad, scale):
    inv = unit_scale(raw)
    unit = raw * inv
    return (scale * inv) * (grad - unit * jnp.sum(grad * unit, axis=-1, keepdims=True))


def running_decay(write_rate, log_decay):
    row, col = iotas()
    same = (row >> 6) == (col >> 6)
    upto = jnp.where(same & (row <= col), 1.0, 0.0).astype(F32)
    both = jnp.concatenate([by_block(log_decay), by_block(write_rate)], axis=0)
    summed = dot_exact(both, upto)
    rows = jnp.concatenate([summed[:4], both[4:]], axis=0)
    return rows[:4], turned(rows)


def block_columns(rows, columns, b):
    cum_row = rows[b : b + 1]
    cum = columns[:, b : b + 1]
    rate = columns[:, 4 + b : 5 + b]
    first = lax.broadcasted_iota(jnp.int32, (128, 1), 0) < 64
    last = jnp.where(first, cum_row[:, 63:64], cum_row[:, 127:128])
    return cum_row, cum, rate, jnp.exp(cum), jnp.exp(last - cum)


def last_growth(rows, b):
    lane = lax.broadcasted_iota(jnp.int32, (1, 256), 1)
    return jnp.exp(jnp.where(lane < 128, rows[b : b + 1, 63:64], rows[b : b + 1, 127:128]))


def block_tables(query, key, rows, columns, b):
    row, col = iotas()
    causal = ((row >> 6) == (col >> 6)) & (row >= col)
    cum_row, cum, rate, _, _ = block_columns(rows, columns, b)
    within = jnp.where(causal, jnp.exp(jnp.where(causal, cum - cum_row, 0.0)), 0.0)
    key2 = twice(key)
    strict = jnp.where(row > col, within, 0.0) * rate
    system = strict * dot3(key2, key2, "nt")
    query_key = dot3(twice(query), key2, "nt") * within
    return within, system, query_key


def inverse(systems, between=None):
    row, col = iotas()
    found = None
    for level in range(6):
        here = ((row >> (level + 1)) == (col >> (level + 1))) & ((row >> level) != (col >> level))
        below = [jnp.where(here, system, 0.0) for system in systems]
        if found is None:
            eye = jnp.where(row == col, 1.0, 0.0).astype(F32)
            found = [eye - one for one in below]
        else:
            half = [dot3(one, two) for one, two in zip(found, below)]
            found = [one - dot3(two, one) for one, two in zip(found, half)]
            if between is not None:
                between(level)
    return found


def gated(out, gate):
    inv = lax.rsqrt(jnp.mean(out * out, axis=-1, keepdims=True) + EPS)
    return out * inv * (gate / (1.0 + jnp.exp(-gate)))


def gated_back(out, gate, grad):
    inv = lax.rsqrt(jnp.mean(out * out, axis=-1, keepdims=True) + EPS)
    sig = 1.0 / (1.0 + jnp.exp(-gate))
    weighted = grad * (gate * sig)
    grad_gate = grad * out * inv * (sig * (1.0 + gate * (1.0 - sig)))
    along = jnp.mean(weighted * out, axis=-1, keepdims=True)
    return inv * (weighted - out * (inv * inv * along)), grad_gate


def block_grads(
    query, key, value, cols, growth_last, tables, step, update, grad_out, grad_state, state_in
):
    _, _, rate, growth, remain = cols
    within, system, query_key = tables
    row, col = iotas()
    key2, query2 = twice(key), twice(query)
    grad_scores = dot3(grad_out, update, "nt")
    grad_system = -dot(step, update, "nt")
    masked = grad_scores * within
    strict = jnp.where(row > col, grad_system * within, 0.0) * rate
    pulled = grad_system * system
    spread = grad_scores * query_key + pulled
    grad_query = fold(dot(masked, key2))
    state_key = dot(diagonal_heads(update), grad_state, "nt")
    grad_key = fold(
        dot(masked, query2, "tn") + dot(strict, key2) + dot(strict, key2, "tn") + remain * state_key
    )
    tail = remain * jnp.sum(key2 * state_key, axis=-1, keepdims=True)
    grad_cum = jnp.sum(spread, axis=-1, keepdims=True) - tail
    grad_row = -jnp.sum(spread, axis=0, keepdims=True)
    end0 = jnp.sum(tail[:64], axis=0, keepdims=True)
    end1 = jnp.sum(tail[64:], axis=0, keepdims=True)
    grad_value = rate * step
    if state_in is None:
        inner = value
    else:
        state, key_state, query_state = state_in
        inner = value - growth * key_state
        out_growth = growth * grad_out
        in_growth = growth * grad_value
        grad_cum += jnp.sum(out_growth * query_state - in_growth * key_state, axis=-1, keepdims=True)
        grad_query += dot3(side_heads(out_growth), state, "nt")
        grad_key -= dot(side_heads(in_growth), state, "nt")
        kept = jnp.sum(growth_last * (state * grad_state), axis=0, keepdims=True)
        end0 += jnp.sum(kept[:, :128], axis=1, keepdims=True)
        end1 += jnp.sum(kept[:, 128:], axis=1, keepdims=True)
    lane = lax.broadcasted_iota(jnp.int32, (1, 128), 1)
    grad_row += jnp.where(lane == 63, end0, 0.0) + jnp.where(lane == 127, end1, 0.0)
    grad_rate = jnp.sum(step * inner, axis=-1, keepdims=True) + (
        jnp.sum(pulled, axis=-1, keepdims=True) / rate
    )
    return grad_query, grad_key, grad_value, grad_rate, grad_cum, grad_row


def decay_grads(grad_cums, grad_rates, grad_rows):
    row, col = iotas()
    packed = jnp.zeros((128, 128), F32)
    for b in range(4):
        packed = jnp.where(col == b, grad_cums[b], packed)
        packed = jnp.where(col == 4 + b, grad_rates[b], packed)
    packed = jnp.transpose(packed)[:8]
    since = jnp.where(((row >> 6) == (col >> 6)) & (row >= col), 1.0, 0.0).astype(F32)
    grad_cum = packed[:4] + jnp.concatenate(grad_rows, axis=0)
    grad_cum = jnp.concatenate([grad_cum, jnp.zeros((4, 128), F32)], axis=0)
    return by_head(packed[4:]), by_head(dot_exact(grad_cum, since)[:4])


def rows_of(index, size):
    return pl.ds(pl.multiple_of(index * size, size), size)


def send(src, dst, send_sem, recv_sem, device):
    copy = pltpu.make_async_remote_copy(
        src_ref=src,
        dst_ref=dst,
        send_sem=send_sem,
        recv_sem=recv_sem,
        device_id=device,
        device_id_type=MESH,
    )
    copy.start()


def await_bytes(ref, sem):
    pltpu.make_async_copy(ref, ref, sem).wait()


def layer_kernel(
    query_hbm,
    key_hbm,
    value_hbm,
    gate_hbm,
    rate_hbm,
    decay_hbm,
    weight_hbm,
    cot_hbm,
    response_ref,
    owner_ref,
    layer_ref,
    grad_query_ref,
    grad_key_ref,
    grad_value_ref,
    grad_gate_ref,
    grad_rate_ref,
    grad_decay_ref,
    grad_weight_ref,
    query_ref,
    key_ref,
    value_ref,
    gate_ref,
    rate_ref,
    decay_ref,
    weight_ref,
    cot_ref,
    cots,
    piece_src,
    pieces,
    chosen_src,
    chosen,
    starts,
    grad_src,
    grad_pieces,
    owned_src,
    owned,
    sums_src,
    sums,
    weight_src,
    weight_pair,
    weight_sum,
    weight_in,
    within_s,
    system_s,
    scores_s,
    inverse_s,
    outs_s,
    update_s,
    step_s,
    grad_out_s,
    state_s,
    grad_state_s,
    key_state_s,
    query_state_s,
    normed_s,
    share_s,
    turned_s,
    pick_s,
    gather_s,
    load_sem,
    ring_send,
    ring_recv,
    sum_send,
    sum_recv,
    seq_send,
    seq_recv,
):
    me = lax.axis_index("seq")
    head = lax.axis_index("head")
    chip, core = lax.div(me, 2), lax.rem(me, 2)
    right, left = lax.rem(head + 1, N_HEAD), lax.rem(head + N_HEAD - 1, N_HEAD)

    loads = [
        pltpu.make_async_copy(src, dst, load_sem.at[index])
        for index, (src, dst) in enumerate(
            (
                (rate_hbm, rate_ref),
                (decay_hbm, decay_ref),
                (key_hbm, key_ref),
                (query_hbm, query_ref),
                (value_hbm, value_ref),
                (gate_hbm, gate_ref),
                (cot_hbm, cot_ref),
                (weight_hbm, weight_ref),
            )
        )
    ]
    for load in loads:
        load.start()

    barrier = pltpu.get_barrier_semaphore()

    def greet(offset, carry):
        pl.semaphore_signal(
            barrier, inc=1, device_id={"seq": lax.rem(me + offset, N_SEQ)}, device_id_type=MESH
        )
        return carry

    lax.fori_loop(1, N_SEQ, greet, 0)
    for neighbour in (left, right):
        pl.semaphore_signal(barrier, inc=1, device_id={"head": neighbour}, device_id_type=MESH)

    def ring_order(hop, to_right):
        order = (0, 1, 2, 3) if to_right else (2, 3, 0, 1)
        return order[:2] if hop == 4 else order

    def ring_chunk(hop, to_right, chunk):
        slot = hop - 1 if to_right or hop == 4 else 3 + hop
        return cots.at[slot, pl.ds(64 * chunk, 64)]

    def ring_index(hop, to_right, chunk):
        return 8 * (hop - 1) + (0 if to_right else 4) + chunk

    def ring_start(hop, to_right, chunk):
        if hop == 1:
            src = cot_hbm.at[pl.ds(64 * chunk, 64)]
        else:
            src = ring_chunk(hop - 1, to_right, chunk)
        send(
            src,
            ring_chunk(hop, to_right, chunk),
            ring_send.at[0],
            ring_recv.at[ring_index(hop, to_right, chunk)],
            {"head": right if to_right else left},
        )

    ring_steps = [(hop, place) for hop in (1, 2, 3, 4) for place in range(2 if hop == 4 else 4)]

    def ring_pump(count):
        for _ in range(count):
            hop, place = ring_steps.pop(0)
            for to_right in (True, False):
                chunk = ring_order(hop, to_right)[place]
                await_bytes(
                    ring_chunk(hop, to_right, chunk), ring_recv.at[ring_index(hop, to_right, chunk)]
                )
                if hop < 4 and chunk in ring_order(hop + 1, to_right):
                    ring_start(hop + 1, to_right, chunk)

    def cot_slots():
        yield cot_ref, head
        for hop in (1, 2, 3):
            yield cots.at[hop - 1], (head - hop + N_HEAD) % N_HEAD
            yield cots.at[3 + hop], (head + hop) % N_HEAD
        yield cots.at[3], (head + 4) % N_HEAD

    def turn(index, slot_ref):
        turned_s[index] = jnp.transpose(slot_ref[...])

    for load in loads[:5]:
        load.wait()
    rate2, decay2 = rate_ref[...], decay_ref[...]
    rows, columns = running_decay(rate2, decay2)

    def unit_block(ref, b):
        raw = ref[SPAN * b : SPAN * b + SPAN, :].astype(F32)
        return raw * unit_scale(raw)

    def block_of(ref, b):
        return stack_heads(ref[SPAN * b : SPAN * b + SPAN, :]).astype(F32)

    queries = [unit_block(query_ref, b) * SCALE for b in range(4)]
    keys = [unit_block(key_ref, b) for b in range(4)]
    cols = [block_columns(rows, columns, b) for b in range(4)]

    def tables_of(b):
        within, system, query_key = block_tables(queries[b], keys[b], rows, columns, b)
        within_s[b] = within
        system_s[b] = system
        scores_s[b] = query_key
        return system

    def tail_of(b):
        return twice(keys[b]) * cols[b][4]

    first_system = tables_of(0)
    pl.semaphore_wait(barrier, N_SEQ + 1)
    for place in range(4):
        for to_right in (True, False):
            ring_start(1, to_right, ring_order(1, to_right)[place])
    inverse_s[0] = inverse([first_system])[0].astype(BF16)
    update = dot(inverse_s[0], cols[0][2] * block_of(value_ref, 0))
    update_s[0] = update
    final = dot(tail_of(0), diagonal_heads(update), "tn")
    piece_src[0:128, :] = final[:, :128].astype(BF16)
    piece_src[128:256, :] = final[:, 128:].astype(BF16)

    def send_pieces(offset, carry):
        to = lax.rem(me + offset, N_SEQ)
        send(
            piece_src.at[rows_of(lax.div(to, 2), 16)],
            pieces.at[rows_of(offset - 1, 16)],
            seq_send.at[0],
            seq_recv.at[0],
            {"seq": to},
        )
        return carry

    lax.fori_loop(1, N_SEQ, send_pieces, 0)
    pieces[496:512, :] = piece_src[rows_of(chip, 16), :]

    def owner_of(device, slot):
        prompt = (response_ref[3 * device] >> 1) + slot
        found = owner_ref[jnp.minimum(prompt, N_SEQ - 1)]
        return jnp.where(prompt < N_SEQ, found, -1)

    row, _ = iotas((32, 1))
    _, col = iotas((1, 512))
    source = (me + 31 - (col >> 4)) % N_SEQ
    same_row = (row & 15) == (col & 15)
    for place in range(CHIPS):
        to = 2 * lax.rem(chip + place + 1, CHIPS) + core
        wanted = jnp.where(row < 16, owner_of(to, 0), owner_of(to, 1))
        here = (source == wanted) & same_row
        pick_s[32 * place : 32 * place + 32, :] = jnp.where(here, 1.0, 0.0).astype(BF16)

    systems = []
    for b in (1, 2, 3):
        systems.append(tables_of(b))
        ring_pump(2 if b == 3 else 1)

    await_bytes(pieces.at[pl.ds(0, 496)], seq_recv.at[0])

    chosen_src[...] = dot(pick_s[...], pieces[...]).astype(BF16)

    def send_chosen(offset, carry):
        send(
            chosen_src.at[rows_of(offset - 1, 32)],
            chosen.at[rows_of(offset - 1, 32)],
            seq_send.at[1],
            seq_recv.at[1],
            {"seq": 2 * lax.rem(chip + offset, CHIPS) + core},
        )
        return carry

    lax.fori_loop(1, CHIPS, send_chosen, 0)
    chosen[480:512, :] = chosen_src[480:512, :]

    def between(level):
        if level < 5:
            ring_pump(1)

    for b, found in zip((1, 2, 3), inverse(systems, between)):
        inverse_s[b] = found.astype(BF16)
    loads[5].wait()

    def norm_block(b, out):
        outs_s[b] = out
        result = side_heads(gated(out, block_of(gate_ref, b))).astype(BF16)
        normed_s[SPAN * b : SPAN * b + SPAN, :] = result

    norm_block(0, dot3(scores_s[0], update_s[0]))
    loads[6].wait()
    for index, (slot_ref, _) in enumerate(cot_slots()):
        if index < 5:
            turn(index, slot_ref)
    ring_pump(2)

    await_bytes(chosen.at[pl.ds(0, 480)], seq_recv.at[1])
    for slot in range(2):
        for piece in range(CHIPS):
            place = lax.rem(chip + 15 - piece, CHIPS)
            starts[slot, 16 * (piece % 8) : 16 * (piece % 8) + 16, 128 * (piece // 8) : 128 * (piece // 8) + 128] = (
                chosen[pl.ds(pl.multiple_of(place * 32 + 16 * slot, 16), 16), :].astype(F32)
            )
    own = [response_ref[3 * me + j] for j in range(3)]
    fresh, later = [None, None], [None, None]
    for j in (1, 2):
        fresh.append(jnp.where(own[j] != own[j - 1], 1.0, 0.0).astype(F32))
        later.append(jnp.where((own[j] >> 1) != (own[0] >> 1), 1.0, 0.0).astype(F32))

    state = None
    for b in (1, 2, 3):
        if b == 1:
            state = starts[0]
        else:
            begun = (1.0 - later[b]) * starts[0] + later[b] * starts[1]
            state = fresh[b] * begun + (1.0 - fresh[b]) * state
        state_s[b - 1] = state
        _, _, rate, growth, _ = cols[b]
        both = dot3(jnp.concatenate([keys[b], queries[b]], axis=0), state)
        key_state, query_state = stack_heads(both[:64]), stack_heads(both[64:])
        key_state_s[b - 1] = key_state
        query_state_s[b - 1] = query_state
        update = dot(inverse_s[b], rate * (block_of(value_ref, b) - growth * key_state))
        update_s[b] = update
        if b < 3:
            state = last_growth(rows, b) * state + dot(tail_of(b), diagonal_heads(update), "tn")
        norm_block(b, growth * query_state + dot3(scores_s[b], update))
        if b < 3:
            ring_pump(1)

    def share(distance):
        block = (head + distance + N_HEAD) % N_HEAD
        return dot(normed_s[...], weight_ref[rows_of(block, 256), :], "nt")

    def sums_order(hop, to_right):
        if hop == 1:
            return (0, 1) if to_right else (2, 3)
        return (2, 3, 0, 1) if to_right else (0, 1, 2, 3)

    def sums_slot(hop, to_right):
        return 2 * (hop - 1) + (0 if to_right else 1)

    def sums_start(hop, to_right, chunk):
        here = (sums_slot(hop, to_right), pl.ds(64 * chunk, 64))
        send(
            sums_src.at[here],
            sums.at[here],
            sum_send.at[0],
            sum_recv.at[ring_index(hop, to_right, chunk)],
            {"head": right if to_right else left},
        )

    def sums_prepare(hop):
        for to_right in (True, False):
            share_s[sums_slot(hop, to_right)] = share(5 - hop if to_right else hop - 5)

    def sums_begin():
        across = share(4)
        for to_right in (True, False):
            low = 0 if to_right else 128
            sums_src[sums_slot(1, to_right), low : low + 128, :] = across[low : low + 128].astype(BF16)
        for place in range(2):
            for to_right in (True, False):
                sums_start(1, to_right, sums_order(1, to_right)[place])
        sums_prepare(2)
        for to_right in (True, False):
            slot, low = sums_slot(2, to_right), 128 if to_right else 0
            sums_src[slot, low : low + 128, :] = share_s[slot, low : low + 128, :].astype(BF16)
        for place in range(2):
            for to_right in (True, False):
                sums_start(2, to_right, sums_order(2, to_right)[place])

    sums_steps = [(hop, place) for hop in (1, 2, 3, 4) for place in range(2 if hop == 1 else 4)]

    def sums_pump(count):
        for _ in range(count):
            hop, place = sums_steps.pop(0)
            for to_right in (True, False):
                chunk = sums_order(hop, to_right)[place]
                here = pl.ds(64 * chunk, 64)
                arrived = sums.at[sums_slot(hop, to_right), here]
                await_bytes(arrived, sum_recv.at[ring_index(hop, to_right, chunk)])
                if hop < 4:
                    slot = sums_slot(hop + 1, to_right)
                    sums_src[slot, here, :] = (
                        share_s[slot, here, :] + arrived[...].astype(F32)
                    ).astype(BF16)
                    sums_start(hop + 1, to_right, chunk)

    loads[7].wait()
    sums_begin()
    for index, (slot_ref, _) in enumerate(cot_slots()):
        if index in (5, 6):
            turn(index, slot_ref)

    grad_normed = None
    for index, (slot_ref, block) in enumerate(cot_slots()):
        if index == 7:
            ring_pump(2)
            turn(7, slot_ref)
        term = dot(slot_ref[...], weight_ref[rows_of(block, 256), :])
        grad_normed = term if grad_normed is None else grad_normed + term
        share_w = dot(turned_s[index], normed_s[...]).astype(BF16)
        for quarter in range(4):
            place = (quarter % 2) * 1024 + (2 * block + quarter // 2) * 64
            weight_src[pl.ds(pl.multiple_of(place, 64), 64), :] = share_w[
                64 * quarter : 64 * quarter + 64
            ]
    send(
        weight_src.at[rows_of(1 - core, 1024)],
        weight_pair,
        seq_send.at[4],
        seq_recv.at[4],
        {"seq": 2 * chip + 1 - core},
    )
    for b in range(4):
        grad_out, grad_gate = gated_back(
            outs_s[b], block_of(gate_ref, b), stack_heads(grad_normed[SPAN * b : SPAN * b + SPAN])
        )
        grad_out_s[b] = grad_out
        grad_gate_ref[SPAN * b : SPAN * b + SPAN, :] = side_heads(grad_gate)

    grad_state = jnp.zeros((128, 256), F32)
    begun = [jnp.zeros((128, 256), F32), jnp.zeros((128, 256), F32)]
    for b in (3, 2, 1):
        _, _, rate, growth, remain = cols[b]
        grad_out = grad_out_s[b]
        grad_state_s[b] = grad_state
        grad_update = dot(scores_s[b], grad_out, "tn")
        if b < 3:
            grad_update += remain * stack_heads(dot(keys[b], grad_state))
        step = dot(inverse_s[b], grad_update, "tn")
        step_s[b] = step
        sides = jnp.concatenate(
            [side_heads(-(rate * growth) * step), side_heads(growth * grad_out)], axis=0
        )
        grad_in = dot(jnp.concatenate([keys[b], queries[b]], axis=0), sides, "tn")
        if b < 3:
            grad_in += last_growth(rows, b) * grad_state
        if b > 1:
            begun[0] += (fresh[b] * (1.0 - later[b])) * grad_in
            begun[1] += (fresh[b] * later[b]) * grad_in
            grad_state = (1.0 - fresh[b]) * grad_in
            if b == 2:
                sums_pump(1)
        else:
            begun[0] += grad_in
    for slot in range(2):
        for piece in range(CHIPS):
            grad_src[32 * piece + 16 * slot : 32 * piece + 16 * slot + 16, :] = begun[slot][
                16 * (piece % 8) : 16 * (piece % 8) + 16,
                128 * (piece // 8) : 128 * (piece // 8) + 128,
            ].astype(BF16)

    def send_grads(offset, carry):
        to = lax.rem(chip + offset, CHIPS)
        send(
            grad_src.at[rows_of(to, 32)],
            grad_pieces.at[rows_of(offset - 1, 32)],
            seq_send.at[2],
            seq_recv.at[2],
            {"seq": 2 * to + core},
        )
        return carry

    lax.fori_loop(1, CHIPS, send_grads, 0)
    grad_pieces[480:512, :] = grad_src[rows_of(chip, 32), :]

    sums_prepare(3)
    sums_pump(1)

    await_bytes(weight_pair, seq_recv.at[4])
    for part in range(4):
        place = core * 1024 + 256 * part
        weight_sum[256 * part : 256 * part + 256, :] = (
            weight_src[pl.ds(pl.multiple_of(place, 256), 256), :].astype(F32)
            + weight_pair[256 * part : 256 * part + 256, :].astype(F32)
        ).astype(BF16)

    def send_weight(offset, carry):
        to = lax.rem(chip + offset, CHIPS)
        send(
            weight_sum.at[rows_of(to, 64)],
            weight_in.at[rows_of(offset - 1, 64)],
            seq_send.at[5],
            seq_recv.at[5],
            {"seq": 2 * to + core},
        )
        return carry

    lax.fori_loop(1, 12, send_weight, 0)
    sums_pump(4)
    sums_prepare(4)
    _, col = iotas((1, 128))
    row, _ = iotas((512, 1))
    target = (me + 1 + (row >> 4)) % N_SEQ
    for part in range(4):
        owner = jnp.full((1, 128), -1, jnp.int32)
        for index in range(4):
            device = 2 * lax.rem(chip + 31 - (4 * part + index), CHIPS) + core
            for slot in range(2):
                owner = jnp.where((col >> 4) == 2 * index + slot, owner_of(device, slot), owner)
        here = (owner == target) & ((row & 15) == (col & 15))
        gather_s[:, 128 * part : 128 * part + 128] = jnp.where(here, 1.0, 0.0).astype(BF16)

    await_bytes(grad_pieces.at[pl.ds(0, 480)], seq_recv.at[2])

    owned_src[...] = dot(gather_s[...], grad_pieces[...]).astype(BF16)

    def send_owned(offset, carry):
        send(
            owned_src.at[rows_of(offset - 1, 16)],
            owned.at[rows_of(offset - 1, 16)],
            seq_send.at[3],
            seq_recv.at[3],
            {"seq": lax.rem(me + offset, N_SEQ)},
        )
        return carry

    lax.fori_loop(1, N_SEQ, send_owned, 0)
    sums_pump(2)
    owned[496:512, :] = owned_src[496:512, :]

    lax.fori_loop(12, CHIPS, send_weight, 0)

    grad_cums, grad_rates, grad_rows = [None] * 4, [None] * 4, [None] * 4

    def finish_block(b, grad_state, state_in):
        tables = (within_s[b], system_s[b], scores_s[b])
        found = block_grads(
            queries[b],
            keys[b],
            block_of(value_ref, b),
            cols[b],
            last_growth(rows, b),
            tables,
            step_s[b],
            update_s[b],
            grad_out_s[b],
            grad_state,
            state_in,
        )
        for raw_ref, out_ref, grad, scale in (
            (query_ref, grad_query_ref, found[0], SCALE),
            (key_ref, grad_key_ref, found[1], 1.0),
        ):
            raw = raw_ref[SPAN * b : SPAN * b + SPAN, :].astype(F32)
            out_ref[SPAN * b : SPAN * b + SPAN, :] = unit_back(raw, grad, scale)
        grad_value_ref[SPAN * b : SPAN * b + SPAN, :] = side_heads(found[2])
        grad_rates[b], grad_cums[b], grad_rows[b] = found[3:]

    for b in (1, 2, 3):
        finish_block(b, grad_state_s[b], (state_s[b - 1], key_state_s[b - 1], query_state_s[b - 1]))
        if b < 3:
            sums_pump(1)

    share_s[0] = share(0)
    await_bytes(owned.at[pl.ds(0, 496)], seq_recv.at[3])
    for piece in range(CHIPS):
        low, lane = 16 * (piece % 8), 128 * (piece // 8)
        one, two = [lax.rem(me + 63 - (2 * piece + side), N_SEQ) for side in range(2)]
        grad_state_s[0, low : low + 16, lane : lane + 128] = owned[rows_of(one, 16), :].astype(
            F32
        ) + owned[rows_of(two, 16), :].astype(F32)
    grad_state = grad_state_s[0]
    grad_update = dot(scores_s[0], grad_out_s[0], "tn")
    grad_update += cols[0][4] * stack_heads(dot(keys[0], grad_state))
    step_s[0] = dot(inverse_s[0], grad_update, "tn")
    finish_block(0, grad_state, None)
    grad_rate_ref[...], grad_decay_ref[...] = decay_grads(grad_cums, grad_rates, grad_rows)

    await_bytes(weight_in.at[pl.ds(0, 15 * 64)], seq_recv.at[5])
    total = weight_sum[rows_of(chip, 64), :].astype(F32)
    for slot in range(15):
        total += weight_in[64 * slot : 64 * slot + 64, :].astype(F32)
    grad_weight_ref[...] = total
    sums_pump(4)
    layer_ref[...] = (share_s[0] + sums[6].astype(F32) + sums[7].astype(F32)).astype(BF16)

    await_bytes(cots, ring_send.at[0])
    await_bytes(sums.at[pl.ds(0, 7)], sum_send.at[0])
    await_bytes(pieces.at[pl.ds(0, 496)], seq_send.at[0])
    await_bytes(chosen.at[pl.ds(0, 480)], seq_send.at[1])
    await_bytes(grad_pieces.at[pl.ds(0, 480)], seq_send.at[2])
    await_bytes(owned.at[pl.ds(0, 496)], seq_send.at[3])
    await_bytes(weight_pair, seq_send.at[4])
    await_bytes(weight_in.at[pl.ds(0, 15 * 64)], seq_send.at[5])


SCRATCH = [
    pltpu.VMEM((256, 128), BF16),
    pltpu.VMEM((256, 128), BF16),
    pltpu.VMEM((256, 256), BF16),
    pltpu.VMEM((256, 256), BF16),
    pltpu.VMEM((2, 256), F32),
    pltpu.VMEM((2, 256), F32),
    pltpu.VMEM((2048, 256), BF16),
    pltpu.VMEM((256, 256), BF16),
    pltpu.VMEM((7, 256, 256), BF16),
    pltpu.VMEM((256, 128), BF16),
    pltpu.VMEM((512, 128), BF16),
    pltpu.VMEM((512, 128), BF16),
    pltpu.VMEM((512, 128), BF16),
    pltpu.VMEM((2, 128, 256), F32),
    pltpu.VMEM((512, 128), BF16),
    pltpu.VMEM((512, 128), BF16),
    pltpu.VMEM((512, 128), BF16),
    pltpu.VMEM((512, 128), BF16),
    pltpu.VMEM((8, 256, 256), BF16),
    pltpu.VMEM((8, 256, 256), BF16),
    pltpu.VMEM((2048, 256), BF16),
    pltpu.VMEM((1024, 256), BF16),
    pltpu.VMEM((1024, 256), BF16),
    pltpu.VMEM((960, 256), BF16),
    pltpu.VMEM((4, 128, 128), F32),
    pltpu.VMEM((4, 128, 128), F32),
    pltpu.VMEM((4, 128, 128), F32),
    pltpu.VMEM((4, 128, 128), BF16),
    pltpu.VMEM((4, 128, 128), F32),
    pltpu.VMEM((4, 128, 128), F32),
    pltpu.VMEM((4, 128, 128), F32),
    pltpu.VMEM((4, 128, 128), F32),
    pltpu.VMEM((3, 128, 256), F32),
    pltpu.VMEM((4, 128, 256), F32),
    pltpu.VMEM((3, 128, 128), F32),
    pltpu.VMEM((3, 128, 128), F32),
    pltpu.VMEM((256, 256), BF16),
    pltpu.VMEM((8, 256, 256), F32),
    pltpu.VMEM((8, 256, 256), BF16),
    pltpu.VMEM((512, 512), BF16),
    pltpu.VMEM((512, 512), BF16),
    pltpu.SemaphoreType.DMA((8,)),
    pltpu.SemaphoreType.DMA((1,)),
    pltpu.SemaphoreType.DMA((32,)),
    pltpu.SemaphoreType.DMA((1,)),
    pltpu.SemaphoreType.DMA((32,)),
    pltpu.SemaphoreType.DMA((6,)),
    pltpu.SemaphoreType.DMA((6,)),
]


def finish_kernel(*refs):
    for index in range(8):
        refs[8 + index][...] = refs[index][...]


RESULTS = [
    jax.ShapeDtypeStruct((256, 256), BF16),
    jax.ShapeDtypeStruct((256, 128), F32),
    jax.ShapeDtypeStruct((256, 128), F32),
    jax.ShapeDtypeStruct((256, 256), F32),
    jax.ShapeDtypeStruct((256, 256), F32),
    jax.ShapeDtypeStruct((2, 256), F32),
    jax.ShapeDtypeStruct((2, 256), F32),
    jax.ShapeDtypeStruct((64, 256), F32),
]


def per_device(
    query_rows, key_rows, value_rows, output_gate, write_rate, log_decay,
    out_weight, out_cotangent, block_response, prefix_owner,
):
    vmem = pl.BlockSpec(memory_space=pltpu.VMEM)
    smem = pl.BlockSpec(memory_space=pltpu.SMEM)
    whole = pl.BlockSpec(memory_space=pl.ANY)
    results = pl.pallas_call(
        layer_kernel,
        out_shape=RESULTS,
        in_specs=[whole] * 8 + [smem] * 2,
        out_specs=[vmem] * 8,
        scratch_shapes=SCRATCH,
        compiler_params=pltpu.CompilerParams(
            collective_id=0, has_side_effects=True, vmem_limit_bytes=56 * 1024 * 1024
        ),
    )(
        query_rows, key_rows, value_rows, output_gate, write_rate, log_decay,
        out_weight, out_cotangent, block_response, prefix_owner,
    )
    return pl.pallas_call(
        finish_kernel,
        out_shape=RESULTS,
        in_specs=[vmem] * 8,
        out_specs=[vmem] * 8,
    )(*results)


def solution(mesh):
    rows = P("seq", "head")
    return jax.shard_map(
        per_device,
        mesh=mesh,
        in_specs=(rows, rows, rows, rows, P("head", "seq"), P("head", "seq"), P(None, "head"), rows, P(), P()),
        out_specs=(rows, rows, rows, rows, rows, P("head", "seq"), P("head", "seq"), rows),
        check_vma=False,
    )
```

```python
import functools

import jax
import jax.numpy as jnp
from jax import lax
from jax.experimental import pallas as pl
from jax.experimental.pallas import tpu as pltpu
from jax.sharding import PartitionSpec as P

N_SEQ = 32
N_HEAD = 8
CHIPS = 16
SPAN = 64
EPS = 1e-06
F32 = jnp.float32
BF16 = jnp.bfloat16
HIGHEST = lax.Precision.HIGHEST
MESH = pl.DeviceIdType.MESH
SCALE = 128 ** (-0.5)

KINDS = {"nn": ((1,), (0,)), "nt": ((1,), (1,)), "tn": ((0,), (0,))}


def dot(a, b, kind="nn"):
    return lax.dot_general(
        a.astype(BF16), b.astype(BF16), (KINDS[kind], ((), ())), preferred_element_type=F32
    )


def parts(x):
    high = x.astype(BF16)
    return high, (x - high.astype(F32)).astype(BF16)


def dot3(a, b, kind="nn"):
    a_high, a_low = parts(a)
    b_high, b_low = parts(b)
    return dot(a_high, b_high, kind) + (dot(a_high, b_low, kind) + dot(a_low, b_high, kind))


def dot_exact(a, b):
    return lax.dot_general(
        a, b, (KINDS["nn"], ((), ())), precision=HIGHEST, preferred_element_type=F32
    )


def iotas(shape=(128, 128)):
    return lax.broadcasted_iota(jnp.int32, shape, 0), lax.broadcasted_iota(jnp.int32, shape, 1)


def stack_heads(x):
    return jnp.concatenate([x[:, :128], x[:, 128:]], axis=0)


def side_heads(x):
    return jnp.concatenate([x[:64], x[64:]], axis=1)


def diagonal_heads(x):
    zero = jnp.zeros_like(x[:64])
    return jnp.concatenate(
        [jnp.concatenate([x[:64], zero], axis=1), jnp.concatenate([zero, x[64:]], axis=1)], axis=0
    )


def twice(x):
    return jnp.concatenate([x, x], axis=0)


def fold(x):
    return x[:64] + x[64:]


def half_swap(x):
    return jnp.concatenate([x[:, 64:], x[:, :64]], axis=1)


def by_block(x):
    lower = lax.broadcasted_iota(jnp.int32, (1, 128), 1) < 64
    rows = []
    for pair in range(2):
        first = x[0:1, 128 * pair : 128 * pair + 128]
        second = x[1:2, 128 * pair : 128 * pair + 128]
        rows.append(jnp.where(lower, first, half_swap(second)))
        rows.append(jnp.where(lower, half_swap(first), second))
    return jnp.concatenate(rows, axis=0)


def by_head(x):
    lower = lax.broadcasted_iota(jnp.int32, (1, 128), 1) < 64
    heads = ([], [])
    for pair in range(2):
        even, odd = x[2 * pair : 2 * pair + 1], x[2 * pair + 1 : 2 * pair + 2]
        heads[0].append(jnp.where(lower, even, half_swap(odd)))
        heads[1].append(jnp.where(lower, half_swap(even), odd))
    return jnp.concatenate([jnp.concatenate(row, axis=1) for row in heads], axis=0)


def turned(x):
    return jnp.transpose(jnp.concatenate([x, jnp.zeros((120, 128), F32)], axis=0))


def unit_scale(x):
    return lax.rsqrt(jnp.sum(x * x, axis=-1, keepdims=True) + EPS)


def unit_back(raw, grad, scale):
    inv = unit_scale(raw)
    unit = raw * inv
    return (scale * inv) * (grad - unit * jnp.sum(grad * unit, axis=-1, keepdims=True))


def running_decay(write_rate, log_decay):
    row, col = iotas()
    same = (row >> 6) == (col >> 6)
    upto = jnp.where(same & (row <= col), 1.0, 0.0).astype(F32)
    both = jnp.concatenate([by_block(log_decay), by_block(write_rate)], axis=0)
    summed = dot_exact(both, upto)
    rows = jnp.concatenate([summed[:4], both[4:]], axis=0)
    return rows[:4], turned(rows)


def block_columns(rows, columns, b):
    cum_row = rows[b : b + 1]
    cum = columns[:, b : b + 1]
    rate = columns[:, 4 + b : 5 + b]
    first = lax.broadcasted_iota(jnp.int32, (128, 1), 0) < 64
    last = jnp.where(first, cum_row[:, 63:64], cum_row[:, 127:128])
    return cum_row, cum, rate, jnp.exp(cum), jnp.exp(last - cum)


def last_growth(rows, b):
    lane = lax.broadcasted_iota(jnp.int32, (1, 256), 1)
    return jnp.exp(jnp.where(lane < 128, rows[b : b + 1, 63:64], rows[b : b + 1, 127:128]))


def block_tables(query, key, rows, columns, b):
    row, col = iotas()
    causal = ((row >> 6) == (col >> 6)) & (row >= col)
    cum_row, cum, rate, _, _ = block_columns(rows, columns, b)
    within = jnp.where(causal, jnp.exp(jnp.where(causal, cum - cum_row, 0.0)), 0.0)
    key2 = twice(key)
    strict = jnp.where(row > col, within, 0.0) * rate
    system = strict * dot3(key2, key2, "nt")
    query_key = dot3(twice(query), key2, "nt") * within
    return within, system, query_key


def inverse(systems, between=None):
    row, col = iotas()
    found = None
    for level in range(6):
        here = ((row >> (level + 1)) == (col >> (level + 1))) & ((row >> level) != (col >> level))
        below = [jnp.where(here, system, 0.0) for system in systems]
        if found is None:
            eye = jnp.where(row == col, 1.0, 0.0).astype(F32)
            found = [eye - one for one in below]
        else:
            half = [dot3(one, two) for one, two in zip(found, below)]
            found = [one - dot3(two, one) for one, two in zip(found, half)]
            if between is not None:
                between(level)
    return found


def gated(out, gate):
    inv = lax.rsqrt(jnp.mean(out * out, axis=-1, keepdims=True) + EPS)
    return out * inv * (gate / (1.0 + jnp.exp(-gate)))


def gated_back(out, gate, grad):
    inv = lax.rsqrt(jnp.mean(out * out, axis=-1, keepdims=True) + EPS)
    sig = 1.0 / (1.0 + jnp.exp(-gate))
    weighted = grad * (gate * sig)
    grad_gate = grad * out * inv * (sig * (1.0 + gate * (1.0 - sig)))
    along = jnp.mean(weighted * out, axis=-1, keepdims=True)
    return inv * (weighted - out * (inv * inv * along)), grad_gate


def score_grads(query, key, tables, update, grad_out):
    within, _, query_key = tables
    grad_scores = dot3(grad_out, update, "nt")
    masked = grad_scores * within
    return grad_scores * query_key, fold(dot(masked, twice(key))), dot(masked, twice(query), "tn")


def block_grads(
    key, value, cols, growth_last, tables, step, update, grad_out, grad_state, state_in, scored
):
    _, _, rate, growth, remain = cols
    within, system, _ = tables
    scored_spread, grad_query, scored_key = scored
    row, col = iotas()
    key2 = twice(key)
    grad_system = -dot(step, update, "nt")
    strict = jnp.where(row > col, grad_system * within, 0.0) * rate
    pulled = grad_system * system
    spread = scored_spread + pulled
    state_key = dot(diagonal_heads(update), grad_state, "nt")
    grad_key = fold(
        scored_key + dot(strict, key2) + dot(strict, key2, "tn") + remain * state_key
    )
    tail = remain * jnp.sum(key2 * state_key, axis=-1, keepdims=True)
    grad_cum = jnp.sum(spread, axis=-1, keepdims=True) - tail
    grad_row = -jnp.sum(spread, axis=0, keepdims=True)
    end0 = jnp.sum(tail[:64], axis=0, keepdims=True)
    end1 = jnp.sum(tail[64:], axis=0, keepdims=True)
    grad_value = rate * step
    if state_in is None:
        inner = value
    else:
        state, key_state, query_state = state_in
        inner = value - growth * key_state
        out_growth = growth * grad_out
        in_growth = growth * grad_value
        grad_cum += jnp.sum(out_growth * query_state - in_growth * key_state, axis=-1, keepdims=True)
        grad_query += dot3(side_heads(out_growth), state, "nt")
        grad_key -= dot(side_heads(in_growth), state, "nt")
        kept = jnp.sum(growth_last * (state * grad_state), axis=0, keepdims=True)
        end0 += jnp.sum(kept[:, :128], axis=1, keepdims=True)
        end1 += jnp.sum(kept[:, 128:], axis=1, keepdims=True)
    lane = lax.broadcasted_iota(jnp.int32, (1, 128), 1)
    grad_row += jnp.where(lane == 63, end0, 0.0) + jnp.where(lane == 127, end1, 0.0)
    grad_rate = jnp.sum(step * inner, axis=-1, keepdims=True) + (
        jnp.sum(pulled, axis=-1, keepdims=True) / rate
    )
    return grad_query, grad_key, grad_value, grad_rate, grad_cum, grad_row


def decay_grads(grad_cums, grad_rates, grad_rows):
    row, col = iotas()
    packed = jnp.zeros((128, 128), F32)
    for b in range(4):
        packed = jnp.where(col == b, grad_cums[b], packed)
        packed = jnp.where(col == 4 + b, grad_rates[b], packed)
    packed = jnp.transpose(packed)[:8]
    since = jnp.where(((row >> 6) == (col >> 6)) & (row >= col), 1.0, 0.0).astype(F32)
    grad_cum = packed[:4] + jnp.concatenate(grad_rows, axis=0)
    grad_cum = jnp.concatenate([grad_cum, jnp.zeros((4, 128), F32)], axis=0)
    return by_head(packed[4:]), by_head(dot_exact(grad_cum, since)[:4])


def rows_of(index, size):
    return pl.ds(pl.multiple_of(index * size, size), size)


def send(src, dst, send_sem, recv_sem, device):
    copy = pltpu.make_async_remote_copy(
        src_ref=src,
        dst_ref=dst,
        send_sem=send_sem,
        recv_sem=recv_sem,
        device_id=device,
        device_id_type=MESH,
    )
    copy.start()


def await_bytes(ref, sem):
    pltpu.make_async_copy(ref, ref, sem).wait()


def layer_kernel(
    query_hbm,
    key_hbm,
    value_hbm,
    gate_hbm,
    rate_hbm,
    decay_hbm,
    weight_hbm,
    cot_hbm,
    response_ref,
    owner_ref,
    layer_ref,
    grad_query_ref,
    grad_key_ref,
    grad_value_ref,
    grad_gate_ref,
    grad_rate_ref,
    grad_decay_ref,
    grad_weight_ref,
    query_ref,
    key_ref,
    value_ref,
    gate_ref,
    rate_ref,
    decay_ref,
    weight_ref,
    cot_ref,
    cots,
    piece_src,
    pieces,
    chosen_src,
    chosen,
    starts,
    grad_src,
    grad_pieces,
    owned_src,
    owned,
    sums_src,
    sums,
    weight_src,
    weight_pair,
    weight_sum,
    weight_in,
    within_s,
    system_s,
    scores_s,
    inverse_s,
    outs_s,
    update_s,
    step_s,
    grad_out_s,
    state_s,
    grad_state_s,
    key_state_s,
    query_state_s,
    normed_s,
    share_s,
    turned_s,
    pick_s,
    gather_s,
    load_sem,
    ring_send,
    ring_recv,
    sum_send,
    sum_recv,
    seq_send,
    seq_recv,
):
    me = lax.axis_index("seq")
    head = lax.axis_index("head")
    chip, core = lax.div(me, 2), lax.rem(me, 2)
    right, left = lax.rem(head + 1, N_HEAD), lax.rem(head + N_HEAD - 1, N_HEAD)

    loads = [
        pltpu.make_async_copy(src, dst, load_sem.at[index])
        for index, (src, dst) in enumerate(
            (
                (rate_hbm, rate_ref),
                (decay_hbm, decay_ref),
                (key_hbm, key_ref),
                (query_hbm, query_ref),
                (value_hbm, value_ref),
                (gate_hbm, gate_ref),
                (cot_hbm, cot_ref),
                (weight_hbm, weight_ref),
            )
        )
    ]
    for load in loads:
        load.start()

    barrier = pltpu.get_barrier_semaphore()

    def greet(offset, carry):
        pl.semaphore_signal(
            barrier, inc=1, device_id={"seq": lax.rem(me + offset, N_SEQ)}, device_id_type=MESH
        )
        return carry

    lax.fori_loop(1, N_SEQ, greet, 0)
    for neighbour in (left, right):
        pl.semaphore_signal(barrier, inc=1, device_id={"head": neighbour}, device_id_type=MESH)

    def ring_order(hop, to_right):
        order = (0, 1, 2, 3) if to_right else (2, 3, 0, 1)
        return order[:2] if hop == 4 else order

    def ring_chunk(hop, to_right, chunk):
        slot = hop - 1 if to_right or hop == 4 else 3 + hop
        return cots.at[slot, pl.ds(64 * chunk, 64)]

    def ring_index(hop, to_right, chunk):
        return 8 * (hop - 1) + (0 if to_right else 4) + chunk

    def ring_start(hop, to_right, chunk):
        if hop == 1:
            src = cot_hbm.at[pl.ds(64 * chunk, 64)]
        else:
            src = ring_chunk(hop - 1, to_right, chunk)
        send(
            src,
            ring_chunk(hop, to_right, chunk),
            ring_send.at[0],
            ring_recv.at[ring_index(hop, to_right, chunk)],
            {"head": right if to_right else left},
        )

    ring_steps = [(hop, place) for hop in (1, 2, 3, 4) for place in range(2 if hop == 4 else 4)]

    def ring_pump(count):
        for _ in range(count):
            hop, place = ring_steps.pop(0)
            for to_right in (True, False):
                chunk = ring_order(hop, to_right)[place]
                await_bytes(
                    ring_chunk(hop, to_right, chunk), ring_recv.at[ring_index(hop, to_right, chunk)]
                )
                if hop < 4 and chunk in ring_order(hop + 1, to_right):
                    ring_start(hop + 1, to_right, chunk)

    def cot_slots():
        yield cot_ref, head
        for hop in (1, 2, 3):
            yield cots.at[hop - 1], (head - hop + N_HEAD) % N_HEAD
            yield cots.at[3 + hop], (head + hop) % N_HEAD
        yield cots.at[3], (head + 4) % N_HEAD

    def turn(index, slot_ref):
        turned_s[index] = jnp.transpose(slot_ref[...])

    for load in loads[:5]:
        load.wait()
    rate2, decay2 = rate_ref[...], decay_ref[...]
    rows, columns = running_decay(rate2, decay2)

    def unit_block(ref, b):
        raw = ref[SPAN * b : SPAN * b + SPAN, :].astype(F32)
        return raw * unit_scale(raw)

    def block_of(ref, b):
        return stack_heads(ref[SPAN * b : SPAN * b + SPAN, :]).astype(F32)

    queries = [unit_block(query_ref, b) * SCALE for b in range(4)]
    keys = [unit_block(key_ref, b) for b in range(4)]
    cols = [block_columns(rows, columns, b) for b in range(4)]

    def tables_of(b):
        within, system, query_key = block_tables(queries[b], keys[b], rows, columns, b)
        within_s[b] = within
        system_s[b] = system
        scores_s[b] = query_key
        return system

    def tail_of(b):
        return twice(keys[b]) * cols[b][4]

    first_system = tables_of(0)
    pl.semaphore_wait(barrier, N_SEQ + 1)
    for place in range(4):
        for to_right in (True, False):
            ring_start(1, to_right, ring_order(1, to_right)[place])
    inverse_s[0] = inverse([first_system])[0].astype(BF16)
    update = dot(inverse_s[0], cols[0][2] * block_of(value_ref, 0))
    update_s[0] = update
    final = dot(tail_of(0), diagonal_heads(update), "tn")
    piece_src[0:128, :] = final[:, :128].astype(BF16)
    piece_src[128:256, :] = final[:, 128:].astype(BF16)

    def send_pieces(offset, carry):
        to = lax.rem(me + offset, N_SEQ)
        send(
            piece_src.at[rows_of(lax.div(to, 2), 16)],
            pieces.at[rows_of(offset - 1, 16)],
            seq_send.at[0],
            seq_recv.at[0],
            {"seq": to},
        )
        return carry

    lax.fori_loop(1, N_SEQ, send_pieces, 0)
    pieces[496:512, :] = piece_src[rows_of(chip, 16), :]

    def owner_of(device, slot):
        prompt = (response_ref[3 * device] >> 1) + slot
        found = owner_ref[jnp.minimum(prompt, N_SEQ - 1)]
        return jnp.where(prompt < N_SEQ, found, -1)

    row, _ = iotas((32, 1))
    _, col = iotas((1, 512))
    source = (me + 31 - (col >> 4)) % N_SEQ
    same_row = (row & 15) == (col & 15)
    for place in range(CHIPS):
        to = 2 * lax.rem(chip + place + 1, CHIPS) + core
        wanted = jnp.where(row < 16, owner_of(to, 0), owner_of(to, 1))
        here = (source == wanted) & same_row
        pick_s[32 * place : 32 * place + 32, :] = jnp.where(here, 1.0, 0.0).astype(BF16)

    systems = []
    for b in (1, 2, 3):
        systems.append(tables_of(b))
        ring_pump(2 if b == 3 else 1)

    await_bytes(pieces.at[pl.ds(0, 496)], seq_recv.at[0])

    chosen_src[...] = dot(pick_s[...], pieces[...]).astype(BF16)

    def send_chosen(offset, carry):
        send(
            chosen_src.at[rows_of(offset - 1, 32)],
            chosen.at[rows_of(offset - 1, 32)],
            seq_send.at[1],
            seq_recv.at[1],
            {"seq": 2 * lax.rem(chip + offset, CHIPS) + core},
        )
        return carry

    lax.fori_loop(1, CHIPS, send_chosen, 0)
    chosen[480:512, :] = chosen_src[480:512, :]

    def between(level):
        if level < 5:
            ring_pump(1)

    for b, found in zip((1, 2, 3), inverse(systems, between)):
        inverse_s[b] = found.astype(BF16)
    loads[5].wait()

    def norm_block(b, out):
        outs_s[b] = out
        result = side_heads(gated(out, block_of(gate_ref, b))).astype(BF16)
        normed_s[SPAN * b : SPAN * b + SPAN, :] = result

    norm_block(0, dot3(scores_s[0], update_s[0]))
    loads[6].wait()
    for index, (slot_ref, _) in enumerate(cot_slots()):
        if index < 5:
            turn(index, slot_ref)
    ring_pump(2)

    await_bytes(chosen.at[pl.ds(0, 480)], seq_recv.at[1])
    for slot in range(2):
        for piece in range(CHIPS):
            place = lax.rem(chip + 15 - piece, CHIPS)
            starts[slot, 16 * (piece % 8) : 16 * (piece % 8) + 16, 128 * (piece // 8) : 128 * (piece // 8) + 128] = (
                chosen[pl.ds(pl.multiple_of(place * 32 + 16 * slot, 16), 16), :].astype(F32)
            )
    own = [response_ref[3 * me + j] for j in range(3)]
    fresh, later = [None, None], [None, None]
    for j in (1, 2):
        fresh.append(jnp.where(own[j] != own[j - 1], 1.0, 0.0).astype(F32))
        later.append(jnp.where((own[j] >> 1) != (own[0] >> 1), 1.0, 0.0).astype(F32))

    state = None
    for b in (1, 2, 3):
        if b == 1:
            state = starts[0]
        else:
            begun = (1.0 - later[b]) * starts[0] + later[b] * starts[1]
            state = fresh[b] * begun + (1.0 - fresh[b]) * state
        state_s[b - 1] = state
        _, _, rate, growth, _ = cols[b]
        both = dot3(jnp.concatenate([keys[b], queries[b]], axis=0), state)
        key_state, query_state = stack_heads(both[:64]), stack_heads(both[64:])
        key_state_s[b - 1] = key_state
        query_state_s[b - 1] = query_state
        update = dot(inverse_s[b], rate * (block_of(value_ref, b) - growth * key_state))
        update_s[b] = update
        if b < 3:
            state = last_growth(rows, b) * state + dot(tail_of(b), diagonal_heads(update), "tn")
        norm_block(b, growth * query_state + dot3(scores_s[b], update))
        if b < 3:
            ring_pump(1)

    def share(distance):
        block = (head + distance + N_HEAD) % N_HEAD
        return dot(normed_s[...], weight_ref[rows_of(block, 256), :], "nt")

    def sums_order(hop, to_right):
        if hop == 1:
            return (0, 1) if to_right else (2, 3)
        return (2, 3, 0, 1) if to_right else (0, 1, 2, 3)

    def sums_slot(hop, to_right):
        return 2 * (hop - 1) + (0 if to_right else 1)

    def sums_start(hop, to_right, chunk):
        here = (sums_slot(hop, to_right), pl.ds(64 * chunk, 64))
        send(
            sums_src.at[here],
            sums.at[here],
            sum_send.at[0],
            sum_recv.at[ring_index(hop, to_right, chunk)],
            {"head": right if to_right else left},
        )

    def sums_prepare(hop):
        for to_right in (True, False):
            share_s[sums_slot(hop, to_right)] = share(5 - hop if to_right else hop - 5)

    def sums_begin():
        across = share(4)
        for to_right in (True, False):
            low = 0 if to_right else 128
            sums_src[sums_slot(1, to_right), low : low + 128, :] = across[low : low + 128].astype(BF16)
        for place in range(2):
            for to_right in (True, False):
                sums_start(1, to_right, sums_order(1, to_right)[place])
        sums_prepare(2)
        for to_right in (True, False):
            slot, low = sums_slot(2, to_right), 128 if to_right else 0
            sums_src[slot, low : low + 128, :] = share_s[slot, low : low + 128, :].astype(BF16)
        for place in range(2):
            for to_right in (True, False):
                sums_start(2, to_right, sums_order(2, to_right)[place])

    sums_steps = [(hop, place) for hop in (1, 2, 3, 4) for place in range(2 if hop == 1 else 4)]

    def sums_pump(count):
        for _ in range(count):
            hop, place = sums_steps.pop(0)
            for to_right in (True, False):
                chunk = sums_order(hop, to_right)[place]
                here = pl.ds(64 * chunk, 64)
                arrived = sums.at[sums_slot(hop, to_right), here]
                await_bytes(arrived, sum_recv.at[ring_index(hop, to_right, chunk)])
                if hop < 4:
                    slot = sums_slot(hop + 1, to_right)
                    sums_src[slot, here, :] = (
                        share_s[slot, here, :] + arrived[...].astype(F32)
                    ).astype(BF16)
                    sums_start(hop + 1, to_right, chunk)

    loads[7].wait()
    sums_begin()
    for index, (slot_ref, _) in enumerate(cot_slots()):
        if index in (5, 6):
            turn(index, slot_ref)

    grad_normed = None
    for index, (slot_ref, block) in enumerate(cot_slots()):
        if index == 7:
            ring_pump(2)
            turn(7, slot_ref)
        term = dot(slot_ref[...], weight_ref[rows_of(block, 256), :])
        grad_normed = term if grad_normed is None else grad_normed + term
        share_w = dot(turned_s[index], normed_s[...]).astype(BF16)
        for quarter in range(4):
            place = (quarter % 2) * 1024 + (2 * block + quarter // 2) * 64
            weight_src[pl.ds(pl.multiple_of(place, 64), 64), :] = share_w[
                64 * quarter : 64 * quarter + 64
            ]
    send(
        weight_src.at[rows_of(1 - core, 1024)],
        weight_pair,
        seq_send.at[4],
        seq_recv.at[4],
        {"seq": 2 * chip + 1 - core},
    )
    for b in range(4):
        grad_out, grad_gate = gated_back(
            outs_s[b], block_of(gate_ref, b), stack_heads(grad_normed[SPAN * b : SPAN * b + SPAN])
        )
        grad_out_s[b] = grad_out
        grad_gate_ref[SPAN * b : SPAN * b + SPAN, :] = side_heads(grad_gate)

    grad_state = jnp.zeros((128, 256), F32)
    begun = [jnp.zeros((128, 256), F32), jnp.zeros((128, 256), F32)]
    for b in (3, 2, 1):
        _, _, rate, growth, remain = cols[b]
        grad_out = grad_out_s[b]
        grad_state_s[b] = grad_state
        grad_update = dot(scores_s[b], grad_out, "tn")
        if b < 3:
            grad_update += remain * stack_heads(dot(keys[b], grad_state))
        step = dot(inverse_s[b], grad_update, "tn")
        step_s[b] = step
        sides = jnp.concatenate(
            [side_heads(-(rate * growth) * step), side_heads(growth * grad_out)], axis=0
        )
        grad_in = dot(jnp.concatenate([keys[b], queries[b]], axis=0), sides, "tn")
        if b < 3:
            grad_in += last_growth(rows, b) * grad_state
        if b > 1:
            begun[0] += (fresh[b] * (1.0 - later[b])) * grad_in
            begun[1] += (fresh[b] * later[b]) * grad_in
            grad_state = (1.0 - fresh[b]) * grad_in
            if b == 2:
                sums_pump(1)
        else:
            begun[0] += grad_in
    for slot in range(2):
        for piece in range(CHIPS):
            grad_src[32 * piece + 16 * slot : 32 * piece + 16 * slot + 16, :] = begun[slot][
                16 * (piece % 8) : 16 * (piece % 8) + 16,
                128 * (piece // 8) : 128 * (piece // 8) + 128,
            ].astype(BF16)

    def send_grads(offset, carry):
        to = lax.rem(chip + offset, CHIPS)
        send(
            grad_src.at[rows_of(to, 32)],
            grad_pieces.at[rows_of(offset - 1, 32)],
            seq_send.at[2],
            seq_recv.at[2],
            {"seq": 2 * to + core},
        )
        return carry

    lax.fori_loop(1, CHIPS, send_grads, 0)
    grad_pieces[480:512, :] = grad_src[rows_of(chip, 32), :]

    sums_prepare(3)
    sums_pump(1)

    await_bytes(weight_pair, seq_recv.at[4])
    for part in range(4):
        place = core * 1024 + 256 * part
        weight_sum[256 * part : 256 * part + 256, :] = (
            weight_src[pl.ds(pl.multiple_of(place, 256), 256), :].astype(F32)
            + weight_pair[256 * part : 256 * part + 256, :].astype(F32)
        ).astype(BF16)

    def send_weight(offset, carry):
        to = lax.rem(chip + offset, CHIPS)
        send(
            weight_sum.at[rows_of(to, 64)],
            weight_in.at[rows_of(offset - 1, 64)],
            seq_send.at[5],
            seq_recv.at[5],
            {"seq": 2 * to + core},
        )
        return carry

    lax.fori_loop(1, CHIPS, send_weight, 0)
    sums_pump(4)
    sums_prepare(4)
    _, col = iotas((1, 128))
    row, _ = iotas((512, 1))
    target = (me + 1 + (row >> 4)) % N_SEQ
    for part in range(4):
        owner = jnp.full((1, 128), -1, jnp.int32)
        for index in range(4):
            device = 2 * lax.rem(chip + 31 - (4 * part + index), CHIPS) + core
            for slot in range(2):
                owner = jnp.where((col >> 4) == 2 * index + slot, owner_of(device, slot), owner)
        here = (owner == target) & ((row & 15) == (col & 15))
        gather_s[:, 128 * part : 128 * part + 128] = jnp.where(here, 1.0, 0.0).astype(BF16)

    await_bytes(grad_pieces.at[pl.ds(0, 480)], seq_recv.at[2])

    owned_src[...] = dot(gather_s[...], grad_pieces[...]).astype(BF16)

    def send_owned(offset, carry):
        send(
            owned_src.at[rows_of(offset - 1, 16)],
            owned.at[rows_of(offset - 1, 16)],
            seq_send.at[3],
            seq_recv.at[3],
            {"seq": lax.rem(me + offset, N_SEQ)},
        )
        return carry

    lax.fori_loop(1, N_SEQ, send_owned, 0)
    sums_pump(2)
    owned[496:512, :] = owned_src[496:512, :]


    grad_cums, grad_rates, grad_rows = [None] * 4, [None] * 4, [None] * 4

    def tables_found(b):
        return within_s[b], system_s[b], scores_s[b]

    def scored_of(b):
        return score_grads(queries[b], keys[b], tables_found(b), update_s[b], grad_out_s[b])

    def finish_block(b, grad_state, state_in, scored):
        found = block_grads(
            keys[b],
            block_of(value_ref, b),
            cols[b],
            last_growth(rows, b),
            tables_found(b),
            step_s[b],
            update_s[b],
            grad_out_s[b],
            grad_state,
            state_in,
            scored,
        )
        for raw_ref, out_ref, grad, scale in (
            (query_ref, grad_query_ref, found[0], SCALE),
            (key_ref, grad_key_ref, found[1], 1.0),
        ):
            raw = raw_ref[SPAN * b : SPAN * b + SPAN, :].astype(F32)
            out_ref[SPAN * b : SPAN * b + SPAN, :] = unit_back(raw, grad, scale)
        grad_value_ref[SPAN * b : SPAN * b + SPAN, :] = side_heads(found[2])
        grad_rates[b], grad_cums[b], grad_rows[b] = found[3:]

    for b in (1, 2, 3):
        state_in = (state_s[b - 1], key_state_s[b - 1], query_state_s[b - 1])
        finish_block(b, grad_state_s[b], state_in, scored_of(b))
        if b < 3:
            sums_pump(1)

    share_s[0] = share(0)
    scored = scored_of(0)
    grad_update = dot(scores_s[0], grad_out_s[0], "tn")
    await_bytes(weight_in.at[pl.ds(0, 15 * 64)], seq_recv.at[5])
    total = weight_sum[rows_of(chip, 64), :].astype(F32)
    for slot in range(15):
        total += weight_in[64 * slot : 64 * slot + 64, :].astype(F32)
    grad_weight_ref[...] = total
    await_bytes(owned.at[pl.ds(0, 496)], seq_recv.at[3])
    for piece in range(CHIPS):
        low, lane = 16 * (piece % 8), 128 * (piece // 8)
        one, two = [lax.rem(me + 63 - (2 * piece + side), N_SEQ) for side in range(2)]
        grad_state_s[0, low : low + 16, lane : lane + 128] = owned[rows_of(one, 16), :].astype(
            F32
        ) + owned[rows_of(two, 16), :].astype(F32)
    grad_state = grad_state_s[0]
    grad_update += cols[0][4] * stack_heads(dot(keys[0], grad_state))
    step_s[0] = dot(inverse_s[0], grad_update, "tn")
    finish_block(0, grad_state, None, scored)
    grad_rate_ref[...], grad_decay_ref[...] = decay_grads(grad_cums, grad_rates, grad_rows)

    sums_pump(4)
    layer_ref[...] = (share_s[0] + sums[6].astype(F32) + sums[7].astype(F32)).astype(BF16)

    await_bytes(cots, ring_send.at[0])
    await_bytes(sums.at[pl.ds(0, 7)], sum_send.at[0])
    await_bytes(pieces.at[pl.ds(0, 496)], seq_send.at[0])
    await_bytes(chosen.at[pl.ds(0, 480)], seq_send.at[1])
    await_bytes(grad_pieces.at[pl.ds(0, 480)], seq_send.at[2])
    await_bytes(owned.at[pl.ds(0, 496)], seq_send.at[3])
    await_bytes(weight_pair, seq_send.at[4])
    await_bytes(weight_in.at[pl.ds(0, 15 * 64)], seq_send.at[5])


SCRATCH = [
    pltpu.VMEM((256, 128), BF16),
    pltpu.VMEM((256, 128), BF16),
    pltpu.VMEM((256, 256), BF16),
    pltpu.VMEM((256, 256), BF16),
    pltpu.VMEM((2, 256), F32),
    pltpu.VMEM((2, 256), F32),
    pltpu.VMEM((2048, 256), BF16),
    pltpu.VMEM((256, 256), BF16),
    pltpu.VMEM((7, 256, 256), BF16),
    pltpu.VMEM((256, 128), BF16),
    pltpu.VMEM((512, 128), BF16),
    pltpu.VMEM((512, 128), BF16),
    pltpu.VMEM((512, 128), BF16),
    pltpu.VMEM((2, 128, 256), F32),
    pltpu.VMEM((512, 128), BF16),
    pltpu.VMEM((512, 128), BF16),
    pltpu.VMEM((512, 128), BF16),
    pltpu.VMEM((512, 128), BF16),
    pltpu.VMEM((8, 256, 256), BF16),
    pltpu.VMEM((8, 256, 256), BF16),
    pltpu.VMEM((2048, 256), BF16),
    pltpu.VMEM((1024, 256), BF16),
    pltpu.VMEM((1024, 256), BF16),
    pltpu.VMEM((960, 256), BF16),
    pltpu.VMEM((4, 128, 128), F32),
    pltpu.VMEM((4, 128, 128), F32),
    pltpu.VMEM((4, 128, 128), F32),
    pltpu.VMEM((4, 128, 128), BF16),
    pltpu.VMEM((4, 128, 128), F32),
    pltpu.VMEM((4, 128, 128), F32),
    pltpu.VMEM((4, 128, 128), F32),
    pltpu.VMEM((4, 128, 128), F32),
    pltpu.VMEM((3, 128, 256), F32),
    pltpu.VMEM((4, 128, 256), F32),
    pltpu.VMEM((3, 128, 128), F32),
    pltpu.VMEM((3, 128, 128), F32),
    pltpu.VMEM((256, 256), BF16),
    pltpu.VMEM((8, 256, 256), F32),
    pltpu.VMEM((8, 256, 256), BF16),
    pltpu.VMEM((512, 512), BF16),
    pltpu.VMEM((512, 512), BF16),
    pltpu.SemaphoreType.DMA((8,)),
    pltpu.SemaphoreType.DMA((1,)),
    pltpu.SemaphoreType.DMA((32,)),
    pltpu.SemaphoreType.DMA((1,)),
    pltpu.SemaphoreType.DMA((32,)),
    pltpu.SemaphoreType.DMA((6,)),
    pltpu.SemaphoreType.DMA((6,)),
]


def finish_kernel(*refs):
    for index in range(8):
        refs[8 + index][...] = refs[index][...]


RESULTS = [
    jax.ShapeDtypeStruct((256, 256), BF16),
    jax.ShapeDtypeStruct((256, 128), F32),
    jax.ShapeDtypeStruct((256, 128), F32),
    jax.ShapeDtypeStruct((256, 256), F32),
    jax.ShapeDtypeStruct((256, 256), F32),
    jax.ShapeDtypeStruct((2, 256), F32),
    jax.ShapeDtypeStruct((2, 256), F32),
    jax.ShapeDtypeStruct((64, 256), F32),
]


def per_device(
    query_rows, key_rows, value_rows, output_gate, write_rate, log_decay,
    out_weight, out_cotangent, block_response, prefix_owner,
):
    vmem = pl.BlockSpec(memory_space=pltpu.VMEM)
    smem = pl.BlockSpec(memory_space=pltpu.SMEM)
    whole = pl.BlockSpec(memory_space=pl.ANY)
    results = pl.pallas_call(
        layer_kernel,
        out_shape=RESULTS,
        in_specs=[whole] * 8 + [smem] * 2,
        out_specs=[vmem] * 8,
        scratch_shapes=SCRATCH,
        compiler_params=pltpu.CompilerParams(
            collective_id=0, has_side_effects=True, vmem_limit_bytes=56 * 1024 * 1024
        ),
    )(
        query_rows, key_rows, value_rows, output_gate, write_rate, log_decay,
        out_weight, out_cotangent, block_response, prefix_owner,
    )
    return pl.pallas_call(
        finish_kernel,
        out_shape=RESULTS,
        in_specs=[vmem] * 8,
        out_specs=[vmem] * 8,
    )(*results)


def solution(mesh):
    rows = P("seq", "head")
    return jax.shard_map(
        per_device,
        mesh=mesh,
        in_specs=(rows, rows, rows, rows, P("head", "seq"), P("head", "seq"), P(None, "head"), rows, P(), P()),
        out_specs=(rows, rows, rows, rows, rows, P("head", "seq"), P("head", "seq"), rows),
        check_vma=False,
    )
```

```python
import functools

import jax
import jax.numpy as jnp
from jax import lax
from jax.experimental import pallas as pl
from jax.experimental.pallas import tpu as pltpu
from jax.sharding import PartitionSpec as P

N_SEQ = 32
N_HEAD = 8
CHIPS = 16
SPAN = 64
EPS = 1e-06
F32 = jnp.float32
BF16 = jnp.bfloat16
HIGHEST = lax.Precision.HIGHEST
MESH = pl.DeviceIdType.MESH
SCALE = 128 ** (-0.5)

KINDS = {"nn": ((1,), (0,)), "nt": ((1,), (1,)), "tn": ((0,), (0,))}


def dot(a, b, kind="nn"):
    return lax.dot_general(
        a.astype(BF16), b.astype(BF16), (KINDS[kind], ((), ())), preferred_element_type=F32
    )


def parts(x):
    high = x.astype(BF16)
    return high, (x - high.astype(F32)).astype(BF16)


def dot3(a, b, kind="nn"):
    a_high, a_low = parts(a)
    b_high, b_low = parts(b)
    return dot(a_high, b_high, kind) + (dot(a_high, b_low, kind) + dot(a_low, b_high, kind))


def dot_exact(a, b):
    return lax.dot_general(
        a, b, (KINDS["nn"], ((), ())), precision=HIGHEST, preferred_element_type=F32
    )


def iotas(shape=(128, 128)):
    return lax.broadcasted_iota(jnp.int32, shape, 0), lax.broadcasted_iota(jnp.int32, shape, 1)


def stack_heads(x):
    return jnp.concatenate([x[:, :128], x[:, 128:]], axis=0)


def side_heads(x):
    return jnp.concatenate([x[:64], x[64:]], axis=1)


def diagonal_heads(x):
    zero = jnp.zeros_like(x[:64])
    return jnp.concatenate(
        [jnp.concatenate([x[:64], zero], axis=1), jnp.concatenate([zero, x[64:]], axis=1)], axis=0
    )


def twice(x):
    return jnp.concatenate([x, x], axis=0)


def fold(x):
    return x[:64] + x[64:]


def half_swap(x):
    return jnp.concatenate([x[:, 64:], x[:, :64]], axis=1)


def by_block(x):
    lower = lax.broadcasted_iota(jnp.int32, (1, 128), 1) < 64
    rows = []
    for pair in range(2):
        first = x[0:1, 128 * pair : 128 * pair + 128]
        second = x[1:2, 128 * pair : 128 * pair + 128]
        rows.append(jnp.where(lower, first, half_swap(second)))
        rows.append(jnp.where(lower, half_swap(first), second))
    return jnp.concatenate(rows, axis=0)


def by_head(x):
    lower = lax.broadcasted_iota(jnp.int32, (1, 128), 1) < 64
    heads = ([], [])
    for pair in range(2):
        even, odd = x[2 * pair : 2 * pair + 1], x[2 * pair + 1 : 2 * pair + 2]
        heads[0].append(jnp.where(lower, even, half_swap(odd)))
        heads[1].append(jnp.where(lower, half_swap(even), odd))
    return jnp.concatenate([jnp.concatenate(row, axis=1) for row in heads], axis=0)


def turned(x):
    return jnp.transpose(jnp.concatenate([x, jnp.zeros((120, 128), F32)], axis=0))


def unit_scale(x):
    return lax.rsqrt(jnp.sum(x * x, axis=-1, keepdims=True) + EPS)


def unit_back(raw, grad, scale):
    inv = unit_scale(raw)
    unit = raw * inv
    return (scale * inv) * (grad - unit * jnp.sum(grad * unit, axis=-1, keepdims=True))


def running_decay(write_rate, log_decay):
    row, col = iotas()
    same = (row >> 6) == (col >> 6)
    upto = jnp.where(same & (row <= col), 1.0, 0.0).astype(F32)
    both = jnp.concatenate([by_block(log_decay), by_block(write_rate)], axis=0)
    summed = dot_exact(both, upto)
    rows = jnp.concatenate([summed[:4], both[4:]], axis=0)
    return rows[:4], turned(rows)


def block_columns(rows, columns, b):
    cum_row = rows[b : b + 1]
    cum = columns[:, b : b + 1]
    rate = columns[:, 4 + b : 5 + b]
    first = lax.broadcasted_iota(jnp.int32, (128, 1), 0) < 64
    last = jnp.where(first, cum_row[:, 63:64], cum_row[:, 127:128])
    return cum_row, cum, rate, jnp.exp(cum), jnp.exp(last - cum)


def last_growth(rows, b):
    lane = lax.broadcasted_iota(jnp.int32, (1, 256), 1)
    return jnp.exp(jnp.where(lane < 128, rows[b : b + 1, 63:64], rows[b : b + 1, 127:128]))


def block_tables(query, key, rows, columns, b):
    row, col = iotas()
    causal = ((row >> 6) == (col >> 6)) & (row >= col)
    cum_row, cum, rate, _, _ = block_columns(rows, columns, b)
    within = jnp.where(causal, jnp.exp(jnp.where(causal, cum - cum_row, 0.0)), 0.0)
    key2 = twice(key)
    strict = jnp.where(row > col, within, 0.0) * rate
    system = strict * dot3(key2, key2, "nt")
    query_key = dot3(twice(query), key2, "nt") * within
    return within, system, query_key


def inverse(systems, between=None):
    row, col = iotas()
    found = None
    for level in range(6):
        here = ((row >> (level + 1)) == (col >> (level + 1))) & ((row >> level) != (col >> level))
        below = [jnp.where(here, system, 0.0) for system in systems]
        if found is None:
            eye = jnp.where(row == col, 1.0, 0.0).astype(F32)
            found = [eye - one for one in below]
        else:
            half = [dot3(one, two) for one, two in zip(found, below)]
            found = [one - dot3(two, one) for one, two in zip(found, half)]
            if between is not None:
                between(level)
    return found


def gated(out, gate):
    inv = lax.rsqrt(jnp.mean(out * out, axis=-1, keepdims=True) + EPS)
    return out * inv * (gate / (1.0 + jnp.exp(-gate)))


def gated_back(out, gate, grad):
    inv = lax.rsqrt(jnp.mean(out * out, axis=-1, keepdims=True) + EPS)
    sig = 1.0 / (1.0 + jnp.exp(-gate))
    weighted = grad * (gate * sig)
    grad_gate = grad * out * inv * (sig * (1.0 + gate * (1.0 - sig)))
    along = jnp.mean(weighted * out, axis=-1, keepdims=True)
    return inv * (weighted - out * (inv * inv * along)), grad_gate


def score_grads(query, key, tables, update, grad_out):
    within, _, query_key = tables
    grad_scores = dot3(grad_out, update, "nt")
    masked = grad_scores * within
    return grad_scores * query_key, fold(dot(masked, twice(key))), dot(masked, twice(query), "tn")


def block_grads(
    key, value, cols, growth_last, tables, step, update, grad_out, grad_state, state_in, scored
):
    _, _, rate, growth, remain = cols
    within, system, _ = tables
    scored_spread, grad_query, scored_key = scored
    row, col = iotas()
    key2 = twice(key)
    grad_system = -dot(step, update, "nt")
    strict = jnp.where(row > col, grad_system * within, 0.0) * rate
    pulled = grad_system * system
    spread = scored_spread + pulled
    state_key = dot(diagonal_heads(update), grad_state, "nt")
    grad_key = fold(
        scored_key + dot(strict, key2) + dot(strict, key2, "tn") + remain * state_key
    )
    tail = remain * jnp.sum(key2 * state_key, axis=-1, keepdims=True)
    grad_cum = jnp.sum(spread, axis=-1, keepdims=True) - tail
    grad_row = -jnp.sum(spread, axis=0, keepdims=True)
    end0 = jnp.sum(tail[:64], axis=0, keepdims=True)
    end1 = jnp.sum(tail[64:], axis=0, keepdims=True)
    grad_value = rate * step
    if state_in is None:
        inner = value
    else:
        state, key_state, query_state = state_in
        inner = value - growth * key_state
        out_growth = growth * grad_out
        in_growth = growth * grad_value
        grad_cum += jnp.sum(out_growth * query_state - in_growth * key_state, axis=-1, keepdims=True)
        grad_query += dot3(side_heads(out_growth), state, "nt")
        grad_key -= dot(side_heads(in_growth), state, "nt")
        kept = jnp.sum(growth_last * (state * grad_state), axis=0, keepdims=True)
        end0 += jnp.sum(kept[:, :128], axis=1, keepdims=True)
        end1 += jnp.sum(kept[:, 128:], axis=1, keepdims=True)
    lane = lax.broadcasted_iota(jnp.int32, (1, 128), 1)
    grad_row += jnp.where(lane == 63, end0, 0.0) + jnp.where(lane == 127, end1, 0.0)
    grad_rate = jnp.sum(step * inner, axis=-1, keepdims=True) + (
        jnp.sum(pulled, axis=-1, keepdims=True) / rate
    )
    return grad_query, grad_key, grad_value, grad_rate, grad_cum, grad_row


def decay_grads(grad_cums, grad_rates, grad_rows):
    row, col = iotas()
    packed = jnp.zeros((128, 128), F32)
    for b in range(4):
        packed = jnp.where(col == b, grad_cums[b], packed)
        packed = jnp.where(col == 4 + b, grad_rates[b], packed)
    packed = jnp.transpose(packed)[:8]
    since = jnp.where(((row >> 6) == (col >> 6)) & (row >= col), 1.0, 0.0).astype(F32)
    grad_cum = packed[:4] + jnp.concatenate(grad_rows, axis=0)
    grad_cum = jnp.concatenate([grad_cum, jnp.zeros((4, 128), F32)], axis=0)
    return by_head(packed[4:]), by_head(dot_exact(grad_cum, since)[:4])


def rows_of(index, size):
    return pl.ds(pl.multiple_of(index * size, size), size)


def send(src, dst, send_sem, recv_sem, device):
    copy = pltpu.make_async_remote_copy(
        src_ref=src,
        dst_ref=dst,
        send_sem=send_sem,
        recv_sem=recv_sem,
        device_id=device,
        device_id_type=MESH,
    )
    copy.start()


def await_bytes(ref, sem):
    pltpu.make_async_copy(ref, ref, sem).wait()


def layer_kernel(
    query_hbm,
    key_hbm,
    value_hbm,
    gate_hbm,
    rate_hbm,
    decay_hbm,
    weight_hbm,
    cot_hbm,
    response_ref,
    owner_ref,
    layer_ref,
    grad_query_ref,
    grad_key_ref,
    grad_value_ref,
    grad_gate_ref,
    grad_rate_ref,
    grad_decay_ref,
    grad_weight_ref,
    query_ref,
    key_ref,
    value_ref,
    gate_ref,
    rate_ref,
    decay_ref,
    weight_ref,
    cot_ref,
    cots,
    piece_src,
    pieces,
    chosen_src,
    chosen,
    starts,
    grad_src,
    grad_pieces,
    owned_src,
    owned,
    sums_src,
    sums,
    weight_src,
    weight_pair,
    weight_sum,
    weight_in,
    within_s,
    system_s,
    scores_s,
    inverse_s,
    outs_s,
    update_s,
    step_s,
    grad_out_s,
    state_s,
    grad_state_s,
    key_state_s,
    query_state_s,
    normed_s,
    share_s,
    turned_s,
    pick_s,
    gather_s,
    load_sem,
    ring_send,
    ring_recv,
    sum_send,
    sum_recv,
    seq_send,
    seq_recv,
):
    me = lax.axis_index("seq")
    head = lax.axis_index("head")
    chip, core = lax.div(me, 2), lax.rem(me, 2)
    right, left = lax.rem(head + 1, N_HEAD), lax.rem(head + N_HEAD - 1, N_HEAD)

    loads = [
        pltpu.make_async_copy(src, dst, load_sem.at[index])
        for index, (src, dst) in enumerate(
            (
                (rate_hbm, rate_ref),
                (decay_hbm, decay_ref),
                (key_hbm, key_ref),
                (query_hbm, query_ref),
                (value_hbm, value_ref),
                (gate_hbm, gate_ref),
                (cot_hbm, cot_ref),
                (weight_hbm, weight_ref),
            )
        )
    ]
    for load in loads:
        load.start()

    barrier = pltpu.get_barrier_semaphore()

    def greet(offset, carry):
        pl.semaphore_signal(
            barrier, inc=1, device_id={"seq": lax.rem(me + offset, N_SEQ)}, device_id_type=MESH
        )
        return carry

    lax.fori_loop(1, N_SEQ, greet, 0)
    for neighbour in (left, right):
        pl.semaphore_signal(barrier, inc=1, device_id={"head": neighbour}, device_id_type=MESH)

    def ring_order(hop, to_right):
        order = (0, 1, 2, 3) if to_right else (2, 3, 0, 1)
        return order[:2] if hop == 4 else order

    def ring_chunk(hop, to_right, chunk):
        slot = hop - 1 if to_right or hop == 4 else 3 + hop
        return cots.at[slot, pl.ds(64 * chunk, 64)]

    def ring_index(hop, to_right, chunk):
        return 8 * (hop - 1) + (0 if to_right else 4) + chunk

    def ring_start(hop, to_right, chunk):
        if hop == 1:
            src = cot_hbm.at[pl.ds(64 * chunk, 64)]
        else:
            src = ring_chunk(hop - 1, to_right, chunk)
        send(
            src,
            ring_chunk(hop, to_right, chunk),
            ring_send.at[0],
            ring_recv.at[ring_index(hop, to_right, chunk)],
            {"head": right if to_right else left},
        )

    ring_steps = [(hop, place) for hop in (1, 2, 3, 4) for place in range(2 if hop == 4 else 4)]

    def ring_pump(count):
        for _ in range(count):
            hop, place = ring_steps.pop(0)
            for to_right in (True, False):
                chunk = ring_order(hop, to_right)[place]
                await_bytes(
                    ring_chunk(hop, to_right, chunk), ring_recv.at[ring_index(hop, to_right, chunk)]
                )
                if hop < 4 and chunk in ring_order(hop + 1, to_right):
                    ring_start(hop + 1, to_right, chunk)

    def cot_slots():
        yield cot_ref, head
        for hop in (1, 2, 3):
            yield cots.at[hop - 1], (head - hop + N_HEAD) % N_HEAD
            yield cots.at[3 + hop], (head + hop) % N_HEAD
        yield cots.at[3], (head + 4) % N_HEAD

    def turn(index, slot_ref):
        turned_s[index] = jnp.transpose(slot_ref[...])

    for load in loads[:5]:
        load.wait()
    rate2, decay2 = rate_ref[...], decay_ref[...]
    rows, columns = running_decay(rate2, decay2)

    def unit_block(ref, b):
        raw = ref[SPAN * b : SPAN * b + SPAN, :].astype(F32)
        return raw * unit_scale(raw)

    def block_of(ref, b):
        return stack_heads(ref[SPAN * b : SPAN * b + SPAN, :]).astype(F32)

    queries = [unit_block(query_ref, b) * SCALE for b in range(4)]
    keys = [unit_block(key_ref, b) for b in range(4)]
    cols = [block_columns(rows, columns, b) for b in range(4)]

    def tables_of(b):
        within, system, query_key = block_tables(queries[b], keys[b], rows, columns, b)
        within_s[b] = within
        system_s[b] = system
        scores_s[b] = query_key
        return system

    def tail_of(b):
        return twice(keys[b]) * cols[b][4]

    first_system = tables_of(0)
    pl.semaphore_wait(barrier, N_SEQ + 1)
    for place in range(4):
        for to_right in (True, False):
            ring_start(1, to_right, ring_order(1, to_right)[place])
    inverse_s[0] = inverse([first_system])[0].astype(BF16)
    update = dot(inverse_s[0], cols[0][2] * block_of(value_ref, 0))
    update_s[0] = update
    final = dot(tail_of(0), diagonal_heads(update), "tn")
    piece_src[0:128, :] = final[:, :128].astype(BF16)
    piece_src[128:256, :] = final[:, 128:].astype(BF16)

    def send_pieces(offset, carry):
        to = lax.rem(me + offset, N_SEQ)
        send(
            piece_src.at[rows_of(lax.div(to, 2), 16)],
            pieces.at[rows_of(offset - 1, 16)],
            seq_send.at[0],
            seq_recv.at[0],
            {"seq": to},
        )
        return carry

    lax.fori_loop(1, N_SEQ, send_pieces, 0)
    pieces[496:512, :] = piece_src[rows_of(chip, 16), :]

    def owner_of(device, slot):
        prompt = (response_ref[3 * device] >> 1) + slot
        found = owner_ref[jnp.minimum(prompt, N_SEQ - 1)]
        return jnp.where(prompt < N_SEQ, found, -1)

    row, _ = iotas((32, 1))
    _, col = iotas((1, 512))
    source = (me + 31 - (col >> 4)) % N_SEQ
    same_row = (row & 15) == (col & 15)
    for place in range(CHIPS):
        to = 2 * lax.rem(chip + place + 1, CHIPS) + core
        wanted = jnp.where(row < 16, owner_of(to, 0), owner_of(to, 1))
        here = (source == wanted) & same_row
        pick_s[32 * place : 32 * place + 32, :] = jnp.where(here, 1.0, 0.0).astype(BF16)

    systems = []
    for b in (1, 2, 3):
        systems.append(tables_of(b))
        ring_pump(2 if b == 3 else 1)

    await_bytes(pieces.at[pl.ds(0, 496)], seq_recv.at[0])

    chosen_src[...] = dot(pick_s[...], pieces[...]).astype(BF16)

    def send_chosen(offset, carry):
        send(
            chosen_src.at[rows_of(offset - 1, 32)],
            chosen.at[rows_of(offset - 1, 32)],
            seq_send.at[1],
            seq_recv.at[1],
            {"seq": 2 * lax.rem(chip + offset, CHIPS) + core},
        )
        return carry

    lax.fori_loop(1, CHIPS, send_chosen, 0)
    chosen[480:512, :] = chosen_src[480:512, :]

    def between(level):
        if level < 5:
            ring_pump(1)

    for b, found in zip((1, 2, 3), inverse(systems, between)):
        inverse_s[b] = found.astype(BF16)
    loads[5].wait()

    def norm_block(b, out):
        outs_s[b] = out
        result = side_heads(gated(out, block_of(gate_ref, b))).astype(BF16)
        normed_s[SPAN * b : SPAN * b + SPAN, :] = result

    norm_block(0, dot3(scores_s[0], update_s[0]))
    loads[6].wait()
    for index, (slot_ref, _) in enumerate(cot_slots()):
        if index < 5:
            turn(index, slot_ref)
    ring_pump(2)

    await_bytes(chosen.at[pl.ds(0, 480)], seq_recv.at[1])
    for slot in range(2):
        for piece in range(CHIPS):
            place = lax.rem(chip + 15 - piece, CHIPS)
            starts[slot, 16 * (piece % 8) : 16 * (piece % 8) + 16, 128 * (piece // 8) : 128 * (piece // 8) + 128] = (
                chosen[pl.ds(pl.multiple_of(place * 32 + 16 * slot, 16), 16), :].astype(F32)
            )
    own = [response_ref[3 * me + j] for j in range(3)]
    fresh, later = [None, None], [None, None]
    for j in (1, 2):
        fresh.append(jnp.where(own[j] != own[j - 1], 1.0, 0.0).astype(F32))
        later.append(jnp.where((own[j] >> 1) != (own[0] >> 1), 1.0, 0.0).astype(F32))

    state = None
    for b in (1, 2, 3):
        if b == 1:
            state = starts[0]
        else:
            begun = (1.0 - later[b]) * starts[0] + later[b] * starts[1]
            state = fresh[b] * begun + (1.0 - fresh[b]) * state
        state_s[b - 1] = state
        _, _, rate, growth, _ = cols[b]
        both = dot3(jnp.concatenate([keys[b], queries[b]], axis=0), state)
        key_state, query_state = stack_heads(both[:64]), stack_heads(both[64:])
        key_state_s[b - 1] = key_state
        query_state_s[b - 1] = query_state
        update = dot(inverse_s[b], rate * (block_of(value_ref, b) - growth * key_state))
        update_s[b] = update
        if b < 3:
            state = last_growth(rows, b) * state + dot(tail_of(b), diagonal_heads(update), "tn")
        norm_block(b, growth * query_state + dot3(scores_s[b], update))
        if b < 3:
            ring_pump(1)

    def share(distance):
        block = (head + distance + N_HEAD) % N_HEAD
        return dot(normed_s[...], weight_ref[rows_of(block, 256), :], "nt")

    def sums_order(hop, to_right):
        if hop == 1:
            return (0, 1) if to_right else (2, 3)
        return (2, 3, 0, 1) if to_right else (0, 1, 2, 3)

    def sums_slot(hop, to_right):
        return 2 * (hop - 1) + (0 if to_right else 1)

    def sums_start(hop, to_right, chunk):
        here = (sums_slot(hop, to_right), pl.ds(64 * chunk, 64))
        send(
            sums_src.at[here],
            sums.at[here],
            sum_send.at[0],
            sum_recv.at[ring_index(hop, to_right, chunk)],
            {"head": right if to_right else left},
        )

    def sums_prepare(hop):
        for to_right in (True, False):
            share_s[sums_slot(hop, to_right)] = share(5 - hop if to_right else hop - 5)

    def sums_begin():
        across = share(4)
        for to_right in (True, False):
            low = 0 if to_right else 128
            sums_src[sums_slot(1, to_right), low : low + 128, :] = across[low : low + 128].astype(BF16)
        for place in range(2):
            for to_right in (True, False):
                sums_start(1, to_right, sums_order(1, to_right)[place])
        sums_prepare(2)
        for to_right in (True, False):
            slot, low = sums_slot(2, to_right), 128 if to_right else 0
            sums_src[slot, low : low + 128, :] = share_s[slot, low : low + 128, :].astype(BF16)
        for place in range(2):
            for to_right in (True, False):
                sums_start(2, to_right, sums_order(2, to_right)[place])

    sums_steps = [(hop, place) for hop in (1, 2, 3, 4) for place in range(2 if hop == 1 else 4)]

    def sums_pump(count):
        for _ in range(count):
            hop, place = sums_steps.pop(0)
            for to_right in (True, False):
                chunk = sums_order(hop, to_right)[place]
                here = pl.ds(64 * chunk, 64)
                arrived = sums.at[sums_slot(hop, to_right), here]
                await_bytes(arrived, sum_recv.at[ring_index(hop, to_right, chunk)])
                if hop < 4:
                    slot = sums_slot(hop + 1, to_right)
                    sums_src[slot, here, :] = (
                        share_s[slot, here, :] + arrived[...].astype(F32)
                    ).astype(BF16)
                    sums_start(hop + 1, to_right, chunk)

    loads[7].wait()
    sums_begin()
    sums_prepare(3)
    for index, (slot_ref, _) in enumerate(cot_slots()):
        if index in (5, 6):
            turn(index, slot_ref)

    grad_normed = None
    for index, (slot_ref, block) in enumerate(cot_slots()):
        if index == 7:
            ring_pump(2)
            turn(7, slot_ref)
        term = dot(slot_ref[...], weight_ref[rows_of(block, 256), :])
        grad_normed = term if grad_normed is None else grad_normed + term
        share_w = dot(turned_s[index], normed_s[...]).astype(BF16)
        for quarter in range(4):
            place = (quarter % 2) * 1024 + (2 * block + quarter // 2) * 64
            weight_src[pl.ds(pl.multiple_of(place, 64), 64), :] = share_w[
                64 * quarter : 64 * quarter + 64
            ]
    send(
        weight_src.at[rows_of(1 - core, 1024)],
        weight_pair,
        seq_send.at[4],
        seq_recv.at[4],
        {"seq": 2 * chip + 1 - core},
    )
    for b in range(4):
        grad_out, grad_gate = gated_back(
            outs_s[b], block_of(gate_ref, b), stack_heads(grad_normed[SPAN * b : SPAN * b + SPAN])
        )
        grad_out_s[b] = grad_out
        grad_gate_ref[SPAN * b : SPAN * b + SPAN, :] = side_heads(grad_gate)

    grad_state = jnp.zeros((128, 256), F32)
    begun = [jnp.zeros((128, 256), F32), jnp.zeros((128, 256), F32)]
    for b in (3, 2, 1):
        _, _, rate, growth, remain = cols[b]
        grad_out = grad_out_s[b]
        grad_state_s[b] = grad_state
        grad_update = dot(scores_s[b], grad_out, "tn")
        if b < 3:
            grad_update += remain * stack_heads(dot(keys[b], grad_state))
        step = dot(inverse_s[b], grad_update, "tn")
        step_s[b] = step
        sides = jnp.concatenate(
            [side_heads(-(rate * growth) * step), side_heads(growth * grad_out)], axis=0
        )
        grad_in = dot(jnp.concatenate([keys[b], queries[b]], axis=0), sides, "tn")
        if b < 3:
            grad_in += last_growth(rows, b) * grad_state
        if b > 1:
            begun[0] += (fresh[b] * (1.0 - later[b])) * grad_in
            begun[1] += (fresh[b] * later[b]) * grad_in
            grad_state = (1.0 - fresh[b]) * grad_in
            if b == 2:
                sums_pump(1)
        else:
            begun[0] += grad_in
    for slot in range(2):
        for piece in range(CHIPS):
            grad_src[32 * piece + 16 * slot : 32 * piece + 16 * slot + 16, :] = begun[slot][
                16 * (piece % 8) : 16 * (piece % 8) + 16,
                128 * (piece // 8) : 128 * (piece // 8) + 128,
            ].astype(BF16)

    def send_grads(offset, carry):
        to = lax.rem(chip + offset, CHIPS)
        send(
            grad_src.at[rows_of(to, 32)],
            grad_pieces.at[rows_of(offset - 1, 32)],
            seq_send.at[2],
            seq_recv.at[2],
            {"seq": 2 * to + core},
        )
        return carry

    lax.fori_loop(1, CHIPS, send_grads, 0)
    grad_pieces[480:512, :] = grad_src[rows_of(chip, 32), :]

    sums_pump(1)

    await_bytes(weight_pair, seq_recv.at[4])
    for part in range(4):
        place = core * 1024 + 256 * part
        weight_sum[256 * part : 256 * part + 256, :] = (
            weight_src[pl.ds(pl.multiple_of(place, 256), 256), :].astype(F32)
            + weight_pair[256 * part : 256 * part + 256, :].astype(F32)
        ).astype(BF16)

    def send_weight(offset, carry):
        to = lax.rem(chip + offset, CHIPS)
        send(
            weight_sum.at[rows_of(to, 64)],
            weight_in.at[rows_of(offset - 1, 64)],
            seq_send.at[5],
            seq_recv.at[5],
            {"seq": 2 * to + core},
        )
        return carry

    lax.fori_loop(1, CHIPS, send_weight, 0)
    sums_prepare(4)
    sums_pump(4)
    _, col = iotas((1, 128))
    row, _ = iotas((512, 1))
    target = (me + 1 + (row >> 4)) % N_SEQ
    for part in range(4):
        owner = jnp.full((1, 128), -1, jnp.int32)
        for index in range(4):
            device = 2 * lax.rem(chip + 31 - (4 * part + index), CHIPS) + core
            for slot in range(2):
                owner = jnp.where((col >> 4) == 2 * index + slot, owner_of(device, slot), owner)
        here = (owner == target) & ((row & 15) == (col & 15))
        gather_s[:, 128 * part : 128 * part + 128] = jnp.where(here, 1.0, 0.0).astype(BF16)
    sums_pump(1)

    await_bytes(grad_pieces.at[pl.ds(0, 480)], seq_recv.at[2])

    owned_src[...] = dot(gather_s[...], grad_pieces[...]).astype(BF16)

    def send_owned(offset, carry):
        send(
            owned_src.at[rows_of(offset - 1, 16)],
            owned.at[rows_of(offset - 1, 16)],
            seq_send.at[3],
            seq_recv.at[3],
            {"seq": lax.rem(me + offset, N_SEQ)},
        )
        return carry

    lax.fori_loop(1, N_SEQ, send_owned, 0)
    sums_pump(1)
    owned[496:512, :] = owned_src[496:512, :]


    grad_cums, grad_rates, grad_rows = [None] * 4, [None] * 4, [None] * 4

    def tables_found(b):
        return within_s[b], system_s[b], scores_s[b]

    def scored_of(b):
        return score_grads(queries[b], keys[b], tables_found(b), update_s[b], grad_out_s[b])

    def finish_block(b, grad_state, state_in, scored):
        found = block_grads(
            keys[b],
            block_of(value_ref, b),
            cols[b],
            last_growth(rows, b),
            tables_found(b),
            step_s[b],
            update_s[b],
            grad_out_s[b],
            grad_state,
            state_in,
            scored,
        )
        for raw_ref, out_ref, grad, scale in (
            (query_ref, grad_query_ref, found[0], SCALE),
            (key_ref, grad_key_ref, found[1], 1.0),
        ):
            raw = raw_ref[SPAN * b : SPAN * b + SPAN, :].astype(F32)
            out_ref[SPAN * b : SPAN * b + SPAN, :] = unit_back(raw, grad, scale)
        grad_value_ref[SPAN * b : SPAN * b + SPAN, :] = side_heads(found[2])
        grad_rates[b], grad_cums[b], grad_rows[b] = found[3:]

    for b in (1, 2, 3):
        state_in = (state_s[b - 1], key_state_s[b - 1], query_state_s[b - 1])
        finish_block(b, grad_state_s[b], state_in, scored_of(b))
        if b < 3:
            sums_pump(1)

    share_s[0] = share(0)
    scored = scored_of(0)
    grad_update = dot(scores_s[0], grad_out_s[0], "tn")
    await_bytes(weight_in.at[pl.ds(0, 15 * 64)], seq_recv.at[5])
    total = weight_sum[rows_of(chip, 64), :].astype(F32)
    for slot in range(15):
        total += weight_in[64 * slot : 64 * slot + 64, :].astype(F32)
    grad_weight_ref[...] = total
    await_bytes(owned.at[pl.ds(0, 496)], seq_recv.at[3])
    for piece in range(CHIPS):
        low, lane = 16 * (piece % 8), 128 * (piece // 8)
        one, two = [lax.rem(me + 63 - (2 * piece + side), N_SEQ) for side in range(2)]
        grad_state_s[0, low : low + 16, lane : lane + 128] = owned[rows_of(one, 16), :].astype(
            F32
        ) + owned[rows_of(two, 16), :].astype(F32)
    grad_state = grad_state_s[0]
    grad_update += cols[0][4] * stack_heads(dot(keys[0], grad_state))
    step_s[0] = dot(inverse_s[0], grad_update, "tn")
    finish_block(0, grad_state, None, scored)
    grad_rate_ref[...], grad_decay_ref[...] = decay_grads(grad_cums, grad_rates, grad_rows)

    sums_pump(4)
    layer_ref[...] = (share_s[0] + sums[6].astype(F32) + sums[7].astype(F32)).astype(BF16)

    await_bytes(cots, ring_send.at[0])
    await_bytes(sums.at[pl.ds(0, 7)], sum_send.at[0])
    await_bytes(pieces.at[pl.ds(0, 496)], seq_send.at[0])
    await_bytes(chosen.at[pl.ds(0, 480)], seq_send.at[1])
    await_bytes(grad_pieces.at[pl.ds(0, 480)], seq_send.at[2])
    await_bytes(owned.at[pl.ds(0, 496)], seq_send.at[3])
    await_bytes(weight_pair, seq_send.at[4])
    await_bytes(weight_in.at[pl.ds(0, 15 * 64)], seq_send.at[5])


SCRATCH = [
    pltpu.VMEM((256, 128), BF16),
    pltpu.VMEM((256, 128), BF16),
    pltpu.VMEM((256, 256), BF16),
    pltpu.VMEM((256, 256), BF16),
    pltpu.VMEM((2, 256), F32),
    pltpu.VMEM((2, 256), F32),
    pltpu.VMEM((2048, 256), BF16),
    pltpu.VMEM((256, 256), BF16),
    pltpu.VMEM((7, 256, 256), BF16),
    pltpu.VMEM((256, 128), BF16),
    pltpu.VMEM((512, 128), BF16),
    pltpu.VMEM((512, 128), BF16),
    pltpu.VMEM((512, 128), BF16),
    pltpu.VMEM((2, 128, 256), F32),
    pltpu.VMEM((512, 128), BF16),
    pltpu.VMEM((512, 128), BF16),
    pltpu.VMEM((512, 128), BF16),
    pltpu.VMEM((512, 128), BF16),
    pltpu.VMEM((8, 256, 256), BF16),
    pltpu.VMEM((8, 256, 256), BF16),
    pltpu.VMEM((2048, 256), BF16),
    pltpu.VMEM((1024, 256), BF16),
    pltpu.VMEM((1024, 256), BF16),
    pltpu.VMEM((960, 256), BF16),
    pltpu.VMEM((4, 128, 128), F32),
    pltpu.VMEM((4, 128, 128), F32),
    pltpu.VMEM((4, 128, 128), F32),
    pltpu.VMEM((4, 128, 128), BF16),
    pltpu.VMEM((4, 128, 128), F32),
    pltpu.VMEM((4, 128, 128), F32),
    pltpu.VMEM((4, 128, 128), F32),
    pltpu.VMEM((4, 128, 128), F32),
    pltpu.VMEM((3, 128, 256), F32),
    pltpu.VMEM((4, 128, 256), F32),
    pltpu.VMEM((3, 128, 128), F32),
    pltpu.VMEM((3, 128, 128), F32),
    pltpu.VMEM((256, 256), BF16),
    pltpu.VMEM((8, 256, 256), F32),
    pltpu.VMEM((8, 256, 256), BF16),
    pltpu.VMEM((512, 512), BF16),
    pltpu.VMEM((512, 512), BF16),
    pltpu.SemaphoreType.DMA((8,)),
    pltpu.SemaphoreType.DMA((1,)),
    pltpu.SemaphoreType.DMA((32,)),
    pltpu.SemaphoreType.DMA((1,)),
    pltpu.SemaphoreType.DMA((32,)),
    pltpu.SemaphoreType.DMA((6,)),
    pltpu.SemaphoreType.DMA((6,)),
]


def finish_kernel(*refs):
    given, results, held = refs[:8], refs[8:16], refs[16:24]
    sems = refs[24]
    reads = [pltpu.make_async_copy(given[i], held[i], sems.at[i]) for i in range(8)]
    writes = [pltpu.make_async_copy(held[i], results[i], sems.at[8 + i]) for i in range(8)]
    for read in reads:
        read.start()
    for read, write in zip(reads, writes):
        read.wait()
        write.start()
    for write in writes:
        write.wait()


RESULTS = [
    jax.ShapeDtypeStruct((256, 256), BF16),
    jax.ShapeDtypeStruct((256, 128), F32),
    jax.ShapeDtypeStruct((256, 128), F32),
    jax.ShapeDtypeStruct((256, 256), F32),
    jax.ShapeDtypeStruct((256, 256), F32),
    jax.ShapeDtypeStruct((2, 256), F32),
    jax.ShapeDtypeStruct((2, 256), F32),
    jax.ShapeDtypeStruct((64, 256), F32),
]


def per_device(
    query_rows, key_rows, value_rows, output_gate, write_rate, log_decay,
    out_weight, out_cotangent, block_response, prefix_owner,
):
    vmem = pl.BlockSpec(memory_space=pltpu.VMEM)
    smem = pl.BlockSpec(memory_space=pltpu.SMEM)
    whole = pl.BlockSpec(memory_space=pl.ANY)
    results = pl.pallas_call(
        layer_kernel,
        out_shape=RESULTS,
        in_specs=[whole] * 8 + [smem] * 2,
        out_specs=[vmem] * 8,
        scratch_shapes=SCRATCH,
        compiler_params=pltpu.CompilerParams(
            collective_id=0, has_side_effects=True, vmem_limit_bytes=56 * 1024 * 1024
        ),
    )(
        query_rows, key_rows, value_rows, output_gate, write_rate, log_decay,
        out_weight, out_cotangent, block_response, prefix_owner,
    )
    return pl.pallas_call(
        finish_kernel,
        out_shape=RESULTS,
        in_specs=[whole] * 8,
        out_specs=[whole] * 8,
        scratch_shapes=[pltpu.VMEM(one.shape, one.dtype) for one in RESULTS]
        + [pltpu.SemaphoreType.DMA((16,))],
        compiler_params=pltpu.CompilerParams(vmem_limit_bytes=56 * 1024 * 1024),
    )(*results)


def solution(mesh):
    rows = P("seq", "head")
    return jax.shard_map(
        per_device,
        mesh=mesh,
        in_specs=(rows, rows, rows, rows, P("head", "seq"), P("head", "seq"), P(None, "head"), rows, P(), P()),
        out_specs=(rows, rows, rows, rows, rows, P("head", "seq"), P("head", "seq"), rows),
        check_vma=False,
    )
```
